512 devices in a mesh: dp: 64 (over y, z_hi, core), mp: 8 (over z_lo, x).
Axes of the slice: x: 4, y: 8, z: 8 (z_hi: 4, z_lo: 2; z = z_hi * 2 + z_lo), core: 2. Of those that a mesh axis runs over, the one named last changes fastest.
Arguments:
- tokens: bfloat16 [24576, 3072], P('dp', 'mp'), may hold values from -6 to 6
- gain: bfloat16 [3072], P('mp'), may hold values from 0.099609375 to 1.8984375
- pre_act: bfloat16 [24576, 12288], P('dp', 'mp'), may hold values from -6 to 6
- w_in: bfloat16 [3072, 12288], P('dp', 'mp'), may hold values from -0.109375 to 0.109375
- act_cotangent: bfloat16 [24576, 12288], P('dp', 'mp'), may hold values from -6 to 6
Outputs:
- token_gradient: bfloat16 [24576, 3072], P('dp', 'mp')
- gain_gradient: float32 [3072], P('mp')
The draws below stay inside these ranges and needn't reach their ends.
All inputs are finite; a program needn't handle non-finite values.
Results may differ from the reference program's by a relative error of at most 0.019.
Values may be sent and summed in bfloat16 or wider, within the bound.
No kernel may reach another device: no remote copies, remote signals or barrier semaphores. Data moves between devices by JAX's collectives and lax.ppermute only.
A program may use at most 64 MiB of HBM per device.

```python
import jax
import jax.numpy as jnp
from jax import lax

D = 3072
FF = 12288
TOKENS = 24576
N_MP = 8


def levels(key, extent, shards, least, high):
    factor_of = 1.0
    for axis_at, shards_of in shards:
        heights = jax.random.uniform(jax.random.fold_in(jax.random.fold_in(key, 6), axis_at), (shards_of,), jnp.float32, least / len(shards), high / len(shards))
        factor_of = factor_of * jnp.repeat(jnp.exp(heights), extent[axis_at] // shards_of).reshape((-1,) + (1,) * (len(extent) - 1 - axis_at))
    return factor_of


def gaussian(rng, extent, deviation, reach, shards=(), held_as=jnp.bfloat16):
    array = jax.random.normal(rng, extent, jnp.float32) * deviation
    if len(shards) > 0:
        array = levels(rng, extent, shards, -0.22, 0.18) * array
    return jnp.clip(array, min=-reach, max=reach).astype(held_as)


def setup_inputs(seed: int = 0) -> dict:
    keys = jax.random.split(jax.random.key(seed), 6)
    return {
        "tokens": gaussian(keys[0], (TOKENS, D), 1.0, 6.0, ((0, 64), (1, 8))),
        "gain": jnp.clip(1.0 + 0.18 * jax.random.normal(keys[1], (D,), jnp.float32), 0.099609375, 1.8984375).astype(jnp.bfloat16),
        "pre_act": gaussian(keys[2], (TOKENS, FF), 1.0, 6.0, ((0, 64), (1, 8))),
        "w_in": gaussian(keys[3], (D, FF), D ** -0.5, 0.109375, ((0, 64), (1, 8))),
        "act_cotangent": gaussian(keys[4], (TOKENS, FF), 1.0, 6.0, ((0, 64), (1, 8))),
    }


def gelu_exact(value):
    return jax.nn.gelu(value, approximate=False)

def reference(tokens, gain, pre_act, w_in, act_cotangent):
    rows = tokens.astype(jnp.float32)
    mean_row = lax.optimization_barrier(jnp.mean(rows, axis=1, keepdims=True))
    centered_input = rows - mean_row
    inverse_deviation = 1.0 / jnp.sqrt(lax.optimization_barrier(jnp.mean(centered_input * centered_input, axis=1, keepdims=True)) + 1e-06)
    standardized = centered_input * inverse_deviation
    gain_float = gain.astype(jnp.float32)
    act_f, gelu_back = jax.vjp(gelu_exact, pre_act.astype(jnp.float32))
    d_pre = gelu_back(act_cotangent.astype(jnp.float32))[0].astype(jnp.bfloat16)
    block = FF // N_MP
    normed_gradient = jnp.zeros(rows.shape, jnp.float32)
    for index in range(N_MP):
        part = jnp.dot(d_pre[:, index * block:(index + 1) * block], w_in[:, index * block:(index + 1) * block].T, preferred_element_type=jnp.float32)
        normed_gradient = normed_gradient + part.astype(jnp.bfloat16).astype(jnp.float32)
    gain_gradient = lax.optimization_barrier(jnp.sum(normed_gradient * standardized, axis=0))
    scaled_rows = normed_gradient * gain_float
    first_moment = lax.optimization_barrier(jnp.mean(scaled_rows, axis=1, keepdims=True))
    second_moment = lax.optimization_barrier(jnp.mean(scaled_rows * standardized, axis=1, keepdims=True))
    token_gradient = (inverse_deviation * (scaled_rows - first_moment - standardized * second_moment)).astype(jnp.bfloat16)
    return (token_gradient, gain_gradient)
```

```python
import jax
import jax.numpy as jnp
from jax import lax
from jax.experimental import pallas as pl
from jax.experimental.pallas import tpu as pltpu
from jax.sharding import Mesh, PartitionSpec as P

NAMES = ("y", "zh", "c", "zl", "x")
SIZES = (8, 4, 2, 2, 4)
DP, MP = ("y", "zh", "c"), ("zl", "x")
F32, BF16 = jnp.float32, jnp.bfloat16


def gelu_exact(value):
    return jax.nn.gelu(value, approximate=False)


def spread(row, axes, n):
    return lax.all_to_all(jnp.broadcast_to(row, (n,) + row.shape), axes, 0, 0)


def matmul_kernel(w_ref, d_ref, out_ref):
    out_ref[...] = lax.dot_general(
        w_ref[...], d_ref[0], (((1,), (1,)), ((), ())), preferred_element_type=F32
    ).astype(BF16)[None, None]


def partial_products(w_half, d_pair):
    rows, hidden = w_half.shape
    block, tokens = rows // 8, d_pair.shape[1]
    return pl.pallas_call(
        matmul_kernel,
        grid=(2, 8),
        in_specs=[
            pl.BlockSpec((block, hidden), lambda t, m: (m, 0)),
            pl.BlockSpec((1, tokens, hidden), lambda t, m: (t, 0, 0)),
        ],
        out_specs=pl.BlockSpec((1, 1, block, tokens), lambda t, m: (t, m, 0, 0)),
        out_shape=jax.ShapeDtypeStruct((2, 8, block, tokens), BF16),
        compiler_params=pltpu.CompilerParams(vmem_limit_bytes=32 * 1024 * 1024),
        cost_estimate=pl.CostEstimate(
            flops=4 * rows * hidden * tokens, bytes_accessed=12 << 20, transcendentals=0
        ),
    )(w_half, d_pair)


def sum_kernel(parts_ref, xhat_ref, gain_ref, d_ref, moments_ref, share_ref):
    first, second = 0.0, 0.0
    for z in range(4):
        for c in range(2):
            total = parts_ref[c * 8, pl.ds(z * 48, 48), :].astype(F32)
            for m in range(1, 8):
                total += parts_ref[c * 8 + m, pl.ds(z * 48, 48), :].astype(F32)
            at = pl.ds((z * 2 + c) * 48, 48)
            d_ref[at, :] = total
            xhat = xhat_ref[at, :]
            product = total * xhat
            share_ref[at, :] = jnp.sum(product, axis=1, keepdims=True)
            first += jnp.sum(total * gain_ref[at, :], axis=0, keepdims=True)
            second += jnp.sum(product * gain_ref[at, :], axis=0, keepdims=True)
    moments_ref[...] = jnp.concatenate([first, second, jnp.zeros((6, first.shape[1]), F32)], axis=0)


def final_kernel(d_ref, xhat_ref, gain_ref, moments_ref, rstd_ref, out_ref):
    both = moments_ref[0]
    for m in range(1, 8):
        both += moments_ref[m]
    both = both * (1.0 / 3072)
    g = d_ref[...] * gain_ref[...]
    value = rstd_ref[...] * (g - both[0:1] - xhat_ref[...] * both[1:2])
    out_ref[...] = value.T.astype(BF16)


def on_device(tokens, gain, pre_act, w_in, act_cotangent):
    rows, share = tokens.shape
    core = lax.axis_index("c")

    w_half = lax.all_gather(w_in, "zh", axis=0, tiled=True)
    w_half = lax.all_gather(w_half, "y", axis=0, tiled=True)

    x = tokens.astype(F32).T
    local_mean = jnp.mean(x, axis=0, keepdims=True)
    local_square = jnp.sum((x - local_mean) ** 2, axis=0, keepdims=True)
    stats = spread(jnp.concatenate([local_mean, local_square] * 4, axis=0), MP, 8)
    means, squares = stats[:, 0], stats[:, 1]
    mean = jnp.mean(means, axis=0, keepdims=True)
    variance = (
        jnp.sum(squares, axis=0, keepdims=True)
        + share * jnp.sum((means - mean) ** 2, axis=0, keepdims=True)
    ) / (8 * share)
    rstd = 1.0 / jnp.sqrt(variance + 1e-06)
    xhat = (x - mean) * rstd
    gain_column = gain.astype(F32)[:, None]

    _, gelu_back = jax.vjp(gelu_exact, pre_act.astype(F32))
    d_pre = gelu_back(act_cotangent.astype(F32))[0].astype(BF16)
    other = lax.ppermute(d_pre, "c", [(0, 1), (1, 0)])
    d_pair = jnp.stack([jnp.where(core == 0, d_pre, other), jnp.where(core == 0, other, d_pre)])

    parts = partial_products(w_half, d_pair)
    parts = parts.reshape(16, share // 2, rows)
    parts = lax.all_to_all(parts, ("c", "zl", "x"), 0, 0)

    d_normed, moments, gain_share = pl.pallas_call(
        sum_kernel,
        out_shape=[
            jax.ShapeDtypeStruct((share, rows), F32),
            jax.ShapeDtypeStruct((8, rows), F32),
            jax.ShapeDtypeStruct((share, 1), F32),
        ],
        compiler_params=pltpu.CompilerParams(vmem_limit_bytes=32 * 1024 * 1024),
    )(parts, xhat, gain_column)

    moments = spread(moments, MP, 8)
    token_gradient = pl.pallas_call(
        final_kernel,
        out_shape=jax.ShapeDtypeStruct((rows, share), BF16),
        compiler_params=pltpu.CompilerParams(vmem_limit_bytes=32 * 1024 * 1024),
    )(d_normed, xhat, gain_column, moments, rstd)

    gain_share = jnp.pad(gain_share.reshape(3, 128), ((0, 5), (0, 0)))
    gain_gradient = jnp.sum(spread(gain_share, DP, 64), axis=0)[:3].reshape(share)
    return (token_gradient, gain_gradient)


def solution(mesh):
    fine = Mesh(mesh.devices.reshape(SIZES), NAMES)
    placed = (P(DP, MP), P(MP), P(DP, MP), P(DP, MP), P(DP, MP))
    return jax.shard_map(
        on_device, mesh=fine, in_specs=placed, out_specs=(P(DP, MP), P(MP)), check_vma=False
    )
```

```python
import jax
import jax.numpy as jnp
from jax import lax
from jax.experimental import pallas as pl
from jax.experimental.pallas import tpu as pltpu
from jax.sharding import Mesh, PartitionSpec as P

NAMES = ("y", "zh", "c", "zl", "x")
SIZES = (8, 4, 2, 2, 4)
DP, MP = ("y", "zh", "c"), ("zl", "x")
F32, BF16 = jnp.float32, jnp.bfloat16
SHARD = 48
MEMORY = 40 * 1024 * 1024
CHUNKS = ((0,), (1, 3, 2))


def gelu_exact(value):
    return jax.nn.gelu(value, approximate=False)


def spread(row, axes, n):
    return lax.all_to_all(jnp.broadcast_to(row, (n,) + row.shape), axes, 0, 0)


def shift(array, axis, n, by):
    return lax.ppermute(array, axis, [(i, (i - by) % n) for i in range(n)])


def ring(block, beside=None):
    pieces = [(0, 0, block)]
    behind = ahead = block
    for s in range(1, 4):
        if s == 3:
            behind, ahead, beside = lax.optimization_barrier((behind, ahead, beside))
        behind, ahead = shift(behind, "y", 8, -1), shift(ahead, "y", 8, 1)
        pieces += [(-s, 0, behind), (s, 0, ahead)]
    cut = (block.shape[0] // 2 + 15) // 16 * 16
    pieces += [
        (4, 0, shift(behind[:cut], "y", 8, -1)),
        (4, cut, shift(ahead[cut:], "y", 8, 1)),
    ]
    return pieces, beside


def products(pieces, rows, d_pair, here, name):
    tokens, hidden = d_pair.shape[2], d_pair.shape[1]

    def kernel(here_ref, d_ref, *refs):
        w_refs, out_ref = refs[:-1], refs[-1]
        every = jnp.concatenate([w[...] for w in w_refs], axis=0)
        product = jnp.dot(every, d_ref[0], preferred_element_type=F32).astype(BF16)
        at = 0
        for (offset, first, piece), w in zip(pieces, w_refs, strict=True):
            for k in range(max(piece.shape[0] // rows, 1)):
                height = min(piece.shape[0], rows)
                block = lax.rem(here_ref[0] + (offset + k) % 8, 8)
                out_ref[0, block, first : first + height] = product[at : at + height]
                at += height

    blocks = [w for _, _, w in pieces]
    with jax.named_scope(name):
        return pl.pallas_call(
            kernel,
            grid_spec=pltpu.PrefetchScalarGridSpec(
                num_scalar_prefetch=1,
                grid=(2,),
                in_specs=[pl.BlockSpec((1, hidden, tokens), lambda t, _: (t, 0, 0))]
                + [pl.BlockSpec(w.shape, lambda t, _: (0, 0)) for w in blocks],
                out_specs=pl.BlockSpec((1, 8, rows, tokens), lambda t, _: (t, 0, 0, 0)),
            ),
            out_shape=jax.ShapeDtypeStruct((2, 8, rows, tokens), BF16),
            compiler_params=pltpu.CompilerParams(vmem_limit_bytes=MEMORY),
            cost_estimate=pl.CostEstimate(
                flops=32 * rows * hidden * tokens, bytes_accessed=8 << 20, transcendentals=0
            ),
        )(here, d_pair, *blocks)


def sum_kernel(zh_ref, xhat_ref, gain_ref, *refs):
    parts, (d_ref, moments_ref, share_ref) = refs[:-3], refs[-3:]
    first, second = 0.0, 0.0
    for chunk, ref in zip(CHUNKS, parts, strict=True):
        for k, offset in enumerate(chunk):
            zh = lax.rem(zh_ref[0] + offset, 4)
            for c in range(2):
                total = ref[c * 8, pl.ds(k * SHARD, SHARD), :].astype(F32)
                for m in range(1, 8):
                    total += ref[c * 8 + m, pl.ds(k * SHARD, SHARD), :].astype(F32)
                at = pl.ds(pl.multiple_of((zh * 2 + c) * SHARD, SHARD), SHARD)
                d_ref[at, :] = total
                xhat = xhat_ref[at, :]
                product = total * xhat
                share_ref[at, :] = jnp.sum(product, axis=1, keepdims=True)
                first += jnp.sum(total * gain_ref[at, :], axis=0, keepdims=True)
                second += jnp.sum(product * gain_ref[at, :], axis=0, keepdims=True)
    moments_ref[...] = jnp.concatenate([first, second, jnp.zeros((6, first.shape[1]), F32)], axis=0)


def final_kernel(d_ref, xhat_ref, gain_ref, moments_ref, rstd_ref, out_ref):
    both = moments_ref[0]
    for m in range(1, 8):
        both += moments_ref[m]
    both = both * (1.0 / 3072)
    g = d_ref[...] * gain_ref[...]
    value = rstd_ref[...] * (g - both[0:1] - xhat_ref[...] * both[1:2])
    out_ref[...] = value.T.astype(BF16)


def on_device(tokens, gain, pre_act, w_in, act_cotangent):
    rows, share = tokens.shape
    core = lax.axis_index("c")
    here_y = lax.axis_index("y").astype(jnp.int32).reshape(1)
    here_zh = lax.axis_index("zh").astype(jnp.int32).reshape(1)

    own = lax.all_gather(w_in, "y", axis=0, tiled=True)
    rest = jnp.concatenate([shift(w_in, "zh", 4, k) for k in CHUNKS[1]], axis=0)
    rest, pre_act, act_cotangent, tokens = lax.optimization_barrier(
        (rest, pre_act, act_cotangent, tokens)
    )

    x = tokens.astype(F32).T
    local_mean = jnp.mean(x, axis=0, keepdims=True)
    local_square = jnp.sum((x - local_mean) ** 2, axis=0, keepdims=True)
    stats = spread(jnp.concatenate([local_mean, local_square] * 4, axis=0), MP, 8)
    means, squares = stats[:, 0], stats[:, 1]
    mean = jnp.mean(means, axis=0, keepdims=True)
    variance = (
        jnp.sum(squares, axis=0, keepdims=True)
        + share * jnp.sum((means - mean) ** 2, axis=0, keepdims=True)
    ) / (8 * share)
    rstd = 1.0 / jnp.sqrt(variance + 1e-06)
    xhat = (x - mean) * rstd
    gain_column = gain.astype(F32)[:, None]

    _, gelu_back = jax.vjp(gelu_exact, pre_act.astype(F32))
    d_pre = gelu_back(act_cotangent.astype(F32))[0].astype(BF16).T
    other = lax.ppermute(d_pre, "c", [(0, 1), (1, 0)])
    d_pair = jnp.stack([jnp.where(core == 0, d_pre, other), jnp.where(core == 0, other, d_pre)])

    def exchange(part):
        return lax.all_to_all(part.reshape(16, -1, rows), ("c", "zl", "x"), 0, 0)

    own = products([(0, 0, own)], SHARD, d_pair, here_y * 0, "own")
    rest, own = ring(rest, own)
    parts = [exchange(own), exchange(products(rest, 3 * SHARD, d_pair, here_y, "rest"))]

    whole = lambda shape: pl.BlockSpec(shape, lambda i, _: (0,) * len(shape))
    outs = [
        jax.ShapeDtypeStruct((share, rows), F32),
        jax.ShapeDtypeStruct((8, rows), F32),
        jax.ShapeDtypeStruct((share, 1), F32),
    ]
    d_normed, moments, gain_share = pl.pallas_call(
        sum_kernel,
        grid_spec=pltpu.PrefetchScalarGridSpec(
            num_scalar_prefetch=1,
            grid=(1,),
            in_specs=[whole(a.shape) for a in (xhat, gain_column, *parts)],
            out_specs=[whole(o.shape) for o in outs],
        ),
        out_shape=outs,
        compiler_params=pltpu.CompilerParams(vmem_limit_bytes=MEMORY),
    )(here_zh, xhat, gain_column, *parts)

    gain_share = jnp.pad(gain_share.reshape(3, 128), ((0, 5), (0, 0)))
    gain_share += shift(gain_share, "c", 2, 1)
    gain_gradient = jnp.sum(spread(gain_share, ("y", "zh"), 32), axis=0)[:3].reshape(share)

    moments = spread(moments, MP, 8)
    token_gradient = pl.pallas_call(
        final_kernel,
        out_shape=jax.ShapeDtypeStruct((rows, share), BF16),
        compiler_params=pltpu.CompilerParams(vmem_limit_bytes=MEMORY),
    )(d_normed, xhat, gain_column, moments, rstd)
    return (token_gradient, gain_gradient)


def solution(mesh):
    fine = Mesh(mesh.devices.reshape(SIZES), NAMES)
    placed = (P(DP, MP), P(MP), P(DP, MP), P(DP, MP), P(DP, MP))
    return jax.shard_map(
        on_device, mesh=fine, in_specs=placed, out_specs=(P(DP, MP), P(MP)), check_vma=False
    )
```

```python
import jax
import jax.numpy as jnp
from jax import lax
from jax.experimental import pallas as pl
from jax.experimental.pallas import tpu as pltpu
from jax.sharding import Mesh, PartitionSpec as P

NAMES = ("y", "zh", "c", "zl", "x")
SIZES = (8, 4, 2, 2, 4)
DP, MP = ("y", "zh", "c"), ("zl", "x")
F32, BF16 = jnp.float32, jnp.bfloat16
SHARD = 48
PARAMS = pltpu.CompilerParams(vmem_limit_bytes=40 * 1024 * 1024)
together = lax.optimization_barrier


def gelu_exact(value):
    return jax.nn.gelu(value, approximate=False)


def spread(row, axes, n):
    return lax.all_to_all(jnp.broadcast_to(row, (n,) + row.shape), axes, 0, 0)


def shift(array, axis, n, by):
    return lax.ppermute(array, axis, [(i, (i - by) % n) for i in range(n)])


def both_ways(behind, ahead):
    return shift(behind, "y", 8, -1), shift(ahead, "y", 8, 1)


def product(pieces, offset, d_pair, y, parts):
    _, hidden, tokens = d_pair.shape
    rows = sum(p.shape[0] for p in pieces)
    shape = jax.ShapeDtypeStruct((2, 8, rows, tokens), BF16)

    def kernel(y_ref, d_ref, *refs):
        w_refs, out_ref = refs[: len(pieces)], refs[-1]
        w = jnp.concatenate([r[...] for r in w_refs], axis=0)
        out_ref[0, 0] = jnp.dot(w, d_ref[0], preferred_element_type=F32).astype(BF16)

    return pl.pallas_call(
        kernel,
        grid_spec=pltpu.PrefetchScalarGridSpec(
            num_scalar_prefetch=1,
            grid=(2,),
            in_specs=[pl.BlockSpec((1, hidden, tokens), lambda t, _: (t, 0, 0))]
            + [pl.BlockSpec(p.shape, lambda t, _: (0, 0)) for p in pieces]
            + [pl.BlockSpec(memory_space=pl.ANY)] * (parts is not None),
            out_specs=pl.BlockSpec(
                (1, 1, rows, tokens), lambda t, y: (t, lax.rem(y[0] + offset, 8), 0, 0)
            ),
        ),
        out_shape=shape,
        input_output_aliases={} if parts is None else {2 + len(pieces): 0},
        compiler_params=PARAMS,
        cost_estimate=pl.CostEstimate(
            flops=rows * hidden * tokens, bytes_accessed=1 << 18, transcendentals=0
        ),
    )(y, d_pair, *pieces, *([] if parts is None else [parts]))


def sum_kernel(parts_ref, xhat_ref, gain_ref, d_ref, moments_ref, share_ref):
    first, second = 0.0, 0.0
    for z in range(4):
        for c in range(2):
            total = parts_ref[c * 8, pl.ds(z * SHARD, SHARD), :].astype(F32)
            for m in range(1, 8):
                total += parts_ref[c * 8 + m, pl.ds(z * SHARD, SHARD), :].astype(F32)
            at = pl.ds((z * 2 + c) * SHARD, SHARD)
            d_ref[at, :] = total
            xhat = xhat_ref[at, :]
            product = total * xhat
            share_ref[at, :] = jnp.sum(product, axis=1, keepdims=True)
            first += jnp.sum(total * gain_ref[at, :], axis=0, keepdims=True)
            second += jnp.sum(product * gain_ref[at, :], axis=0, keepdims=True)
    moments_ref[...] = jnp.concatenate([first, second, jnp.zeros((6, first.shape[1]), F32)], axis=0)


def final_kernel(d_ref, xhat_ref, gain_ref, moments_ref, rstd_ref, out_ref):
    both = moments_ref[...] * (1.0 / 3072)
    g = d_ref[...] * gain_ref[...]
    value = rstd_ref[...] * (g - both[0:1] - xhat_ref[...] * both[1:2])
    out_ref[...] = value.T.astype(BF16)


def on_device(tokens, gain, pre_act, w_in, act_cotangent):
    rows, share = tokens.shape
    core = lax.axis_index("c")
    y = lax.axis_index("y").astype(jnp.int32).reshape(1)

    w0 = lax.all_gather(w_in, "zh", axis=0, tiled=True)
    w0, tokens, pre_act, act_cotangent = together((w0, tokens, pre_act, act_cotangent))
    step1 = both_ways(w0, w0)

    _, gelu_back = jax.vjp(gelu_exact, pre_act.astype(F32))
    d_pre = gelu_back(act_cotangent.astype(F32))[0].astype(BF16).T
    x = tokens.astype(F32).T
    local_mean = jnp.mean(x, axis=0, keepdims=True)
    local_square = jnp.sum((x - local_mean) ** 2, axis=0, keepdims=True)
    stats = jnp.concatenate([local_mean, local_square] * 4, axis=0)

    step1, d_pre, stats = together((step1, d_pre, stats))
    step2 = both_ways(*step1)
    other = shift(d_pre, "c", 2, 1)
    stats = spread(stats, MP, 8)

    step2, other, stats = together((step2, other, stats))
    step3 = both_ways(*step2)
    d_pair = jnp.stack([jnp.where(core == 0, d_pre, other), jnp.where(core == 0, other, d_pre)])
    parts = product([w0], 0, d_pair, y, None)
    parts = product([step1[0]], 7, d_pair, y, parts)
    parts = product([step1[1]], 1, d_pair, y, parts)
    parts = product([step2[0]], 6, d_pair, y, parts)
    parts = product([step2[1]], 2, d_pair, y, parts)

    step3, parts = together((step3, parts))
    half = w0.shape[0] // 2
    step4 = both_ways(step3[0][:half], step3[1][half:])
    parts = product([step3[0]], 5, d_pair, y, parts)
    parts = product([step3[1]], 3, d_pair, y, parts)
    means, squares = stats[:, 0], stats[:, 1]
    mean = jnp.mean(means, axis=0, keepdims=True)
    variance = (
        jnp.sum(squares, axis=0, keepdims=True)
        + share * jnp.sum((means - mean) ** 2, axis=0, keepdims=True)
    ) / (8 * share)
    rstd = 1.0 / jnp.sqrt(variance + 1e-06)
    xhat = (x - mean) * rstd

    step4, parts, xhat = together((step4, parts, xhat))
    parts = product(step4, 4, d_pair, y, parts)
    parts = lax.all_to_all(parts.reshape(16, -1, rows), ("c", "zl", "x"), 0, 0)

    gain_column = gain.astype(F32)[:, None]
    d_normed, moments, gain_share = pl.pallas_call(
        sum_kernel,
        out_shape=[
            jax.ShapeDtypeStruct((share, rows), F32),
            jax.ShapeDtypeStruct((8, rows), F32),
            jax.ShapeDtypeStruct((share, 1), F32),
        ],
        compiler_params=PARAMS,
    )(parts, xhat, gain_column)

    gain_share = jnp.pad(gain_share.reshape(3, 128), ((0, 5), (0, 0)))
    gain_gradient = jnp.sum(spread(gain_share, DP, 64), axis=0)[:3].reshape(share)

    moments = lax.psum(moments, MP)
    token_gradient = pl.pallas_call(
        final_kernel,
        out_shape=jax.ShapeDtypeStruct((rows, share), BF16),
        compiler_params=PARAMS,
    )(d_normed, xhat, gain_column, moments, rstd)
    return (token_gradient, gain_gradient)


def solution(mesh):
    fine = Mesh(mesh.devices.reshape(SIZES), NAMES)
    placed = (P(DP, MP), P(MP), P(DP, MP), P(DP, MP), P(DP, MP))
    return jax.shard_map(
        on_device, mesh=fine, in_specs=placed, out_specs=(P(DP, MP), P(MP)), check_vma=False
    )
```

```python
import jax
import jax.numpy as jnp
from jax import lax
from jax.experimental import pallas as pl
from jax.experimental.pallas import tpu as pltpu
from jax.sharding import Mesh, PartitionSpec as P

NAMES = ("y", "zh", "c", "zl", "x")
SIZES = (8, 4, 2, 2, 4)
DP, MP, CHIPS = ("y", "zh", "c"), ("zl", "x"), ("c", "zl", "x")
F32, BF16 = jnp.float32, jnp.bfloat16
SHARD = 48
WIDTH = 3072
PARAMS = pltpu.CompilerParams(vmem_limit_bytes=20 * 1024 * 1024)
together = lax.optimization_barrier


def gelu_exact(value):
    return jax.nn.gelu(value, approximate=False)


def shift(array, axis, n, by):
    return lax.ppermute(array, axis, [(i, (i - by) % n) for i in range(n)])


def partner(array, axis, n, bit):
    return lax.ppermute(array, axis, [(i, i ^ bit) for i in range(n)])


def products(groups, d_own, d_other, place, parts):
    tokens, hidden = d_own.shape
    flat = [p for _, pieces in groups for p in pieces]
    rows, n = sum(p.shape[0] for p in groups[0][1]), len(groups)

    def kernel(place_ref, own_ref, other_ref, *refs):
        w_refs, (out_ref, held, sem) = refs[: len(flat)], refs[-3:]
        w = jnp.concatenate([r[...] for r in w_refs], axis=0)
        copies = []
        for k, d_ref in enumerate((own_ref, other_ref)):
            half = lax.rem(place_ref[1] + k, 2)
            out = lax.dot_general(
                w, d_ref[...], (((1,), (1,)), ((), ())), preferred_element_type=F32
            ).astype(BF16)
            for g, (offset, _) in enumerate(groups):
                held[k, g] = out[g * rows : (g + 1) * rows]
                block = lax.rem(place_ref[0] + offset, 8)
                copies.append(
                    pltpu.make_async_copy(held.at[k, g], out_ref.at[half, block], sem.at[k, g])
                )
                copies[-1].start()
        for copy in copies:
            copy.wait()

    whole = pl.BlockSpec(memory_space=pltpu.VMEM)
    return pl.pallas_call(
        kernel,
        in_specs=[pl.BlockSpec(memory_space=pltpu.SMEM)]
        + [whole] * (2 + len(flat))
        + [pl.BlockSpec(memory_space=pl.ANY)] * (parts is not None),
        out_specs=pl.BlockSpec(memory_space=pl.ANY),
        out_shape=jax.ShapeDtypeStruct((2, 8, rows, tokens), BF16),
        scratch_shapes=[pltpu.VMEM((2, n, rows, tokens), BF16), pltpu.SemaphoreType.DMA((2, n))],
        input_output_aliases={} if parts is None else {3 + len(flat): 0},
        compiler_params=PARAMS,
        cost_estimate=pl.CostEstimate(
            flops=n * rows * hidden * tokens, bytes_accessed=1 << 18, transcendentals=0
        ),
    )(place, d_own, d_other, *flat, *([] if parts is None else [parts]))


def sum_kernel(parts_ref, xhat_ref, gain_ref, d_ref, moments_ref, share_ref):
    first, second = 0.0, 0.0
    for z in range(4):
        for c in range(2):
            total = parts_ref[c * 8, pl.ds(z * SHARD, SHARD), :].astype(F32)
            for m in range(1, 8):
                total += parts_ref[c * 8 + m, pl.ds(z * SHARD, SHARD), :].astype(F32)
            at = pl.ds((z * 2 + c) * SHARD, SHARD)
            xhat, g = xhat_ref[at, :], total * gain_ref[at, :]
            d_ref[at, :] = g
            value = total * xhat
            share_ref[at, :] = value[:, :128] + value[:, 128:256] + value[:, 256:]
            first += jnp.sum(g, axis=0, keepdims=True)
            second += jnp.sum(g * xhat, axis=0, keepdims=True)
    moments_ref[...] = jnp.concatenate([first, second, jnp.zeros((6, first.shape[1]), F32)], axis=0)
    row = jnp.sum(share_ref[...].T, axis=0, keepdims=True)
    share_ref[0:8, :] = jnp.concatenate(
        [row[:, i * 128 : (i + 1) * 128] for i in range(3)] + [jnp.zeros((5, 128), F32)], axis=0
    )


def final_kernel(d_ref, xhat_ref, moments_ref, rstd_ref, out_ref):
    both = moments_ref[...] * (1.0 / WIDTH)
    value = rstd_ref[...] * (d_ref[...] - both[0:1] - xhat_ref[...] * both[1:2])
    out_ref[...] = value.T.astype(BF16)


def on_device(tokens, gain, pre_act, w_in, act_cotangent):
    rows, share = tokens.shape
    here = [lax.axis_index(a).astype(jnp.int32).reshape(1) for a in ("y", "c")]
    place = jnp.concatenate(here)

    def tie(behind, ahead, done, *later):
        (behind_next, _), (ahead_next, _) = together((behind, done)), together((ahead, done))
        return behind_next, ahead_next, *together((behind, ahead, done, *later))[2:]

    w0 = lax.all_gather(w_in, "zh", axis=0, tiled=True)
    w0, pre_act, act_cotangent = together((w0, pre_act, act_cotangent))
    behind1, ahead1 = shift(w0, "y", 8, -1), shift(w0, "y", 8, 1)
    _, gelu_back = jax.vjp(gelu_exact, pre_act.astype(F32))
    d_own = gelu_back(act_cotangent.astype(F32))[0].astype(BF16)

    behind, ahead, d_own = tie(behind1, ahead1, d_own)
    behind2, ahead2 = shift(behind, "y", 8, -1), shift(ahead, "y", 8, 1)
    d_other = partner(d_own, "c", 2, 1)
    parts = products([(0, [w0]), (7, [behind1]), (1, [ahead1])], d_own, d_other, place, None)

    behind, ahead, parts = tie(behind2, ahead2, parts)
    behind3, ahead3 = shift(behind, "y", 8, -1), shift(ahead, "y", 8, 1)
    parts = products([(6, [behind2]), (2, [ahead2])], d_own, d_other, place, parts)

    behind, ahead, parts = tie(behind3, ahead3, parts)
    half = w0.shape[0] // 2
    behind4, ahead4 = shift(behind[:half], "y", 8, -1), shift(ahead[half:], "y", 8, 1)
    parts = products([(5, [behind3]), (3, [ahead3])], d_own, d_other, place, parts)

    behind4, parts, tokens = together((behind4, parts, tokens))
    parts = products([(4, [behind4, ahead4])], d_own, d_other, place, parts)
    parts = lax.all_to_all(parts.reshape(16, share // 2, rows), CHIPS, 0, 0)

    x = tokens.astype(F32).T
    mean = jnp.mean(x, axis=0, keepdims=True)
    square = jnp.sum((x - mean) ** 2, axis=0, keepdims=True)
    for axis, n, bit, count in (("x", 4, 1, 1), ("x", 4, 2, 2), ("zl", 2, 1, 4)):
        other = partner(jnp.concatenate([mean, square] * 4, axis=0), axis, n, bit)
        mean_too, square_too = other[0:1], other[1:2]
        square = square + square_too + (share * count / 2) * (mean - mean_too) ** 2
        mean = (mean + mean_too) * 0.5
    rstd = 1.0 / jnp.sqrt(square * (1.0 / WIDTH) + 1e-06)
    xhat = (x - mean) * rstd

    d_scaled, moments, gain_share = pl.pallas_call(
        sum_kernel,
        out_shape=[
            jax.ShapeDtypeStruct((share, rows), F32),
            jax.ShapeDtypeStruct((8, rows), F32),
            jax.ShapeDtypeStruct((share, 128), F32),
        ],
        compiler_params=PARAMS,
    )(parts, xhat, gain.astype(F32)[:, None])

    gain_share = jnp.broadcast_to(gain_share[:8], (64, 8, 128))
    gain_gradient = jnp.sum(lax.all_to_all(gain_share, DP, 0, 0), axis=0)[:3].reshape(share)

    for axis, n, bit in (("x", 4, 1), ("x", 4, 2), ("zl", 2, 1)):
        moments += partner(moments, axis, n, bit)
    token_gradient = pl.pallas_call(
        final_kernel,
        out_shape=jax.ShapeDtypeStruct((rows, share), BF16),
        compiler_params=PARAMS,
    )(d_scaled, xhat, moments, rstd)
    return (token_gradient, gain_gradient)


def solution(mesh):
    fine = Mesh(mesh.devices.reshape(SIZES), NAMES)
    placed = (P(DP, MP), P(MP), P(DP, MP), P(DP, MP), P(DP, MP))
    return jax.shard_map(
        on_device, mesh=fine, in_specs=placed, out_specs=(P(DP, MP), P(MP)), check_vma=False
    )
```

```python
import jax
import jax.numpy as jnp
from jax import lax
from jax.experimental import pallas as pl
from jax.experimental.pallas import tpu as pltpu
from jax.sharding import Mesh, PartitionSpec as P

NAMES = ("y", "zh", "c", "zl", "x")
SIZES = (8, 4, 2, 2, 4)
DP, MP, CHIPS = ("y", "zh", "c"), ("zl", "x"), ("c", "zl", "x")
F32, BF16 = jnp.float32, jnp.bfloat16
SHARD = 48
WIDTH = 3072
PARAMS = pltpu.CompilerParams(vmem_limit_bytes=20 * 1024 * 1024)
together = lax.optimization_barrier


def gelu_exact(value):
    return jax.nn.gelu(value, approximate=False)


def partner(array, axis, n, bit):
    return lax.ppermute(array, axis, [(i, i ^ bit) for i in range(n)])


def products(groups, d_own, d_other, place, parts):
    tokens, hidden = d_own.shape
    flat = [p for _, pieces in groups for p in pieces]
    rows, n = sum(p.shape[0] for p in groups[0][1]), len(groups)

    def kernel(place_ref, own_ref, other_ref, *refs):
        w_refs, (out_ref, held, sem) = refs[: len(flat)], refs[-3:]
        w = jnp.concatenate([r[...] for r in w_refs], axis=0)
        copies = []
        for k, d_ref in enumerate((own_ref, other_ref)):
            half = lax.rem(place_ref[1] + k, 2)
            out = lax.dot_general(
                w, d_ref[...], (((1,), (1,)), ((), ())), preferred_element_type=F32
            ).astype(BF16)
            for g, (offset, _) in enumerate(groups):
                held[k, g] = out[g * rows : (g + 1) * rows]
                block = lax.rem(place_ref[0] + offset + place_ref[1] * ((8 - 2 * offset) % 8), 8)
                copies.append(
                    pltpu.make_async_copy(held.at[k, g], out_ref.at[half, block], sem.at[k, g])
                )
                copies[-1].start()
        for copy in copies:
            copy.wait()

    whole = pl.BlockSpec(memory_space=pltpu.VMEM)
    return pl.pallas_call(
        kernel,
        in_specs=[pl.BlockSpec(memory_space=pltpu.SMEM)]
        + [whole] * (2 + len(flat))
        + [pl.BlockSpec(memory_space=pl.ANY)] * (parts is not None),
        out_specs=pl.BlockSpec(memory_space=pl.ANY),
        out_shape=jax.ShapeDtypeStruct((2, 8, rows, tokens), BF16),
        scratch_shapes=[pltpu.VMEM((2, n, rows, tokens), BF16), pltpu.SemaphoreType.DMA((2, n))],
        input_output_aliases={} if parts is None else {3 + len(flat): 0},
        compiler_params=PARAMS,
        cost_estimate=pl.CostEstimate(
            flops=n * rows * hidden * tokens, bytes_accessed=1 << 18, transcendentals=0
        ),
    )(place, d_own, d_other, *flat, *([] if parts is None else [parts]))


def sum_kernel(parts_ref, xhat_ref, gain_ref, d_ref, moments_ref, share_ref):
    first, second = 0.0, 0.0
    for z in range(4):
        for c in range(2):
            total = parts_ref[c * 8, pl.ds(z * SHARD, SHARD), :].astype(F32)
            for m in range(1, 8):
                total += parts_ref[c * 8 + m, pl.ds(z * SHARD, SHARD), :].astype(F32)
            at = pl.ds((z * 2 + c) * SHARD, SHARD)
            xhat, g = xhat_ref[at, :], total * gain_ref[at, :]
            d_ref[at, :] = g
            value = total * xhat
            share_ref[at, :] = value[:, :128] + value[:, 128:256] + value[:, 256:]
            first += jnp.sum(g, axis=0, keepdims=True)
            second += jnp.sum(g * xhat, axis=0, keepdims=True)
    moments_ref[...] = jnp.concatenate([first, second, jnp.zeros((6, first.shape[1]), F32)], axis=0)
    row = jnp.sum(share_ref[...].T, axis=0, keepdims=True)
    share_ref[0:8, :] = jnp.concatenate(
        [row[:, i * 128 : (i + 1) * 128] for i in range(3)] + [jnp.zeros((5, 128), F32)], axis=0
    )


def final_kernel(d_ref, xhat_ref, moments_ref, rstd_ref, out_ref):
    both = moments_ref[...] * (1.0 / WIDTH)
    value = rstd_ref[...] * (d_ref[...] - both[0:1] - xhat_ref[...] * both[1:2])
    out_ref[...] = value.T.astype(BF16)


def on_device(tokens, gain, pre_act, w_in, act_cotangent):
    rows, share = tokens.shape
    here = [lax.axis_index(a).astype(jnp.int32).reshape(1) for a in ("y", "c")]
    place = jnp.concatenate(here)

    def step(array, way):
        moves = [((i + way) % 8, i, 0) for i in range(8)] + [((i - way) % 8, i, 1) for i in range(8)]
        return lax.ppermute(array, ("y", "c"), [(a * 2 + c, b * 2 + c) for a, b, c in moves])

    def tie(first, second, done, *later):
        (first_next, _), (second_next, _) = together((first, done)), together((second, done))
        return first_next, second_next, *together((first, second, done, *later))[2:]

    def merge(stats, other, count):
        mean, square = (stats[0:1] + other[0:1]) * 0.5, stats[1:2] + other[1:2]
        square = square + (share * count / 2) * (stats[0:1] - other[0:1]) ** 2
        return jnp.concatenate([mean, square] * 4, axis=0)

    w0 = lax.all_gather(w_in, "zh", axis=0, tiled=True)
    w0, pre_act, act_cotangent = together((w0, pre_act, act_cotangent))
    first1, second1 = step(w0, 1), step(w0, -1)
    _, gelu_back = jax.vjp(gelu_exact, pre_act.astype(F32))
    d_own = gelu_back(act_cotangent.astype(F32))[0].astype(BF16)

    first, second, d_own, tokens = tie(first1, second1, d_own, tokens)
    first2, second2 = step(first, 1), step(second, -1)
    d_other = partner(d_own, "c", 2, 1)
    x = tokens.astype(F32).T
    mean = jnp.mean(x, axis=0, keepdims=True)
    square = jnp.sum((x - mean) ** 2, axis=0, keepdims=True)
    stats = jnp.concatenate([mean, square] * 4, axis=0)
    other = partner(stats, "x", 4, 1)

    first, second, (d_other, stats, other) = tie(first2, second2, (d_other, stats, other))
    first3, second3 = step(first, 1), step(second, -1)
    groups = [(0, [w0]), (1, [first1]), (7, [second1]), (2, [first2]), (6, [second2])]
    parts = products(groups, d_own, d_other, place, None)
    stats = merge(stats, other, 1)
    other = partner(stats, "x", 4, 2)

    first, second, (parts, stats, other) = tie(first3, second3, (parts, stats, other))
    half = w0.shape[0] // 2
    first4, second4 = step(first[:half], 1), step(second[half:], -1)
    parts = products([(3, [first3]), (5, [second3])], d_own, d_other, place, parts)
    stats = merge(stats, other, 2)
    other = partner(stats, "zl", 2, 1)

    first4, parts, stats, other = together((first4, parts, stats, other))
    parts = products([(4, [first4, second4])], d_own, d_other, place, parts)
    parts = lax.all_to_all(parts.reshape(16, share // 2, rows), CHIPS, 0, 0)

    stats = merge(stats, other, 4)
    rstd = 1.0 / jnp.sqrt(stats[1:2] * (1.0 / WIDTH) + 1e-06)
    xhat = (x - stats[0:1]) * rstd

    d_scaled, moments, gain_share = pl.pallas_call(
        sum_kernel,
        out_shape=[
            jax.ShapeDtypeStruct((share, rows), F32),
            jax.ShapeDtypeStruct((8, rows), F32),
            jax.ShapeDtypeStruct((share, 128), F32),
        ],
        compiler_params=PARAMS,
    )(parts, xhat, gain.astype(F32)[:, None])

    gain_share = jnp.broadcast_to(gain_share[:8], (64, 8, 128))
    gain_gradient = jnp.sum(lax.all_to_all(gain_share, DP, 0, 0), axis=0)[:3].reshape(share)

    for axis, n, bit in (("x", 4, 1), ("x", 4, 2), ("zl", 2, 1)):
        moments += partner(moments, axis, n, bit)
    token_gradient = pl.pallas_call(
        final_kernel,
        out_shape=jax.ShapeDtypeStruct((rows, share), BF16),
        compiler_params=PARAMS,
    )(d_scaled, xhat, moments, rstd)
    return (token_gradient, gain_gradient)


def solution(mesh):
    fine = Mesh(mesh.devices.reshape(SIZES), NAMES)
    placed = (P(DP, MP), P(MP), P(DP, MP), P(DP, MP), P(DP, MP))
    return jax.shard_map(
        on_device, mesh=fine, in_specs=placed, out_specs=(P(DP, MP), P(MP)), check_vma=False
    )
```

```python
import jax
import jax.numpy as jnp
from jax import lax
from jax.experimental import pallas as pl
from jax.experimental.pallas import tpu as pltpu
from jax.sharding import Mesh, PartitionSpec as P

NAMES = ("y", "zh", "c", "zl", "x")
SIZES = (8, 4, 2, 2, 4)
DP, MP, CHIPS = ("y", "zh", "c"), ("zl", "x"), ("c", "zl", "x")
F32, BF16 = jnp.float32, jnp.bfloat16
SHARD = 48
WIDTH = 3072
EXTRA = 16
PARAMS = pltpu.CompilerParams(vmem_limit_bytes=20 * 1024 * 1024)
together = lax.optimization_barrier


def gelu_exact(value):
    return jax.nn.gelu(value, approximate=False)


def partner(array, axis, n, bit):
    return lax.ppermute(array, axis, [(i, i ^ bit) for i in range(n)])


def products(groups, d_own, d_other, place, parts, extra=None):
    tokens, hidden = d_own.shape
    weights = [w for _, w in groups]
    rows, n = weights[0].shape[0], len(groups)

    def kernel(place_ref, own_ref, other_ref, *refs):
        w_refs, (out_ref, held, sem, extra_sem) = refs[:n], refs[-4:]
        copies = []
        if extra is not None:
            for t in range(2):
                for m in range(8):
                    to = out_ref.at[t, m, pl.ds(rows, EXTRA)]
                    copies.append(pltpu.make_async_copy(refs[n], to, extra_sem.at[t, m]))
                    copies[-1].start()
        w = jnp.concatenate([r[...] for r in w_refs], axis=0)
        for k, d_ref in enumerate((own_ref, other_ref)):
            half = lax.rem(place_ref[1] + k, 2)
            out = lax.dot_general(
                w, d_ref[...], (((1,), (1,)), ((), ())), preferred_element_type=F32
            ).astype(BF16)
            for g, (offset, _) in enumerate(groups):
                held[k, g] = out[g * rows : (g + 1) * rows]
                block = lax.rem(place_ref[0] + offset + place_ref[1] * ((8 - 2 * offset) % 8), 8)
                to = out_ref.at[half, block, pl.ds(0, rows)]
                copies.append(pltpu.make_async_copy(held.at[k, g], to, sem.at[k, g]))
                copies[-1].start()
        for copy in copies:
            copy.wait()

    whole = pl.BlockSpec(memory_space=pltpu.VMEM)
    more = [] if extra is None else [extra]
    return pl.pallas_call(
        kernel,
        in_specs=[pl.BlockSpec(memory_space=pltpu.SMEM)]
        + [whole] * (2 + n + len(more))
        + [pl.BlockSpec(memory_space=pl.ANY)] * (parts is not None),
        out_specs=pl.BlockSpec(memory_space=pl.ANY),
        out_shape=jax.ShapeDtypeStruct((2, 8, rows + EXTRA, tokens), BF16),
        scratch_shapes=[
            pltpu.VMEM((2, n, rows, tokens), BF16),
            pltpu.SemaphoreType.DMA((2, n)),
            pltpu.SemaphoreType.DMA((2, 8)),
        ],
        input_output_aliases={} if parts is None else {3 + n + len(more): 0},
        compiler_params=PARAMS,
        cost_estimate=pl.CostEstimate(
            flops=n * rows * hidden * tokens, bytes_accessed=1 << 18, transcendentals=0
        ),
    )(place, d_own, d_other, *weights, *more, *([] if parts is None else [parts]))


def tokens_kernel(tokens_ref, x_ref, stats_ref):
    x = tokens_ref[...].astype(F32).T
    x_ref[...] = x
    mean = jnp.sum(x, axis=0, keepdims=True) * (1.0 / x.shape[0])
    square = jnp.sum((x - mean) ** 2, axis=0, keepdims=True)
    rows = []
    for rest in (mean, square):
        for _ in range(3):
            rows.append(rest.astype(BF16).astype(F32))
            rest = rest - rows[-1]
    rows.append(jnp.zeros((EXTRA - 6, x.shape[1]), F32))
    stats_ref[...] = jnp.concatenate(rows, axis=0).astype(BF16)


def sum_kernel(core_ref, parts_ref, x_ref, gain_ref, d_out, xhat_out, moments_ref, share_ref, d_ref, xhat_ref, sem):
    copies = []
    rows, share = parts_ref.shape[1] - EXTRA, x_ref.shape[0]
    means, squares = [], []
    for m in range(8):
        stat = parts_ref[core_ref[0] * 8 + m, pl.ds(rows, EXTRA), :].astype(F32)
        means.append(stat[0:1] + stat[1:2] + stat[2:3])
        squares.append(stat[3:4] + stat[4:5] + stat[5:6])
    mean = sum(means) * 0.125
    variance = (sum(squares) + share * sum((m - mean) ** 2 for m in means)) * (1.0 / WIDTH)
    rstd = 1.0 / jnp.sqrt(variance + 1e-06)
    first, second = 0.0, 0.0
    for z in range(4):
        for c in range(2):
            total = parts_ref[c * 8, pl.ds(z * SHARD, SHARD), :].astype(F32)
            for m in range(1, 8):
                total += parts_ref[c * 8 + m, pl.ds(z * SHARD, SHARD), :].astype(F32)
            at = pl.ds((z * 2 + c) * SHARD, SHARD)
            xhat, g = (x_ref[at, :] - mean) * rstd, total * gain_ref[at, :]
            xhat_ref[at, :] = xhat
            d_ref[at, :] = g
            for k, (held, out) in enumerate(((d_ref, d_out), (xhat_ref, xhat_out))):
                copies.append(pltpu.make_async_copy(held.at[at], out.at[at], sem.at[k, z, c]))
                copies[-1].start()
            value = total * xhat
            share_ref[at, :] = value[:, :128] + value[:, 128:256] + value[:, 256:]
            first += jnp.sum(g, axis=0, keepdims=True)
            second += jnp.sum(g * xhat, axis=0, keepdims=True)
    moments_ref[...] = jnp.concatenate(
        [first, second, rstd * 0.125, jnp.zeros((5, rstd.shape[1]), F32)], axis=0
    )
    row = jnp.sum(share_ref[...].T, axis=0, keepdims=True)
    share_ref[0:8, :] = jnp.concatenate(
        [row[:, i * 128 : (i + 1) * 128] for i in range(3)] + [jnp.zeros((5, 128), F32)], axis=0
    )
    for copy in copies:
        copy.wait()


def final_kernel(d_in, xhat_in, moments_ref, out_ref, d_ref, xhat_ref, sem):
    copies = [
        pltpu.make_async_copy(d_in, d_ref, sem.at[0]),
        pltpu.make_async_copy(xhat_in, xhat_ref, sem.at[1]),
    ]
    for copy in copies:
        copy.start()
    for copy in copies:
        copy.wait()
    both = moments_ref[0:2, :] * (1.0 / WIDTH)
    value = moments_ref[2:3, :] * (d_ref[...] - both[0:1] - xhat_ref[...] * both[1:2])
    out_ref[...] = value.T.astype(BF16)


def on_device(tokens, gain, pre_act, w_in, act_cotangent):
    rows, share = tokens.shape
    here = [lax.axis_index(a).astype(jnp.int32).reshape(1) for a in ("y", "c")]
    place = jnp.concatenate(here)

    def step(array, way):
        moves = [((i + way) % 8, i, 0) for i in range(8)] + [((i - way) % 8, i, 1) for i in range(8)]
        return lax.ppermute(array, ("y", "c"), [(a * 2 + c, b * 2 + c) for a, b, c in moves])

    def tie(first, second, done, *later):
        (first_next, _), (second_next, _) = together((first, done)), together((second, done))
        return first_next, second_next, *together((first, second, done, *later))[2:]

    w0 = lax.all_gather(w_in, "zh", axis=0, tiled=True)
    w0, pre_act, act_cotangent = together((w0, pre_act, act_cotangent))
    first1, second1 = step(w0, 1), step(w0, -1)
    _, gelu_back = jax.vjp(gelu_exact, pre_act.astype(F32))
    d_own = gelu_back(act_cotangent.astype(F32))[0].astype(BF16)

    first, second, d_own, tokens = tie(first1, second1, d_own, tokens)
    first2, second2 = step(first, 1), step(second, -1)
    d_other = partner(d_own, "c", 2, 1)
    x, stats = pl.pallas_call(
        tokens_kernel,
        out_shape=[
            jax.ShapeDtypeStruct((share, rows), F32),
            jax.ShapeDtypeStruct((EXTRA, rows), BF16),
        ],
        compiler_params=PARAMS,
    )(tokens)

    first, second, (d_other, stats) = tie(first2, second2, (d_other, stats))
    first3, second3 = step(first, 1), step(second, -1)
    groups = [(0, w0), (1, first1), (7, second1), (2, first2), (6, second2)]
    parts = products(groups, d_own, d_other, place, None, stats)

    first, second, parts = tie(first3, second3, parts)
    first4 = step(first, 1)
    parts = products([(3, first3), (5, second)], d_own, d_other, place, parts)

    first4, parts = together((first4, parts))
    parts = products([(4, first4)], d_own, d_other, place, parts)
    parts = lax.all_to_all(parts.reshape(16, -1, rows), CHIPS, 0, 0)

    vmem, hbm = pl.BlockSpec(memory_space=pltpu.VMEM), pl.BlockSpec(memory_space=pltpu.HBM)
    d_scaled, xhat, moments, gain_share = pl.pallas_call(
        sum_kernel,
        in_specs=[pl.BlockSpec(memory_space=pltpu.SMEM), vmem, vmem, vmem],
        out_specs=[hbm, hbm, vmem, vmem],
        scratch_shapes=[pltpu.VMEM((share, rows), F32)] * 2 + [pltpu.SemaphoreType.DMA((2, 4, 2))],
        out_shape=[
            jax.ShapeDtypeStruct((share, rows), F32),
            jax.ShapeDtypeStruct((share, rows), F32),
            jax.ShapeDtypeStruct((8, rows), F32),
            jax.ShapeDtypeStruct((share, 128), F32),
        ],
        compiler_params=PARAMS,
    )(here[1], parts, x, gain.astype(F32)[:, None])

    gain_share = jnp.broadcast_to(gain_share[:8], (64, 8, 128))
    gain_gradient = jnp.sum(lax.all_to_all(gain_share, DP, 0, 0), axis=0)[:3].reshape(share)

    for axis, n, bit in (("x", 4, 1), ("x", 4, 2), ("zl", 2, 1)):
        moments += partner(moments, axis, n, bit)
    token_gradient = pl.pallas_call(
        final_kernel,
        in_specs=[hbm, hbm, vmem],
        scratch_shapes=[pltpu.VMEM((share, rows), F32)] * 2 + [pltpu.SemaphoreType.DMA((2,))],
        out_shape=jax.ShapeDtypeStruct((rows, share), BF16),
        compiler_params=pltpu.CompilerParams(vmem_limit_bytes=60 * 1024 * 1024),
    )(d_scaled, xhat, moments)
    return (token_gradient, gain_gradient)


def solution(mesh):
    fine = Mesh(mesh.devices.reshape(SIZES), NAMES)
    placed = (P(DP, MP), P(MP), P(DP, MP), P(DP, MP), P(DP, MP))
    return jax.shard_map(
        on_device, mesh=fine, in_specs=placed, out_specs=(P(DP, MP), P(MP)), check_vma=False
    )
```

```python
import jax
import jax.numpy as jnp
from jax import lax
from jax.experimental import pallas as pl
from jax.experimental.pallas import tpu as pltpu
from jax.sharding import Mesh, PartitionSpec as P

NAMES = ("y", "zh", "c", "zl", "x")
SIZES = (8, 4, 2, 2, 4)
DP, MP, CHIPS = ("y", "zh", "c"), ("zl", "x"), ("c", "zl", "x")
F32, BF16 = jnp.float32, jnp.bfloat16
SHARD = 48
HALF = 1536
PARAMS = pltpu.CompilerParams(vmem_limit_bytes=20 * 1024 * 1024)
together = lax.optimization_barrier


def gelu_exact(value):
    return jax.nn.gelu(value, approximate=False)


def partner(array, axis, n, bit):
    return lax.ppermute(array, axis, [(i, i ^ bit) for i in range(n)])


def products(groups, d_own, d_other, place, parts):
    tokens, hidden = d_own.shape
    weights = [w for _, w in groups]
    rows, n = weights[0].shape[0], len(groups)

    def kernel(place_ref, own_ref, other_ref, *refs):
        w_refs, (out_ref, held, sem) = refs[:n], refs[-3:]
        copies = []
        w = jnp.concatenate([r[...] for r in w_refs], axis=0)
        for k, d_ref in enumerate((own_ref, other_ref)):
            half = lax.rem(place_ref[1] + k, 2)
            out = lax.dot_general(
                w, d_ref[...], (((1,), (1,)), ((), ())), preferred_element_type=F32
            ).astype(BF16)
            for g, (offset, _) in enumerate(groups):
                held[k, g] = out[g * rows : (g + 1) * rows]
                block = lax.rem(place_ref[0] + offset + place_ref[1] * ((8 - 2 * offset) % 8), 8)
                to = out_ref.at[half, block]
                copies.append(pltpu.make_async_copy(held.at[k, g], to, sem.at[k, g]))
                copies[-1].start()
        for copy in copies:
            copy.wait()

    whole = pl.BlockSpec(memory_space=pltpu.VMEM)
    return pl.pallas_call(
        kernel,
        in_specs=[pl.BlockSpec(memory_space=pltpu.SMEM)]
        + [whole] * (2 + n)
        + [pl.BlockSpec(memory_space=pl.ANY)] * (parts is not None),
        out_specs=pl.BlockSpec(memory_space=pl.ANY),
        out_shape=jax.ShapeDtypeStruct((2, 8, rows, tokens), BF16),
        scratch_shapes=[
            pltpu.VMEM((2, n, rows, tokens), BF16),
            pltpu.SemaphoreType.DMA((2, n)),
        ],
        input_output_aliases={} if parts is None else {3 + n: 0},
        compiler_params=PARAMS,
        cost_estimate=pl.CostEstimate(
            flops=1 << 38, bytes_accessed=64 << 20, transcendentals=0
        ),
    )(place, d_own, d_other, *weights, *([] if parts is None else [parts]))


def stats_kernel(x_ref, out_ref):
    for t in range(2):
        total = 0.0
        for m in range(8):
            total += jnp.sum(x_ref[t * 8 + m].astype(F32), axis=0, keepdims=True)
        mean = total * (1.0 / HALF)
        square = 0.0
        for m in range(8):
            centred = x_ref[t * 8 + m].astype(F32) - mean
            square += jnp.sum(centred * centred, axis=0, keepdims=True)
        out_ref[t] = jnp.concatenate([mean, square] * 4, axis=0)


def mean_and_rstd(one, two):
    mean = (one[0:1] + two[0:1]) * 0.5
    between = (one[0:1] - mean) ** 2 + (two[0:1] - mean) ** 2
    variance = (one[1:2] + two[1:2] + HALF * between) * (1.0 / (2 * HALF))
    return mean, 1.0 / jnp.sqrt(variance + 1e-06)


def gain_kernel(parts_ref, x_ref, one_ref, two_ref, out_ref):
    total = 0.0
    for t in range(2):
        mean, rstd = mean_and_rstd(one_ref[t], two_ref[t])
        xhat = (x_ref[t, 0].astype(F32) - mean) * rstd
        value = parts_ref[t, 0].astype(F32) * xhat
        total += value[:, :128] + value[:, 128:256] + value[:, 256:]
    total = jnp.concatenate([total, jnp.zeros((64, 128), F32)], axis=0)
    out_ref[pl.ds(pl.program_id(0), 1), :] = jnp.sum(total.T, axis=0, keepdims=True)


def gain_share(parts, x_all, one, two):
    _, _, rows, tokens = parts.shape
    block = pl.BlockSpec((2, 1, rows, tokens), lambda m: (0, m, 0, 0))
    stat = pl.BlockSpec((2, 8, tokens), lambda m: (0, 0, 0))
    return pl.pallas_call(
        gain_kernel,
        grid=(8,),
        in_specs=[block, block, stat, stat],
        out_specs=pl.BlockSpec((8, 256), lambda m: (0, 0)),
        out_shape=jax.ShapeDtypeStruct((8, 256), F32),
        compiler_params=PARAMS,
    )(parts, x_all.reshape(parts.shape), one, two)


def sum_kernel(core_ref, parts_ref, x_ref, gain_ref, one_ref, two_ref, d_ref, moments_ref):
    mean, rstd = mean_and_rstd(one_ref[core_ref[0]], two_ref[core_ref[0]])
    first, second = 0.0, 0.0
    for z in range(4):
        for c in range(2):
            total = parts_ref[c * 8, pl.ds(z * SHARD, SHARD), :].astype(F32)
            for m in range(1, 8):
                total += parts_ref[c * 8 + m, pl.ds(z * SHARD, SHARD), :].astype(F32)
            at = pl.ds((z * 2 + c) * SHARD, SHARD)
            g = total * gain_ref[at, :]
            d_ref[at, :] = g
            xhat = (x_ref[at, :].astype(F32) - mean) * rstd
            first += jnp.sum(g, axis=0, keepdims=True)
            second += jnp.sum(g * xhat, axis=0, keepdims=True)
    moments_ref[...] = jnp.concatenate([first, second, jnp.zeros((6, first.shape[1]), F32)], axis=0)


def final_kernel(core_ref, d_ref, x_ref, one_ref, two_ref, small_ref, out_ref, gain_ref):
    core = core_ref[0]
    mean, rstd = mean_and_rstd(one_ref[core], two_ref[core])
    both = small_ref[core * 8]
    for m in range(1, 8):
        both += small_ref[core * 8 + m]
    both = both * (1.0 / (2 * HALF))
    xhat = (x_ref[...].astype(F32) - mean) * rstd
    value = rstd * (d_ref[...] - both[0:1] - xhat * both[1:2])
    out_ref[...] = value.T.astype(BF16)
    rows = []
    for c in range(2):
        row = small_ref[c * 8, 2:3]
        for m in range(1, 8):
            row += small_ref[c * 8 + m, 2:3]
        rows.append(row)
    gain_ref[...] = jnp.concatenate(rows + [jnp.zeros((6, row.shape[1]), F32)], axis=0)


def on_device(tokens, gain, pre_act, w_in, act_cotangent):
    rows, share = tokens.shape
    here = [lax.axis_index(a).astype(jnp.int32).reshape(1) for a in ("y", "c")]
    place = jnp.concatenate(here)

    def step(array, way):
        moves = [((i + way) % 8, i, 0) for i in range(8)] + [((i - way) % 8, i, 1) for i in range(8)]
        return lax.ppermute(array, ("y", "c"), [(a * 2 + c, b * 2 + c) for a, b, c in moves])

    def tie(first, second, done, *later):
        (first_next, _), (second_next, _) = together((first, done)), together((second, done))
        return first_next, second_next, *together((first, second, done, *later))[2:]

    w0 = lax.all_gather(w_in, "zh", axis=0, tiled=True)
    w0, pre_act, act_cotangent = together((w0, pre_act, act_cotangent))
    first1, second1 = step(w0, 1), step(w0, -1)
    _, gelu_back = jax.vjp(gelu_exact, pre_act.astype(F32))
    d_own = gelu_back(act_cotangent.astype(F32))[0].astype(BF16)

    first, second, d_own, tokens = tie(first1, second1, d_own, tokens)
    first2, second2 = step(first, 1), step(second, -1)
    d_other = partner(d_own, "c", 2, 1)
    x = tokens.T
    x_all = jnp.swapaxes(x.reshape(4, 2, SHARD, rows), 0, 1).reshape(2, 1, share // 2, rows)
    x_all = jnp.broadcast_to(x_all, (2, 8, share // 2, rows)).reshape(16, share // 2, rows)
    x_all = lax.all_to_all(x_all, CHIPS, 0, 0)
    parts = products([(0, w0), (1, first1), (7, second1)], d_own, d_other, place, None)

    first, second, parts = tie(first2, second2, parts)
    first3, second3 = step(first, 1), step(second, -1)
    parts = products([(2, first2), (6, second2)], d_own, d_other, place, parts)

    first, second, parts = tie(first3, second3, parts)
    first4 = step(first, 1)
    parts = products([(3, first3), (5, second)], d_own, d_other, place, parts)

    first4, parts = together((first4, parts))
    parts = products([(4, first4)], d_own, d_other, place, parts)
    received = lax.all_to_all(parts.reshape(16, share // 2, rows), CHIPS, 0, 0)

    one = pl.pallas_call(
        stats_kernel,
        out_shape=jax.ShapeDtypeStruct((2, 8, rows), F32),
        compiler_params=PARAMS,
    )(x_all)
    two = partner(one, "c", 2, 1)
    shares = gain_share(parts, x_all, one, two)
    for axis, n, bit in (("y", 8, 1), ("y", 8, 2), ("y", 8, 4), ("zh", 4, 1), ("zh", 4, 2)):
        shares += partner(shares, axis, n, bit)

    gain_column = gain.astype(F32)[:, None]
    vmem = pl.BlockSpec(memory_space=pltpu.VMEM)
    smem = pl.BlockSpec(memory_space=pltpu.SMEM)
    d_scaled, moments = pl.pallas_call(
        sum_kernel,
        in_specs=[smem] + [vmem] * 5,
        out_shape=[
            jax.ShapeDtypeStruct((share, rows), F32),
            jax.ShapeDtypeStruct((8, rows), F32),
        ],
        compiler_params=PARAMS,
    )(here[1], received, x, gain_column, one, two)

    small = jnp.concatenate(
        [
            jnp.broadcast_to(moments[None, :2], (8, 2, rows)),
            jnp.pad(shares, ((0, 0), (0, rows - 256)))[:, None],
            jnp.zeros((8, 5, rows), F32),
        ],
        axis=1,
    )
    small = lax.all_to_all(jnp.concatenate([small, small], axis=0), CHIPS, 0, 0)
    token_gradient, gain_rows = pl.pallas_call(
        final_kernel,
        in_specs=[smem] + [vmem] * 5,
        out_shape=[
            jax.ShapeDtypeStruct((rows, share), BF16),
            jax.ShapeDtypeStruct((8, rows), F32),
        ],
        compiler_params=PARAMS,
    )(here[1], d_scaled, x, one, two, small)
    gain_gradient = jnp.swapaxes(gain_rows[:2, : share // 2].reshape(2, 4, SHARD), 0, 1).reshape(share)
    return (token_gradient, gain_gradient)


def solution(mesh):
    fine = Mesh(mesh.devices.reshape(SIZES), NAMES)
    placed = (P(DP, MP), P(MP), P(DP, MP), P(DP, MP), P(DP, MP))
    return jax.shard_map(
        on_device, mesh=fine, in_specs=placed, out_specs=(P(DP, MP), P(MP)), check_vma=False
    )
```

```python
import jax
import jax.numpy as jnp
from jax import lax
from jax.experimental import pallas as pl
from jax.experimental.pallas import tpu as pltpu
from jax.sharding import Mesh, PartitionSpec as P

NAMES = ("y", "zh", "c", "zl", "x")
SIZES = (8, 4, 2, 2, 4)
DP, MP, CHIPS = ("y", "zh", "c"), ("zl", "x"), ("c", "zl", "x")
F32, BF16 = jnp.float32, jnp.bfloat16
SHARD = 48
HALF = 1536
PARAMS = pltpu.CompilerParams(vmem_limit_bytes=20 * 1024 * 1024)
together = lax.optimization_barrier


def gelu_exact(value):
    return jax.nn.gelu(value, approximate=False)


def partner(array, axis, n, bit):
    return lax.ppermute(array, axis, [(i, i ^ bit) for i in range(n)])


def products(groups, d_own, d_other, place, parts):
    tokens, hidden = d_own.shape
    weights = [w for _, w in groups]
    rows, n = weights[0].shape[0], len(groups)

    def kernel(place_ref, own_ref, other_ref, *refs):
        w_refs, (out_ref, held, sem) = refs[:n], refs[-3:]
        copies = []
        w = jnp.concatenate([r[...] for r in w_refs], axis=0)
        for k, d_ref in enumerate((own_ref, other_ref)):
            half = lax.rem(place_ref[1] + k, 2)
            out = lax.dot_general(
                w, d_ref[...], (((1,), (1,)), ((), ())), preferred_element_type=F32
            ).astype(BF16)
            for g, (offset, _) in enumerate(groups):
                held[k, g] = out[g * rows : (g + 1) * rows]
                block = lax.rem(place_ref[0] + offset + place_ref[1] * ((8 - 2 * offset) % 8), 8)
                to = out_ref.at[half, block]
                copies.append(pltpu.make_async_copy(held.at[k, g], to, sem.at[k, g]))
                copies[-1].start()
        for copy in copies:
            copy.wait()

    whole = pl.BlockSpec(memory_space=pltpu.VMEM)
    return pl.pallas_call(
        kernel,
        in_specs=[pl.BlockSpec(memory_space=pltpu.SMEM)]
        + [whole] * (2 + n)
        + [pl.BlockSpec(memory_space=pl.ANY)] * (parts is not None),
        out_specs=pl.BlockSpec(memory_space=pl.ANY),
        out_shape=jax.ShapeDtypeStruct((2, 8, rows, tokens), BF16),
        scratch_shapes=[
            pltpu.VMEM((2, n, rows, tokens), BF16),
            pltpu.SemaphoreType.DMA((2, n)),
        ],
        input_output_aliases={} if parts is None else {3 + n: 0},
        compiler_params=PARAMS,
        cost_estimate=pl.CostEstimate(
            flops=1 << 38, bytes_accessed=64 << 20, transcendentals=0
        ),
    )(place, d_own, d_other, *weights, *([] if parts is None else [parts]))


def stats_kernel(x_ref, out_ref):
    for t in range(2):
        total = 0.0
        for m in range(8):
            total += jnp.sum(x_ref[t * 8 + m].astype(F32), axis=0, keepdims=True)
        mean = total * (1.0 / HALF)
        square = 0.0
        for m in range(8):
            centred = x_ref[t * 8 + m].astype(F32) - mean
            square += jnp.sum(centred * centred, axis=0, keepdims=True)
        out_ref[t] = jnp.concatenate([mean, square] * 4, axis=0)


def mean_and_rstd(one, two):
    mean = (one[0:1] + two[0:1]) * 0.5
    between = (one[0:1] - mean) ** 2 + (two[0:1] - mean) ** 2
    variance = (one[1:2] + two[1:2] + HALF * between) * (1.0 / (2 * HALF))
    return mean, 1.0 / jnp.sqrt(variance + 1e-06)


def gain_kernel(parts_ref, x_ref, one_ref, two_ref, out_ref):
    total = 0.0
    for t in range(2):
        mean, rstd = mean_and_rstd(one_ref[t], two_ref[t])
        xhat = (x_ref[t, 0].astype(F32) - mean) * rstd
        value = parts_ref[t, 0].astype(F32) * xhat
        total += value[:, :128] + value[:, 128:256] + value[:, 256:]
    total = jnp.concatenate([total, jnp.zeros((64, 128), F32)], axis=0)
    out_ref[pl.ds(pl.program_id(0), 1), :] = jnp.sum(total.T, axis=0, keepdims=True)


def gain_share(parts, x_all, one, two):
    _, _, rows, tokens = parts.shape
    block = pl.BlockSpec((2, 1, rows, tokens), lambda m: (0, m, 0, 0))
    stat = pl.BlockSpec((2, 8, tokens), lambda m: (0, 0, 0))
    return pl.pallas_call(
        gain_kernel,
        grid=(8,),
        in_specs=[block, block, stat, stat],
        out_specs=pl.BlockSpec((8, 256), lambda m: (0, 0)),
        out_shape=jax.ShapeDtypeStruct((8, 256), F32),
        compiler_params=PARAMS,
    )(parts, x_all.reshape(parts.shape), one, two)


def sum_kernel(core_ref, parts_ref, x_ref, gain_ref, one_ref, two_ref, d_ref, moments_ref):
    mean, rstd = mean_and_rstd(one_ref[core_ref[0]], two_ref[core_ref[0]])
    first, second = 0.0, 0.0
    for z in range(4):
        for c in range(2):
            total = parts_ref[c * 8, pl.ds(z * SHARD, SHARD), :].astype(F32)
            for m in range(1, 8):
                total += parts_ref[c * 8 + m, pl.ds(z * SHARD, SHARD), :].astype(F32)
            at = pl.ds((z * 2 + c) * SHARD, SHARD)
            g = total * gain_ref[at, :]
            d_ref[at, :] = g
            xhat = (x_ref[at, :].astype(F32) - mean) * rstd
            first += jnp.sum(g, axis=0, keepdims=True)
            second += jnp.sum(g * xhat, axis=0, keepdims=True)
    rows = [m[:, i * 128 : (i + 1) * 128] for m in (first, second) for i in range(3)]
    moments_ref[...] = jnp.concatenate(rows + [jnp.zeros((2, 128), F32)], axis=0)


def final_kernel(here_ref, d_ref, x_ref, one_ref, two_ref, small_ref, out_ref, gain_ref):
    core, zh = here_ref[0], here_ref[1]
    mean, rstd = mean_and_rstd(one_ref[core], two_ref[core])
    total = small_ref[zh * 16 + core * 8]
    for m in range(1, 8):
        total += small_ref[zh * 16 + core * 8 + m]
    total = total * (1.0 / (2 * HALF))
    first, second = (jnp.concatenate([total[k + i : k + i + 1] for i in range(3)], axis=1) for k in (0, 3))
    xhat = (x_ref[...].astype(F32) - mean) * rstd
    value = rstd * (d_ref[...] - first - xhat * second)
    out_ref[...] = value.T.astype(BF16)
    rows = []
    for c in range(2):
        both = jnp.zeros((8, 128), F32)
        for z in range(4):
            for m in range(8):
                both += small_ref[z * 16 + c * 8 + m]
        rows.append(jnp.concatenate([both[6:7], both[7:8]], axis=1))
    gain_ref[...] = jnp.concatenate(rows + [jnp.zeros((6, 256), F32)], axis=0)


def on_device(tokens, gain, pre_act, w_in, act_cotangent):
    rows, share = tokens.shape
    here = [lax.axis_index(a).astype(jnp.int32).reshape(1) for a in ("y", "c")]
    place = jnp.concatenate(here)

    def step(array, way):
        moves = [((i + way) % 8, i, 0) for i in range(8)] + [((i - way) % 8, i, 1) for i in range(8)]
        return lax.ppermute(array, ("y", "c"), [(a * 2 + c, b * 2 + c) for a, b, c in moves])

    def tie(first, second, done, *later):
        (first_next, _), (second_next, _) = together((first, done)), together((second, done))
        return first_next, second_next, *together((first, second, done, *later))[2:]

    w0 = lax.all_gather(w_in, "zh", axis=0, tiled=True)
    w0, pre_act, act_cotangent = together((w0, pre_act, act_cotangent))
    first1, second1 = step(w0, 1), step(w0, -1)
    _, gelu_back = jax.vjp(gelu_exact, pre_act.astype(F32))
    d_own = gelu_back(act_cotangent.astype(F32))[0].astype(BF16)

    first, second, d_own, tokens = tie(first1, second1, d_own, tokens)
    first2, second2 = step(first, 1), step(second, -1)
    d_other = partner(d_own, "c", 2, 1)
    x = tokens.T
    x_all = jnp.swapaxes(x.reshape(4, 2, SHARD, rows), 0, 1).reshape(2, 1, share // 2, rows)
    x_all = jnp.broadcast_to(x_all, (2, 8, share // 2, rows)).reshape(16, share // 2, rows)
    x_all = lax.all_to_all(x_all, CHIPS, 0, 0)
    parts = products([(0, w0)], d_own, d_other, place, None)

    first, second, parts = tie(first2, second2, parts)
    first3, second3 = step(first, 1), step(second, -1)
    groups = [(1, first1), (7, second1), (2, first2), (6, second2)]
    parts = products(groups, d_own, d_other, place, parts)

    first, second, parts = tie(first3, second3, parts)
    first4 = step(first, 1)
    parts = products([(3, first3), (5, second)], d_own, d_other, place, parts)

    one = pl.pallas_call(
        stats_kernel,
        out_shape=jax.ShapeDtypeStruct((2, 8, rows), F32),
        compiler_params=PARAMS,
    )(x_all)
    two = partner(one, "c", 2, 1)

    first4, parts, one, two = together((first4, parts, one, two))
    parts = products([(4, first4)], d_own, d_other, place, parts)
    received = lax.all_to_all(parts.reshape(16, share // 2, rows), CHIPS, 0, 0)

    shares = gain_share(parts, x_all, one, two)
    for bit in (1, 2, 4):
        shares += partner(shares, "y", 8, bit)

    vmem, smem = pl.BlockSpec(memory_space=pltpu.VMEM), pl.BlockSpec(memory_space=pltpu.SMEM)
    d_scaled, moments = pl.pallas_call(
        sum_kernel,
        in_specs=[smem] + [vmem] * 5,
        out_shape=[
            jax.ShapeDtypeStruct((share, rows), F32),
            jax.ShapeDtypeStruct((8, 128), F32),
        ],
        compiler_params=PARAMS,
    )(here[1], received, x, gain.astype(F32)[:, None], one, two)

    small = jnp.concatenate(
        [jnp.broadcast_to(moments[None, :6], (8, 6, 128)), shares.reshape(8, 2, 128)], axis=1
    )
    small = jnp.broadcast_to(small, (8, 8, 8, 128)).reshape(64, 8, 128)
    small = lax.all_to_all(small, ("zh",) + CHIPS, 0, 0)
    token_gradient, gain_rows = pl.pallas_call(
        final_kernel,
        in_specs=[smem] + [vmem] * 5,
        out_shape=[
            jax.ShapeDtypeStruct((rows, share), BF16),
            jax.ShapeDtypeStruct((8, 256), F32),
        ],
        compiler_params=PARAMS,
    )(jnp.concatenate([here[1], lax.axis_index("zh").astype(jnp.int32).reshape(1)]), d_scaled, x, one, two, small)
    gain_gradient = jnp.swapaxes(gain_rows[:2, : share // 2].reshape(2, 4, SHARD), 0, 1).reshape(share)
    return (token_gradient, gain_gradient)


def solution(mesh):
    fine = Mesh(mesh.devices.reshape(SIZES), NAMES)
    placed = (P(DP, MP), P(MP), P(DP, MP), P(DP, MP), P(DP, MP))
    return jax.shard_map(
        on_device, mesh=fine, in_specs=placed, out_specs=(P(DP, MP), P(MP)), check_vma=False
    )
```

```python
import jax
import jax.numpy as jnp
from jax import lax
from jax.experimental import pallas as pl
from jax.experimental.pallas import tpu as pltpu
from jax.sharding import Mesh, PartitionSpec as P

NAMES = ("y", "zh", "c", "zl", "x")
SIZES = (8, 4, 2, 2, 4)
DP, MP, CHIPS = ("y", "zh", "c"), ("zl", "x"), ("c", "zl", "x")
F32, BF16 = jnp.float32, jnp.bfloat16
SHARD = 48
HALF = 1536
PARAMS = pltpu.CompilerParams(vmem_limit_bytes=20 * 1024 * 1024)
WIDE = pltpu.CompilerParams(vmem_limit_bytes=52 * 1024 * 1024)
together = lax.optimization_barrier


def gelu_exact(value):
    return jax.nn.gelu(value, approximate=False)


def partner(array, axis, n, bit):
    return lax.ppermute(array, axis, [(i, i ^ bit) for i in range(n)])


def products(groups, d_own, d_other, place, parts):
    tokens, hidden = d_own.shape
    weights = [w for _, w in groups]
    rows, n = weights[0].shape[0], len(groups)

    def kernel(place_ref, own_ref, other_ref, *refs):
        w_refs, (out_ref, held, sem) = refs[:n], refs[-3:]
        copies = []
        w = jnp.concatenate([r[...] for r in w_refs], axis=0)
        for k, d_ref in enumerate((own_ref, other_ref)):
            half = lax.rem(place_ref[1] + k, 2)
            out = lax.dot_general(
                w, d_ref[...], (((1,), (1,)), ((), ())), preferred_element_type=F32
            ).astype(BF16)
            for g, (offset, _) in enumerate(groups):
                held[k, g] = out[g * rows : (g + 1) * rows]
                block = lax.rem(place_ref[0] + offset + place_ref[1] * ((8 - 2 * offset) % 8), 8)
                to = out_ref.at[half, block]
                copies.append(pltpu.make_async_copy(held.at[k, g], to, sem.at[k, g]))
                copies[-1].start()
        for copy in copies:
            copy.wait()

    whole = pl.BlockSpec(memory_space=pltpu.VMEM)
    return pl.pallas_call(
        kernel,
        in_specs=[pl.BlockSpec(memory_space=pltpu.SMEM)]
        + [whole] * (2 + n)
        + [pl.BlockSpec(memory_space=pl.ANY)] * (parts is not None),
        out_specs=pl.BlockSpec(memory_space=pl.ANY),
        out_shape=jax.ShapeDtypeStruct((2, 8, rows, tokens), BF16),
        scratch_shapes=[
            pltpu.VMEM((2, n, rows, tokens), BF16),
            pltpu.SemaphoreType.DMA((2, n)),
        ],
        input_output_aliases={} if parts is None else {3 + n: 0},
        compiler_params=WIDE,
        cost_estimate=pl.CostEstimate(
            flops=1 << 38, bytes_accessed=64 << 20, transcendentals=0
        ),
    )(place, d_own, d_other, *weights, *([] if parts is None else [parts]))


def tokens_kernel(tokens_ref, x_ref, send_ref, held, sem):
    x = tokens_ref[...].astype(F32).T.astype(BF16)
    x_ref[...] = x
    copies = []
    for c in range(2):
        for z in range(4):
            held[c, pl.ds(z * SHARD, SHARD)] = x[(z * 2 + c) * SHARD : (z * 2 + c + 1) * SHARD]
        for m in range(8):
            copies.append(pltpu.make_async_copy(held.at[c], send_ref.at[c, m], sem.at[c, m]))
            copies[-1].start()
    for copy in copies:
        copy.wait()


def transposed(tokens):
    rows, share = tokens.shape
    return pl.pallas_call(
        tokens_kernel,
        out_specs=[pl.BlockSpec(memory_space=pltpu.VMEM), pl.BlockSpec(memory_space=pl.ANY)],
        out_shape=[
            jax.ShapeDtypeStruct((share, rows), BF16),
            jax.ShapeDtypeStruct((2, 8, share // 2, rows), BF16),
        ],
        scratch_shapes=[
            pltpu.VMEM((2, share // 2, rows), BF16),
            pltpu.SemaphoreType.DMA((2, 8)),
        ],
        compiler_params=PARAMS,
    )(tokens)


def stats_kernel(x_ref, out_ref):
    for t in range(2):
        total = 0.0
        for m in range(8):
            total += jnp.sum(x_ref[t * 8 + m].astype(F32), axis=0, keepdims=True)
        mean = total * (1.0 / HALF)
        square = 0.0
        for m in range(8):
            centred = x_ref[t * 8 + m].astype(F32) - mean
            square += jnp.sum(centred * centred, axis=0, keepdims=True)
        out_ref[t] = jnp.concatenate([mean, square] * 4, axis=0)


def mean_and_rstd(one, two):
    mean = (one[0:1] + two[0:1]) * 0.5
    between = (one[0:1] - mean) ** 2 + (two[0:1] - mean) ** 2
    variance = (one[1:2] + two[1:2] + HALF * between) * (1.0 / (2 * HALF))
    return mean, 1.0 / jnp.sqrt(variance + 1e-06)


def gain_kernel(parts_ref, x_ref, one_ref, two_ref, out_ref, stat_ref):
    @pl.when(pl.program_id(0) == 0)
    def _():
        for t in range(2):
            mean, rstd = mean_and_rstd(one_ref[t], two_ref[t])
            stat_ref[t] = jnp.concatenate([mean, rstd] * 4, axis=0)

    total = 0.0
    for t in range(2):
        xhat = (x_ref[t, 0].astype(F32) - stat_ref[t, 0:1]) * stat_ref[t, 1:2]
        value = parts_ref[t, 0].astype(F32) * xhat
        total += value[:, :128] + value[:, 128:256] + value[:, 256:]
    total = jnp.concatenate([total, jnp.zeros((64, 128), F32)], axis=0)
    out_ref[pl.ds(pl.program_id(0), 1), :] = jnp.sum(total.T, axis=0, keepdims=True)


def gain_share(parts, x_all, one, two):
    _, _, rows, tokens = parts.shape
    block = pl.BlockSpec((2, 1, rows, tokens), lambda m: (0, m, 0, 0))
    stat = pl.BlockSpec((2, 8, tokens), lambda m: (0, 0, 0))
    return pl.pallas_call(
        gain_kernel,
        grid=(8,),
        in_specs=[block, block, stat, stat],
        out_specs=pl.BlockSpec((8, 256), lambda m: (0, 0)),
        scratch_shapes=[pltpu.VMEM((2, 8, tokens), F32)],
        out_shape=jax.ShapeDtypeStruct((8, 256), F32),
        compiler_params=WIDE,
    )(parts, x_all.reshape(parts.shape), one, two)


def sum_kernel(core_ref, parts_ref, x_ref, gain_ref, one_ref, two_ref, d_ref, moments_ref):
    mean, rstd = mean_and_rstd(one_ref[core_ref[0]], two_ref[core_ref[0]])
    first, second = 0.0, 0.0
    for z in range(4):
        for c in range(2):
            total = parts_ref[c * 8, pl.ds(z * SHARD, SHARD), :].astype(F32)
            for m in range(1, 8):
                total += parts_ref[c * 8 + m, pl.ds(z * SHARD, SHARD), :].astype(F32)
            at = pl.ds((z * 2 + c) * SHARD, SHARD)
            g = total * gain_ref[at, :]
            d_ref[at, :] = g
            xhat = (x_ref[at, :].astype(F32) - mean) * rstd
            first += jnp.sum(g, axis=0, keepdims=True)
            second += jnp.sum(g * xhat, axis=0, keepdims=True)
    rows = [m[:, i * 128 : (i + 1) * 128] for m in (first, second) for i in range(3)]
    moments_ref[...] = jnp.concatenate(rows + [jnp.zeros((2, 128), F32)], axis=0)


def final_kernel(here_ref, d_ref, x_ref, one_ref, two_ref, small_ref, out_ref, gain_ref):
    core, zh = here_ref[0], here_ref[1]
    mean, rstd = mean_and_rstd(one_ref[core], two_ref[core])
    total = small_ref[zh * 16 + core * 8]
    for m in range(1, 8):
        total += small_ref[zh * 16 + core * 8 + m]
    total = total * (1.0 / (2 * HALF))
    first, second = (jnp.concatenate([total[k + i : k + i + 1] for i in range(3)], axis=1) for k in (0, 3))
    xhat = (x_ref[...].astype(F32) - mean) * rstd
    value = rstd * (d_ref[...] - first - xhat * second)
    out_ref[...] = value.T.astype(BF16)
    rows = []
    for c in range(2):
        both = jnp.zeros((8, 128), F32)
        for z in range(4):
            for m in range(8):
                both += small_ref[z * 16 + c * 8 + m]
        rows.append(jnp.concatenate([both[6:7], both[7:8]], axis=1))
    gain_ref[...] = jnp.concatenate(rows + [jnp.zeros((6, 256), F32)], axis=0)


def on_device(tokens, gain, pre_act, w_in, act_cotangent):
    rows, share = tokens.shape
    here = [lax.axis_index(a).astype(jnp.int32).reshape(1) for a in ("y", "c")]
    place = jnp.concatenate(here)

    def step(array, way):
        moves = [((i + way) % 8, i, 0) for i in range(8)] + [((i - way) % 8, i, 1) for i in range(8)]
        return lax.ppermute(array, ("y", "c"), [(a * 2 + c, b * 2 + c) for a, b, c in moves])

    def tie(first, second, done, *later):
        (first_next, _), (second_next, _) = together((first, done)), together((second, done))
        return first_next, second_next, *together((first, second, done, *later))[2:]

    w0 = lax.all_to_all(jnp.broadcast_to(w_in, (4,) + w_in.shape), "zh", 0, 0).reshape(-1, w_in.shape[1])
    w0, pre_act, act_cotangent, tokens = together((w0, pre_act, act_cotangent, tokens))
    first1, second1 = step(w0, 1), step(w0, -1)
    _, gelu_back = jax.vjp(gelu_exact, pre_act.astype(F32))
    d_own = gelu_back(act_cotangent.astype(F32))[0].astype(BF16)

    x, x_all = transposed(tokens)

    first, second, (d_own, x_all) = tie(first1, second1, (d_own, x_all))
    first2, second2 = step(first, 1), step(second, -1)
    d_other = partner(d_own, "c", 2, 1)
    x_all = lax.all_to_all(x_all.reshape(16, share // 2, rows), CHIPS, 0, 0)
    parts = products([(0, w0)], d_own, d_other, place, None)

    first, second, parts = tie(first2, second2, parts)
    first3, second3 = step(first, 1), step(second, -1)
    groups = [(1, first1), (7, second1), (2, first2), (6, second2)]
    parts = products(groups, d_own, d_other, place, parts)

    first, second, parts = tie(first3, second3, parts)
    first4 = step(first, 1)
    parts = products([(3, first3), (5, second)], d_own, d_other, place, parts)

    one = pl.pallas_call(
        stats_kernel,
        out_shape=jax.ShapeDtypeStruct((2, 8, rows), F32),
        compiler_params=PARAMS,
    )(x_all)
    two = partner(one, "c", 2, 1)

    first4, parts, one, two = together((first4, parts, one, two))
    parts = products([(4, first4)], d_own, d_other, place, parts)
    received = lax.all_to_all(parts.reshape(16, share // 2, rows), CHIPS, 0, 0)

    shares = gain_share(parts, x_all, one, two)
    for bit in (1, 2, 4):
        shares += partner(shares, "y", 8, bit)

    vmem, smem = pl.BlockSpec(memory_space=pltpu.VMEM), pl.BlockSpec(memory_space=pltpu.SMEM)
    d_scaled, moments = pl.pallas_call(
        sum_kernel,
        in_specs=[smem] + [vmem] * 5,
        out_shape=[
            jax.ShapeDtypeStruct((share, rows), F32),
            jax.ShapeDtypeStruct((8, 128), F32),
        ],
        compiler_params=PARAMS,
    )(here[1], received, x, gain.astype(F32)[:, None], one, two)

    small = jnp.concatenate(
        [jnp.broadcast_to(moments[None, :6], (8, 6, 128)), shares.reshape(8, 2, 128)], axis=1
    )
    small = jnp.broadcast_to(small, (8, 8, 8, 128)).reshape(64, 8, 128)
    small = lax.all_to_all(small, ("zh",) + CHIPS, 0, 0)
    token_gradient, gain_rows = pl.pallas_call(
        final_kernel,
        in_specs=[smem] + [vmem] * 5,
        out_shape=[
            jax.ShapeDtypeStruct((rows, share), BF16),
            jax.ShapeDtypeStruct((8, 256), F32),
        ],
        compiler_params=PARAMS,
    )(jnp.concatenate([here[1], lax.axis_index("zh").astype(jnp.int32).reshape(1)]), d_scaled, x, one, two, small)
    gain_gradient = jnp.swapaxes(gain_rows[:2, : share // 2].reshape(2, 4, SHARD), 0, 1).reshape(share)
    return (token_gradient, gain_gradient)


def solution(mesh):
    fine = Mesh(mesh.devices.reshape(SIZES), NAMES)
    placed = (P(DP, MP), P(MP), P(DP, MP), P(DP, MP), P(DP, MP))
    return jax.shard_map(
        on_device, mesh=fine, in_specs=placed, out_specs=(P(DP, MP), P(MP)), check_vma=False
    )
```

```python
import jax
import jax.numpy as jnp
from jax import lax
from jax.experimental import pallas as pl
from jax.experimental.pallas import tpu as pltpu
from jax.sharding import Mesh, PartitionSpec as P

NAMES = ("y", "zh", "c", "zl", "x")
SIZES = (8, 4, 2, 2, 4)
DP, MP, CHIPS = ("y", "zh", "c"), ("zl", "x"), ("c", "zl", "x")
F32, BF16 = jnp.float32, jnp.bfloat16
SHARD = 48
HALF = 1536
PARAMS = pltpu.CompilerParams(vmem_limit_bytes=20 * 1024 * 1024)
WIDE = pltpu.CompilerParams(vmem_limit_bytes=52 * 1024 * 1024)
together = lax.optimization_barrier


def gelu_exact(value):
    return jax.nn.gelu(value, approximate=False)


def partner(array, axis, n, bit):
    return lax.ppermute(array, axis, [(i, i ^ bit) for i in range(n)])


def products(groups, d_own, d_other, place, parts):
    tokens, hidden = d_own.shape
    weights = [w for _, w in groups]
    rows, n = weights[0].shape[0], len(groups)

    def kernel(place_ref, own_ref, other_ref, *refs):
        w_refs, (out_ref, held, sem) = refs[:n], refs[-3:]
        copies = []
        w = jnp.concatenate([r[...] for r in w_refs], axis=0)
        for k, d_ref in enumerate((own_ref, other_ref)):
            half = lax.rem(place_ref[1] + k, 2)
            out = lax.dot_general(
                w, d_ref[...], (((1,), (1,)), ((), ())), preferred_element_type=F32
            ).astype(BF16)
            for g, (offset, _) in enumerate(groups):
                held[k, g] = out[g * rows : (g + 1) * rows]
                block = lax.rem(place_ref[0] + offset + place_ref[1] * ((8 - 2 * offset) % 8), 8)
                to = out_ref.at[half, block]
                copies.append(pltpu.make_async_copy(held.at[k, g], to, sem.at[k, g]))
                copies[-1].start()
        for copy in copies:
            copy.wait()

    whole = pl.BlockSpec(memory_space=pltpu.VMEM)
    return pl.pallas_call(
        kernel,
        in_specs=[pl.BlockSpec(memory_space=pltpu.SMEM)]
        + [whole] * (2 + n)
        + [pl.BlockSpec(memory_space=pl.ANY)] * (parts is not None),
        out_specs=pl.BlockSpec(memory_space=pl.ANY),
        out_shape=jax.ShapeDtypeStruct((2, 8, rows, tokens), BF16),
        scratch_shapes=[
            pltpu.VMEM((2, n, rows, tokens), BF16),
            pltpu.SemaphoreType.DMA((2, n)),
        ],
        input_output_aliases={} if parts is None else {3 + n: 0},
        compiler_params=WIDE,
        cost_estimate=pl.CostEstimate(
            flops=1 << 38, bytes_accessed=64 << 20, transcendentals=0
        ),
    )(place, d_own, d_other, *weights, *([] if parts is None else [parts]))


def tokens_kernel(tokens_ref, x_ref, send_ref, held, sem):
    x = tokens_ref[...].astype(F32).T.astype(BF16)
    x_ref[...] = x
    copies = []
    for c in range(2):
        for z in range(4):
            held[c, pl.ds(z * SHARD, SHARD)] = x[(z * 2 + c) * SHARD : (z * 2 + c + 1) * SHARD]
        for m in range(8):
            copies.append(pltpu.make_async_copy(held.at[c], send_ref.at[c, m], sem.at[c, m]))
            copies[-1].start()
    for copy in copies:
        copy.wait()


def transposed(tokens):
    rows, share = tokens.shape
    return pl.pallas_call(
        tokens_kernel,
        out_specs=[pl.BlockSpec(memory_space=pltpu.VMEM), pl.BlockSpec(memory_space=pl.ANY)],
        out_shape=[
            jax.ShapeDtypeStruct((share, rows), BF16),
            jax.ShapeDtypeStruct((2, 8, share // 2, rows), BF16),
        ],
        scratch_shapes=[
            pltpu.VMEM((2, share // 2, rows), BF16),
            pltpu.SemaphoreType.DMA((2, 8)),
        ],
        compiler_params=PARAMS,
    )(tokens)


def stats_kernel(x_ref, out_ref):
    for t in range(2):
        total = 0.0
        for m in range(8):
            total += jnp.sum(x_ref[t * 8 + m].astype(F32), axis=0, keepdims=True)
        mean = total * (1.0 / HALF)
        square = 0.0
        for m in range(8):
            centred = x_ref[t * 8 + m].astype(F32) - mean
            square += jnp.sum(centred * centred, axis=0, keepdims=True)
        out_ref[t] = jnp.concatenate([mean, square] * 4, axis=0)


def mean_and_rstd(one, two):
    mean = (one[0:1] + two[0:1]) * 0.5
    between = (one[0:1] - mean) ** 2 + (two[0:1] - mean) ** 2
    variance = (one[1:2] + two[1:2] + HALF * between) * (1.0 / (2 * HALF))
    return mean, 1.0 / jnp.sqrt(variance + 1e-06)


def gain_kernel(parts_ref, x_ref, one_ref, two_ref, out_ref, stat_ref):
    @pl.when(pl.program_id(0) == 0)
    def _():
        for t in range(2):
            mean, rstd = mean_and_rstd(one_ref[t], two_ref[t])
            stat_ref[t] = jnp.concatenate([mean, rstd] * 4, axis=0)

    per_step = x_ref.shape[1]
    for k in range(per_step):
        total = jnp.zeros((x_ref.shape[2], 128), F32)
        for t in range(2):
            xhat = (x_ref[t, k].astype(F32) - stat_ref[t, 0:1]) * stat_ref[t, 1:2]
            value = parts_ref[t, k].astype(F32) * xhat
            total += value[:, :128] + value[:, 128:256] + value[:, 256:]
        total = jnp.concatenate([total, jnp.zeros((64, 128), F32)], axis=0)
        row = jnp.sum(total.T, axis=0, keepdims=True)
        out_ref[pl.ds(pl.program_id(0) * per_step + k, 1), :] = row


def gain_share(parts, x_all, one, two):
    _, _, rows, tokens = parts.shape
    block = pl.BlockSpec((2, 2, rows, tokens), lambda m: (0, m, 0, 0))
    stat = pl.BlockSpec((2, 8, tokens), lambda m: (0, 0, 0))
    return pl.pallas_call(
        gain_kernel,
        grid=(4,),
        in_specs=[block, block, stat, stat],
        out_specs=pl.BlockSpec((8, 256), lambda m: (0, 0)),
        scratch_shapes=[pltpu.VMEM((2, 8, tokens), F32)],
        out_shape=jax.ShapeDtypeStruct((8, 256), F32),
        compiler_params=WIDE,
    )(parts, x_all.reshape(parts.shape), one, two)


def sum_kernel(core_ref, parts_ref, x_ref, gain_ref, one_ref, two_ref, d_ref, moments_ref):
    mean, rstd = mean_and_rstd(one_ref[core_ref[0]], two_ref[core_ref[0]])
    first, second = 0.0, 0.0
    for z in range(4):
        for c in range(2):
            total = parts_ref[c * 8, pl.ds(z * SHARD, SHARD), :].astype(F32)
            for m in range(1, 8):
                total += parts_ref[c * 8 + m, pl.ds(z * SHARD, SHARD), :].astype(F32)
            at = pl.ds((z * 2 + c) * SHARD, SHARD)
            g = total * gain_ref[at, :]
            d_ref[at, :] = g
            xhat = (x_ref[at, :].astype(F32) - mean) * rstd
            first += jnp.sum(g, axis=0, keepdims=True)
            second += jnp.sum(g * xhat, axis=0, keepdims=True)
    rows = [m[:, i * 128 : (i + 1) * 128] for m in (first, second) for i in range(3)]
    moments_ref[...] = jnp.concatenate(rows + [jnp.zeros((2, 128), F32)], axis=0)


def final_kernel(here_ref, d_ref, x_ref, one_ref, two_ref, small_ref, out_ref, gain_ref):
    core, zh = here_ref[0], here_ref[1]
    mean, rstd = mean_and_rstd(one_ref[core], two_ref[core])
    total = small_ref[zh * 16 + core * 8]
    for m in range(1, 8):
        total += small_ref[zh * 16 + core * 8 + m]
    total = total * (1.0 / (2 * HALF))
    first, second = (jnp.concatenate([total[k + i : k + i + 1] for i in range(3)], axis=1) for k in (0, 3))
    xhat = (x_ref[...].astype(F32) - mean) * rstd
    value = rstd * (d_ref[...] - first - xhat * second)
    out_ref[...] = value.T.astype(BF16)
    rows = []
    for c in range(2):
        both = jnp.zeros((8, 128), F32)
        for z in range(4):
            for m in range(8):
                both += small_ref[z * 16 + c * 8 + m]
        rows.append(jnp.concatenate([both[6:7], both[7:8]], axis=1))
    gain_ref[...] = jnp.concatenate(rows + [jnp.zeros((6, 256), F32)], axis=0)


def on_device(tokens, gain, pre_act, w_in, act_cotangent):
    rows, share = tokens.shape
    here = [lax.axis_index(a).astype(jnp.int32).reshape(1) for a in ("y", "c")]
    place = jnp.concatenate(here)

    def step(array, way):
        moves = [((i + way) % 8, i, 0) for i in range(8)] + [((i - way) % 8, i, 1) for i in range(8)]
        return lax.ppermute(array, ("y", "c"), [(a * 2 + c, b * 2 + c) for a, b, c in moves])

    def tie(first, second, done, *later):
        (first_next, _), (second_next, _) = together((first, done)), together((second, done))
        return first_next, second_next, *together((first, second, done, *later))[2:]

    w0 = lax.all_gather(w_in, "zh", axis=0, tiled=True)
    w0, pre_act, act_cotangent, tokens = together((w0, pre_act, act_cotangent, tokens))
    first1, second1 = step(w0, 1), step(w0, -1)
    _, gelu_back = jax.vjp(gelu_exact, pre_act.astype(F32))
    d_own = gelu_back(act_cotangent.astype(F32))[0].astype(BF16)

    x, x_all = transposed(tokens)

    first, second, (d_own, x_all) = tie(first1, second1, (d_own, x_all))
    first2, second2 = step(first, 1), step(second, -1)
    d_other = partner(d_own, "c", 2, 1)
    x_all = lax.all_to_all(x_all.reshape(16, share // 2, rows), CHIPS, 0, 0)
    parts = products([(0, w0)], d_own, d_other, place, None)

    first, second, parts = tie(first2, second2, parts)
    first3, second3 = step(first, 1), step(second, -1)
    groups = [(1, first1), (7, second1), (2, first2), (6, second2)]
    parts = products(groups, d_own, d_other, place, parts)

    first, second, parts = tie(first3, second3, parts)
    first4 = step(first, 1)
    parts = products([(3, first3), (5, second)], d_own, d_other, place, parts)

    first4, parts = together((first4, parts))
    parts = products([(4, first4)], d_own, d_other, place, parts)
    received = lax.all_to_all(parts.reshape(16, share // 2, rows), CHIPS, 0, 0)

    one = pl.pallas_call(
        stats_kernel,
        out_shape=jax.ShapeDtypeStruct((2, 8, rows), F32),
        compiler_params=PARAMS,
    )(x_all)
    two = partner(one, "c", 2, 1)
    shares = lax.psum(gain_share(parts, x_all, one, two), "y")

    vmem, smem = pl.BlockSpec(memory_space=pltpu.VMEM), pl.BlockSpec(memory_space=pltpu.SMEM)
    d_scaled, moments = pl.pallas_call(
        sum_kernel,
        in_specs=[smem] + [vmem] * 5,
        out_shape=[
            jax.ShapeDtypeStruct((share, rows), F32),
            jax.ShapeDtypeStruct((8, 128), F32),
        ],
        compiler_params=PARAMS,
    )(here[1], received, x, gain.astype(F32)[:, None], one, two)

    small = jnp.concatenate(
        [jnp.broadcast_to(moments[None, :6], (8, 6, 128)), shares.reshape(8, 2, 128)], axis=1
    )
    small = jnp.broadcast_to(small, (8, 8, 8, 128)).reshape(64, 8, 128)
    small = lax.all_to_all(small, ("zh",) + CHIPS, 0, 0)
    token_gradient, gain_rows = pl.pallas_call(
        final_kernel,
        in_specs=[smem] + [vmem] * 5,
        out_shape=[
            jax.ShapeDtypeStruct((rows, share), BF16),
            jax.ShapeDtypeStruct((8, 256), F32),
        ],
        compiler_params=PARAMS,
    )(jnp.concatenate([here[1], lax.axis_index("zh").astype(jnp.int32).reshape(1)]), d_scaled, x, one, two, small)
    gain_gradient = jnp.swapaxes(gain_rows[:2, : share // 2].reshape(2, 4, SHARD), 0, 1).reshape(share)
    return (token_gradient, gain_gradient)


def solution(mesh):
    fine = Mesh(mesh.devices.reshape(SIZES), NAMES)
    placed = (P(DP, MP), P(MP), P(DP, MP), P(DP, MP), P(DP, MP))
    return jax.shard_map(
        on_device, mesh=fine, in_specs=placed, out_specs=(P(DP, MP), P(MP)), check_vma=False
    )
```

```python
import jax
import jax.numpy as jnp
from jax import lax
from jax.experimental import pallas as pl
from jax.experimental.pallas import tpu as pltpu
from jax.sharding import Mesh, PartitionSpec as P

NAMES = ("y", "zh", "c", "zl", "x")
SIZES = (8, 4, 2, 2, 4)
DP, MP, CHIPS = ("y", "zh", "c"), ("zl", "x"), ("c", "zl", "x")
F32, BF16 = jnp.float32, jnp.bfloat16
SHARD = 48
HALF = 1536
PARAMS = pltpu.CompilerParams(vmem_limit_bytes=20 * 1024 * 1024)
WIDE = pltpu.CompilerParams(vmem_limit_bytes=52 * 1024 * 1024)
together = lax.optimization_barrier


def gelu_exact(value):
    return jax.nn.gelu(value, approximate=False)


def partner(array, axis, n, bit):
    return lax.ppermute(array, axis, [(i, i ^ bit) for i in range(n)])


def products(groups, d_own, d_other, place, parts):
    tokens, hidden = d_own.shape
    weights = [w for _, w in groups]
    rows, n = weights[0].shape[0], len(groups)

    def kernel(place_ref, own_ref, other_ref, *refs):
        w_refs, (out_ref, held, sem) = refs[:n], refs[-3:]
        copies = []
        w = jnp.concatenate([r[...] for r in w_refs], axis=0)
        for k, d_ref in enumerate((own_ref, other_ref)):
            half = lax.rem(place_ref[1] + k, 2)
            out = lax.dot_general(
                w, d_ref[...], (((1,), (1,)), ((), ())), preferred_element_type=F32
            ).astype(BF16)
            for g, (offset, _) in enumerate(groups):
                held[k, g] = out[g * rows : (g + 1) * rows]
                block = lax.rem(place_ref[0] + offset + place_ref[1] * ((8 - 2 * offset) % 8), 8)
                to = out_ref.at[half, block]
                copies.append(pltpu.make_async_copy(held.at[k, g], to, sem.at[k, g]))
                copies[-1].start()
        for copy in copies:
            copy.wait()

    whole = pl.BlockSpec(memory_space=pltpu.VMEM)
    return pl.pallas_call(
        kernel,
        in_specs=[pl.BlockSpec(memory_space=pltpu.SMEM)]
        + [whole] * (2 + n)
        + [pl.BlockSpec(memory_space=pl.ANY)] * (parts is not None),
        out_specs=pl.BlockSpec(memory_space=pl.ANY),
        out_shape=jax.ShapeDtypeStruct((2, 8, rows, tokens), BF16),
        scratch_shapes=[
            pltpu.VMEM((2, n, rows, tokens), BF16),
            pltpu.SemaphoreType.DMA((2, n)),
        ],
        input_output_aliases={} if parts is None else {3 + n: 0},
        compiler_params=WIDE,
        cost_estimate=pl.CostEstimate(
            flops=1 << 38, bytes_accessed=64 << 20, transcendentals=0
        ),
    )(place, d_own, d_other, *weights, *([] if parts is None else [parts]))


def tokens_kernel(tokens_ref, x_ref, send_ref, held, sem):
    x = tokens_ref[...].astype(F32).T.astype(BF16)
    x_ref[...] = x
    copies = []
    for c in range(2):
        for z in range(4):
            held[c, pl.ds(z * SHARD, SHARD)] = x[(z * 2 + c) * SHARD : (z * 2 + c + 1) * SHARD]
        for m in range(8):
            copies.append(pltpu.make_async_copy(held.at[c], send_ref.at[c, m], sem.at[c, m]))
            copies[-1].start()
    for copy in copies:
        copy.wait()


def transposed(tokens):
    rows, share = tokens.shape
    return pl.pallas_call(
        tokens_kernel,
        out_specs=[pl.BlockSpec(memory_space=pltpu.VMEM), pl.BlockSpec(memory_space=pl.ANY)],
        out_shape=[
            jax.ShapeDtypeStruct((share, rows), BF16),
            jax.ShapeDtypeStruct((2, 8, share // 2, rows), BF16),
        ],
        scratch_shapes=[
            pltpu.VMEM((2, share // 2, rows), BF16),
            pltpu.SemaphoreType.DMA((2, 8)),
        ],
        compiler_params=PARAMS,
    )(tokens)


def stats_kernel(x_ref, out_ref):
    for t in range(2):
        total = 0.0
        for m in range(8):
            total += jnp.sum(x_ref[t * 8 + m].astype(F32), axis=0, keepdims=True)
        mean = total * (1.0 / HALF)
        square = 0.0
        for m in range(8):
            centred = x_ref[t * 8 + m].astype(F32) - mean
            square += jnp.sum(centred * centred, axis=0, keepdims=True)
        out_ref[t] = jnp.concatenate([mean, square] * 4, axis=0)


def mean_and_rstd(one, two):
    mean = (one[0:1] + two[0:1]) * 0.5
    between = (one[0:1] - mean) ** 2 + (two[0:1] - mean) ** 2
    variance = (one[1:2] + two[1:2] + HALF * between) * (1.0 / (2 * HALF))
    return mean, 1.0 / jnp.sqrt(variance + 1e-06)


def gain_kernel(parts_ref, x_ref, one_ref, two_ref, out_ref, stat_ref):
    @pl.when(pl.program_id(0) == 0)
    def _():
        for t in range(2):
            mean, rstd = mean_and_rstd(one_ref[t], two_ref[t])
            stat_ref[t] = jnp.concatenate([mean, rstd] * 4, axis=0)

    per_step = x_ref.shape[1]
    for k in range(per_step):
        total = jnp.zeros((x_ref.shape[2], 128), F32)
        for t in range(2):
            xhat = (x_ref[t, k].astype(F32) - stat_ref[t, 0:1]) * stat_ref[t, 1:2]
            value = parts_ref[t, k].astype(F32) * xhat
            total += value[:, :128] + value[:, 128:256] + value[:, 256:]
        total = jnp.concatenate([total, jnp.zeros((64, 128), F32)], axis=0)
        row = jnp.sum(total.T, axis=0, keepdims=True)
        out_ref[pl.ds(pl.program_id(0) * per_step + k, 1), :] = row


def gain_share(parts, x_all, one, two):
    _, _, rows, tokens = parts.shape
    block = pl.BlockSpec((2, 2, rows, tokens), lambda m: (0, m, 0, 0))
    stat = pl.BlockSpec((2, 8, tokens), lambda m: (0, 0, 0))
    return pl.pallas_call(
        gain_kernel,
        grid=(4,),
        in_specs=[block, block, stat, stat],
        out_specs=pl.BlockSpec((8, 256), lambda m: (0, 0)),
        scratch_shapes=[pltpu.VMEM((2, 8, tokens), F32)],
        out_shape=jax.ShapeDtypeStruct((8, 256), F32),
        compiler_params=WIDE,
    )(parts, x_all.reshape(parts.shape), one, two)


def sum_kernel(core_ref, parts_ref, x_ref, gain_ref, one_ref, two_ref, d_ref, moments_ref):
    mean, rstd = mean_and_rstd(one_ref[core_ref[0]], two_ref[core_ref[0]])
    first, second = 0.0, 0.0
    for z in range(4):
        for c in range(2):
            total = parts_ref[c * 8, pl.ds(z * SHARD, SHARD), :].astype(F32)
            for m in range(1, 8):
                total += parts_ref[c * 8 + m, pl.ds(z * SHARD, SHARD), :].astype(F32)
            at = pl.ds((z * 2 + c) * SHARD, SHARD)
            g = total * gain_ref[at, :]
            d_ref[at, :] = g
            xhat = (x_ref[at, :].astype(F32) - mean) * rstd
            first += jnp.sum(g, axis=0, keepdims=True)
            second += jnp.sum(g * xhat, axis=0, keepdims=True)
    rows = [m[:, i * 128 : (i + 1) * 128] for m in (first, second) for i in range(3)]
    moments_ref[...] = jnp.concatenate(rows + [jnp.zeros((2, 128), F32)], axis=0)


def final_kernel(here_ref, d_ref, x_ref, one_ref, two_ref, small_ref, out_ref, gain_ref):
    core = here_ref[0]
    mean, rstd = mean_and_rstd(one_ref[core], two_ref[core])
    total = small_ref[core * 8]
    for m in range(1, 8):
        total += small_ref[core * 8 + m]
    total = total * (1.0 / (2 * HALF))
    first, second = (jnp.concatenate([total[k + i : k + i + 1] for i in range(3)], axis=1) for k in (0, 3))
    xhat = (x_ref[...].astype(F32) - mean) * rstd
    value = rstd * (d_ref[...] - first - xhat * second)
    out_ref[...] = value.T.astype(BF16)
    rows = []
    for c in range(2):
        both = jnp.zeros((8, 128), F32)
        for m in range(8):
            both += small_ref[c * 8 + m]
        rows.append(jnp.concatenate([both[6:7], both[7:8]], axis=1))
    gain_ref[...] = jnp.concatenate(rows + [jnp.zeros((6, 256), F32)], axis=0)


def on_device(tokens, gain, pre_act, w_in, act_cotangent):
    rows, share = tokens.shape
    here = [lax.axis_index(a).astype(jnp.int32).reshape(1) for a in ("y", "c")]
    place = jnp.concatenate(here)

    def step(array, way):
        moves = [((i + way) % 8, i, 0) for i in range(8)] + [((i - way) % 8, i, 1) for i in range(8)]
        return lax.ppermute(array, ("y", "c"), [(a * 2 + c, b * 2 + c) for a, b, c in moves])

    def tie(first, second, done, *later):
        (first_next, _), (second_next, _) = together((first, done)), together((second, done))
        return first_next, second_next, *together((first, second, done, *later))[2:]

    w0 = lax.all_gather(w_in, "zh", axis=0, tiled=True)
    w0, pre_act, act_cotangent, tokens = together((w0, pre_act, act_cotangent, tokens))
    first1, second1 = step(w0, 1), step(w0, -1)
    _, gelu_back = jax.vjp(gelu_exact, pre_act.astype(F32))
    d_own = gelu_back(act_cotangent.astype(F32))[0].astype(BF16)

    x, x_all = transposed(tokens)

    first, second, (d_own, x_all) = tie(first1, second1, (d_own, x_all))
    first2, second2 = step(first, 1), step(second, -1)
    d_other = partner(d_own, "c", 2, 1)
    x_all = lax.all_to_all(x_all.reshape(16, share // 2, rows), CHIPS, 0, 0)
    parts = products([(0, w0)], d_own, d_other, place, None)

    first, second, parts = tie(first2, second2, parts)
    first3, second3 = step(first, 1), step(second, -1)
    groups = [(1, first1), (7, second1), (2, first2), (6, second2)]
    parts = products(groups, d_own, d_other, place, parts)

    first, second, parts = tie(first3, second3, parts)
    first4 = step(first, 1)
    parts = products([(3, first3), (5, second)], d_own, d_other, place, parts)

    parts, x_all = together((parts, x_all))
    one = pl.pallas_call(
        stats_kernel,
        out_shape=jax.ShapeDtypeStruct((2, 8, rows), F32),
        compiler_params=PARAMS,
    )(x_all)

    first4, parts, one = together((first4, parts, one))
    parts = products([(4, first4)], d_own, d_other, place, parts)
    received = lax.all_to_all(parts.reshape(16, share // 2, rows), CHIPS, 0, 0)

    two = partner(one, "c", 2, 1)
    shares = lax.psum(lax.psum(gain_share(parts, x_all, one, two), "y"), "zh")

    vmem, smem = pl.BlockSpec(memory_space=pltpu.VMEM), pl.BlockSpec(memory_space=pltpu.SMEM)
    d_scaled, moments = pl.pallas_call(
        sum_kernel,
        in_specs=[smem] + [vmem] * 5,
        out_shape=[
            jax.ShapeDtypeStruct((share, rows), F32),
            jax.ShapeDtypeStruct((8, 128), F32),
        ],
        compiler_params=PARAMS,
    )(here[1], received, x, gain.astype(F32)[:, None], one, two)

    small = jnp.concatenate(
        [jnp.broadcast_to(moments[None, :6], (8, 6, 128)), shares.reshape(8, 2, 128)], axis=1
    )
    small = lax.all_to_all(jnp.concatenate([small, small], axis=0), CHIPS, 0, 0)
    token_gradient, gain_rows = pl.pallas_call(
        final_kernel,
        in_specs=[smem] + [vmem] * 5,
        out_shape=[
            jax.ShapeDtypeStruct((rows, share), BF16),
            jax.ShapeDtypeStruct((8, 256), F32),
        ],
        compiler_params=PARAMS,
    )(here[1], d_scaled, x, one, two, small)
    gain_gradient = jnp.swapaxes(gain_rows[:2, : share // 2].reshape(2, 4, SHARD), 0, 1).reshape(share)
    return (token_gradient, gain_gradient)


def solution(mesh):
    fine = Mesh(mesh.devices.reshape(SIZES), NAMES)
    placed = (P(DP, MP), P(MP), P(DP, MP), P(DP, MP), P(DP, MP))
    return jax.shard_map(
        on_device, mesh=fine, in_specs=placed, out_specs=(P(DP, MP), P(MP)), check_vma=False
    )
```

```python
import jax
import jax.numpy as jnp
from jax import lax
from jax.experimental import pallas as pl
from jax.experimental.pallas import tpu as pltpu
from jax.sharding import Mesh, PartitionSpec as P

NAMES = ("y", "zh", "c", "zl", "x")
SIZES = (8, 4, 2, 2, 4)
DP, MP, CHIPS = ("y", "zh", "c"), ("zl", "x"), ("c", "zl", "x")
F32, BF16 = jnp.float32, jnp.bfloat16
SHARD = 48
HALF = 1536
PARAMS = pltpu.CompilerParams(vmem_limit_bytes=20 * 1024 * 1024)
WIDE = pltpu.CompilerParams(vmem_limit_bytes=52 * 1024 * 1024)
together = lax.optimization_barrier


def gelu_exact(value):
    return jax.nn.gelu(value, approximate=False)


def partner(array, axis, n, bit):
    return lax.ppermute(array, axis, [(i, i ^ bit) for i in range(n)])


def products(groups, d_own, d_other, place, parts, long=False):
    tokens, hidden = d_own.shape
    weights = [w for _, w in groups]
    rows, n = weights[0].shape[0], len(groups)

    def kernel(place_ref, own_ref, other_ref, *refs):
        w_refs, (out_ref, held, sem) = refs[:n], refs[-3:]
        copies = []
        w = jnp.concatenate([r[...] for r in w_refs], axis=0)
        for k, d_ref in enumerate((own_ref, other_ref)):
            half = lax.rem(place_ref[1] + k, 2)
            out = lax.dot_general(
                w, d_ref[...], (((1,), (1,)), ((), ())), preferred_element_type=F32
            ).astype(BF16)
            for g, (offset, _) in enumerate(groups):
                held[k, g] = out[g * rows : (g + 1) * rows]
                block = lax.rem(place_ref[0] + offset + place_ref[1] * ((8 - 2 * offset) % 8), 8)
                to = out_ref.at[half, block]
                copies.append(pltpu.make_async_copy(held.at[k, g], to, sem.at[k, g]))
                copies[-1].start()
        for copy in copies:
            copy.wait()

    whole = pl.BlockSpec(memory_space=pltpu.VMEM)
    return pl.pallas_call(
        kernel,
        in_specs=[pl.BlockSpec(memory_space=pltpu.SMEM)]
        + [whole] * (2 + n)
        + [pl.BlockSpec(memory_space=pl.ANY)] * (parts is not None),
        out_specs=pl.BlockSpec(memory_space=pl.ANY),
        out_shape=jax.ShapeDtypeStruct((2, 8, rows, tokens), BF16),
        scratch_shapes=[
            pltpu.VMEM((2, n, rows, tokens), BF16),
            pltpu.SemaphoreType.DMA((2, n)),
        ],
        input_output_aliases={} if parts is None else {3 + n: 0},
        compiler_params=WIDE,
        cost_estimate=pl.CostEstimate(
            flops=1 << 38 if long else rows * hidden * tokens, bytes_accessed=1 << 18, transcendentals=0
        ),
    )(place, d_own, d_other, *weights, *([] if parts is None else [parts]))


def tokens_kernel(tokens_ref, x_ref, send_ref, held, sem):
    x = tokens_ref[...].astype(F32).T.astype(BF16)
    x_ref[...] = x
    copies = []
    for c in range(2):
        for z in range(4):
            held[c, pl.ds(z * SHARD, SHARD)] = x[(z * 2 + c) * SHARD : (z * 2 + c + 1) * SHARD]
        for m in range(8):
            copies.append(pltpu.make_async_copy(held.at[c], send_ref.at[c, m], sem.at[c, m]))
            copies[-1].start()
    for copy in copies:
        copy.wait()


def transposed(tokens):
    rows, share = tokens.shape
    return pl.pallas_call(
        tokens_kernel,
        out_specs=[pl.BlockSpec(memory_space=pltpu.VMEM), pl.BlockSpec(memory_space=pl.ANY)],
        out_shape=[
            jax.ShapeDtypeStruct((share, rows), BF16),
            jax.ShapeDtypeStruct((2, 8, share // 2, rows), BF16),
        ],
        scratch_shapes=[
            pltpu.VMEM((2, share // 2, rows), BF16),
            pltpu.SemaphoreType.DMA((2, 8)),
        ],
        compiler_params=PARAMS,
    )(tokens)


def stats_kernel(x_ref, out_ref):
    for t in range(2):
        total = 0.0
        for m in range(8):
            total += jnp.sum(x_ref[t * 8 + m].astype(F32), axis=0, keepdims=True)
        mean = total * (1.0 / HALF)
        square = 0.0
        for m in range(8):
            centred = x_ref[t * 8 + m].astype(F32) - mean
            square += jnp.sum(centred * centred, axis=0, keepdims=True)
        out_ref[t] = jnp.concatenate([mean, square] * 4, axis=0)


def mean_and_rstd(one, two):
    mean = (one[0:1] + two[0:1]) * 0.5
    between = (one[0:1] - mean) ** 2 + (two[0:1] - mean) ** 2
    variance = (one[1:2] + two[1:2] + HALF * between) * (1.0 / (2 * HALF))
    return mean, 1.0 / jnp.sqrt(variance + 1e-06)


def gain_kernel(parts_ref, x_ref, one_ref, two_ref, out_ref, stat_ref):
    @pl.when(pl.program_id(0) == 0)
    def _():
        for t in range(2):
            mean, rstd = mean_and_rstd(one_ref[t], two_ref[t])
            stat_ref[t] = jnp.concatenate([mean, rstd] * 4, axis=0)

    per_step = x_ref.shape[1]
    for k in range(per_step):
        total = jnp.zeros((x_ref.shape[2], 128), F32)
        for t in range(2):
            xhat = (x_ref[t, k].astype(F32) - stat_ref[t, 0:1]) * stat_ref[t, 1:2]
            value = parts_ref[t, k].astype(F32) * xhat
            total += value[:, :128] + value[:, 128:256] + value[:, 256:]
        total = jnp.concatenate([total, jnp.zeros((64, 128), F32)], axis=0)
        row = jnp.sum(total.T, axis=0, keepdims=True)
        out_ref[pl.ds(pl.program_id(0) * per_step + k, 1), :] = row


def gain_share(parts, x_all, one, two):
    _, _, rows, tokens = parts.shape
    block = pl.BlockSpec((2, 2, rows, tokens), lambda m: (0, m, 0, 0))
    stat = pl.BlockSpec((2, 8, tokens), lambda m: (0, 0, 0))
    return pl.pallas_call(
        gain_kernel,
        grid=(4,),
        in_specs=[block, block, stat, stat],
        out_specs=pl.BlockSpec((8, 256), lambda m: (0, 0)),
        scratch_shapes=[pltpu.VMEM((2, 8, tokens), F32)],
        out_shape=jax.ShapeDtypeStruct((8, 256), F32),
        compiler_params=WIDE,
    )(parts, x_all.reshape(parts.shape), one, two)


def sum_kernel(core_ref, parts_ref, x_ref, gain_ref, one_ref, two_ref, d_ref, moments_ref):
    mean, rstd = mean_and_rstd(one_ref[core_ref[0]], two_ref[core_ref[0]])
    first, second = 0.0, 0.0
    for z in range(4):
        for c in range(2):
            total = parts_ref[c * 8, pl.ds(z * SHARD, SHARD), :].astype(F32)
            for m in range(1, 8):
                total += parts_ref[c * 8 + m, pl.ds(z * SHARD, SHARD), :].astype(F32)
            at = pl.ds((z * 2 + c) * SHARD, SHARD)
            g = total * gain_ref[at, :]
            d_ref[at, :] = g
            xhat = (x_ref[at, :].astype(F32) - mean) * rstd
            first += jnp.sum(g, axis=0, keepdims=True)
            second += jnp.sum(g * xhat, axis=0, keepdims=True)
    rows = [m[:, i * 128 : (i + 1) * 128] for m in (first, second) for i in range(3)]
    moments_ref[...] = jnp.concatenate(rows + [jnp.zeros((2, 128), F32)], axis=0)


def final_kernel(here_ref, d_ref, x_ref, one_ref, two_ref, small_ref, out_ref, gain_ref):
    core = here_ref[0]
    mean, rstd = mean_and_rstd(one_ref[core], two_ref[core])
    total = small_ref[core * 8]
    for m in range(1, 8):
        total += small_ref[core * 8 + m]
    total = total * (1.0 / (2 * HALF))
    first, second = (jnp.concatenate([total[k + i : k + i + 1] for i in range(3)], axis=1) for k in (0, 3))
    xhat = (x_ref[...].astype(F32) - mean) * rstd
    value = rstd * (d_ref[...] - first - xhat * second)
    out_ref[...] = value.T.astype(BF16)
    rows = []
    for c in range(2):
        both = jnp.zeros((8, 128), F32)
        for m in range(8):
            both += small_ref[c * 8 + m]
        rows.append(jnp.concatenate([both[6:7], both[7:8]], axis=1))
    gain_ref[...] = jnp.concatenate(rows + [jnp.zeros((6, 256), F32)], axis=0)


def on_device(tokens, gain, pre_act, w_in, act_cotangent):
    rows, share = tokens.shape
    here = [lax.axis_index(a).astype(jnp.int32).reshape(1) for a in ("y", "c")]
    place = jnp.concatenate(here)

    def step(array, way):
        moves = [((i + way) % 8, i, 0) for i in range(8)] + [((i - way) % 8, i, 1) for i in range(8)]
        return lax.ppermute(array, ("y", "c"), [(a * 2 + c, b * 2 + c) for a, b, c in moves])

    def tie(first, second, done, *later):
        (first_next, _), (second_next, _) = together((first, done)), together((second, done))
        return first_next, second_next, *together((first, second, done, *later))[2:]

    w0 = lax.all_gather(w_in, "zh", axis=0, tiled=True)
    w0, pre_act, act_cotangent, tokens = together((w0, pre_act, act_cotangent, tokens))
    first1, second1 = step(w0, 1), step(w0, -1)
    _, gelu_back = jax.vjp(gelu_exact, pre_act.astype(F32))
    d_own = gelu_back(act_cotangent.astype(F32))[0].astype(BF16)

    x, x_all = transposed(tokens)

    first, second, (d_own, x_all) = tie(first1, second1, (d_own, x_all))
    first2, second2 = step(first, 1), step(second, -1)
    d_other = partner(d_own, "c", 2, 1)
    x_all = lax.all_to_all(x_all.reshape(16, share // 2, rows), CHIPS, 0, 0)
    parts = products([(0, w0)], d_own, d_other, place, None, long=True)

    first, second, parts = tie(first2, second2, parts)
    first3, second3 = step(first, 1), step(second, -1)
    groups = [(1, first1), (7, second1), (2, first2), (6, second2)]
    parts = products(groups, d_own, d_other, place, parts)

    first, second, parts = tie(first3, second3, parts)
    first4 = step(first, 1)
    parts = products([(3, first3), (5, second)], d_own, d_other, place, parts)

    parts, x_all = together((parts, x_all))
    one = pl.pallas_call(
        stats_kernel,
        out_shape=jax.ShapeDtypeStruct((2, 8, rows), F32),
        compiler_params=PARAMS,
    )(x_all)

    two = partner(one, "c", 2, 1)

    first4, parts, one = together((first4, parts, one))
    parts = products([(4, first4)], d_own, d_other, place, parts)
    received = lax.all_to_all(parts.reshape(16, share // 2, rows), CHIPS, 0, 0)

    shares = lax.psum(lax.psum(gain_share(parts, x_all, one, two), "y"), "zh")

    vmem, smem = pl.BlockSpec(memory_space=pltpu.VMEM), pl.BlockSpec(memory_space=pltpu.SMEM)
    d_scaled, moments = pl.pallas_call(
        sum_kernel,
        in_specs=[smem] + [vmem] * 5,
        out_shape=[
            jax.ShapeDtypeStruct((share, rows), F32),
            jax.ShapeDtypeStruct((8, 128), F32),
        ],
        compiler_params=PARAMS,
    )(here[1], received, x, gain.astype(F32)[:, None], one, two)

    small = jnp.concatenate(
        [jnp.broadcast_to(moments[None, :6], (8, 6, 128)), shares.reshape(8, 2, 128)], axis=1
    )
    small = lax.all_to_all(jnp.concatenate([small, small], axis=0), CHIPS, 0, 0)
    token_gradient, gain_rows = pl.pallas_call(
        final_kernel,
        in_specs=[smem] + [vmem] * 5,
        out_shape=[
            jax.ShapeDtypeStruct((rows, share), BF16),
            jax.ShapeDtypeStruct((8, 256), F32),
        ],
        compiler_params=PARAMS,
    )(here[1], d_scaled, x, one, two, small)
    gain_gradient = jnp.swapaxes(gain_rows[:2, : share // 2].reshape(2, 4, SHARD), 0, 1).reshape(share)
    return (token_gradient, gain_gradient)


def solution(mesh):
    fine = Mesh(mesh.devices.reshape(SIZES), NAMES)
    placed = (P(DP, MP), P(MP), P(DP, MP), P(DP, MP), P(DP, MP))
    return jax.shard_map(
        on_device, mesh=fine, in_specs=placed, out_specs=(P(DP, MP), P(MP)), check_vma=False
    )
```

```python
import jax
import jax.numpy as jnp
from jax import lax
from jax.experimental import pallas as pl
from jax.experimental.pallas import tpu as pltpu
from jax.sharding import Mesh, PartitionSpec as P

NAMES = ("y", "zh", "c", "zl", "x")
SIZES = (8, 4, 2, 2, 4)
DP, MP, CHIPS = ("y", "zh", "c"), ("zl", "x"), ("c", "zl", "x")
F32, BF16 = jnp.float32, jnp.bfloat16
SHARD = 48
SHARE = 384
EXTRA = 16
PARAMS = pltpu.CompilerParams(vmem_limit_bytes=20 * 1024 * 1024)
WIDE = pltpu.CompilerParams(vmem_limit_bytes=52 * 1024 * 1024)
together = lax.optimization_barrier


def gelu_exact(value):
    return jax.nn.gelu(value, approximate=False)


def partner(array, axis, n, bit):
    return lax.ppermute(array, axis, [(i, i ^ bit) for i in range(n)])


def products(groups, d_own, d_other, place, parts, long=False):
    tokens, hidden = d_own.shape
    weights = [w for _, w in groups]
    rows, n = weights[0].shape[0], len(groups)

    def kernel(place_ref, own_ref, other_ref, *refs):
        w_refs, (out_ref, held, sem) = refs[:n], refs[-3:]
        copies = []
        w = jnp.concatenate([r[...] for r in w_refs], axis=0)
        for k, d_ref in enumerate((own_ref, other_ref)):
            half = lax.rem(place_ref[1] + k, 2)
            out = lax.dot_general(
                w, d_ref[...], (((1,), (1,)), ((), ())), preferred_element_type=F32
            ).astype(BF16)
            for g, (offset, _) in enumerate(groups):
                held[k, g] = out[g * rows : (g + 1) * rows]
                block = lax.rem(place_ref[0] + offset + place_ref[1] * ((8 - 2 * offset) % 8), 8)
                to = out_ref.at[half, block]
                copies.append(pltpu.make_async_copy(held.at[k, g], to, sem.at[k, g]))
                copies[-1].start()
        for copy in copies:
            copy.wait()

    whole = pl.BlockSpec(memory_space=pltpu.VMEM)
    return pl.pallas_call(
        kernel,
        in_specs=[pl.BlockSpec(memory_space=pltpu.SMEM)]
        + [whole] * (2 + n)
        + [pl.BlockSpec(memory_space=pl.ANY)] * (parts is not None),
        out_specs=pl.BlockSpec(memory_space=pl.ANY),
        out_shape=jax.ShapeDtypeStruct((2, 8, rows, tokens), BF16),
        scratch_shapes=[
            pltpu.VMEM((2, n, rows, tokens), BF16),
            pltpu.SemaphoreType.DMA((2, n)),
        ],
        input_output_aliases={} if parts is None else {3 + n: 0},
        compiler_params=WIDE,
        cost_estimate=pl.CostEstimate(
            flops=1 << 38 if long else rows * hidden * tokens, bytes_accessed=1 << 18, transcendentals=0
        ),
    )(place, d_own, d_other, *weights, *([] if parts is None else [parts]))


def tokens_kernel(tokens_ref, x_ref, send_ref, held, sem):
    x = tokens_ref[...].astype(F32).T
    x_ref[...] = x.astype(BF16)
    mean = jnp.sum(x, axis=0, keepdims=True) * (1.0 / SHARE)
    parts = []
    for rest in (mean, jnp.sum((x - mean) ** 2, axis=0, keepdims=True)):
        for _ in range(3):
            parts.append(rest.astype(BF16).astype(F32))
            rest = rest - parts[-1]
    parts = jnp.concatenate(parts + [jnp.zeros((EXTRA - 6, x.shape[1]), F32)], axis=0).astype(BF16)
    copies = []
    for c in range(2):
        for z in range(4):
            held[c, pl.ds(z * SHARD, SHARD)] = x[(z * 2 + c) * SHARD : (z * 2 + c + 1) * SHARD].astype(BF16)
        held[c, pl.ds(4 * SHARD, EXTRA)] = parts
        for m in range(8):
            copies.append(pltpu.make_async_copy(held.at[c], send_ref.at[c, m], sem.at[c, m]))
            copies[-1].start()
    for copy in copies:
        copy.wait()


def transposed(tokens):
    rows, share = tokens.shape
    return pl.pallas_call(
        tokens_kernel,
        out_specs=[pl.BlockSpec(memory_space=pltpu.VMEM), pl.BlockSpec(memory_space=pl.ANY)],
        out_shape=[
            jax.ShapeDtypeStruct((share, rows), BF16),
            jax.ShapeDtypeStruct((2, 8, share // 2 + EXTRA, rows), BF16),
        ],
        scratch_shapes=[
            pltpu.VMEM((2, share // 2 + EXTRA, rows), BF16),
            pltpu.SemaphoreType.DMA((2, 8)),
        ],
        compiler_params=PARAMS,
    )(tokens)


def gain_kernel(parts_ref, x_ref, extra_ref, out_ref, stat_ref):
    @pl.when(pl.program_id(0) == 0)
    def _():
        for t in range(2):
            means, squares = [], []
            for m in range(8):
                rows = extra_ref[t, m].astype(F32)
                means.append(rows[0:1] + rows[1:2] + rows[2:3])
                squares.append(rows[3:4] + rows[4:5] + rows[5:6])
            mean = sum(means) * 0.125
            between = sum((m - mean) ** 2 for m in means)
            variance = (sum(squares) + SHARE * between) * (1.0 / (8 * SHARE))
            rstd = 1.0 / jnp.sqrt(variance + 1e-06)
            stat_ref[t] = jnp.concatenate([mean, rstd] * 4, axis=0)

    per_step, features = x_ref.shape[1], parts_ref.shape[2]
    for k in range(per_step):
        total = jnp.zeros((features, 128), F32)
        for t in range(2):
            xhat = (x_ref[t, k, :features].astype(F32) - stat_ref[t, 0:1]) * stat_ref[t, 1:2]
            value = parts_ref[t, k].astype(F32) * xhat
            total += value[:, :128] + value[:, 128:256] + value[:, 256:]
        total = jnp.concatenate([total, jnp.zeros((256 - features, 128), F32)], axis=0)
        row = jnp.sum(total.T, axis=0, keepdims=True)
        out_ref[pl.ds(pl.program_id(0) * per_step + k, 1), :] = row


def gain_share(parts, x_all):
    _, _, rows, tokens = parts.shape
    x_all = x_all.reshape(2, 8, rows + EXTRA, tokens)
    return pl.pallas_call(
        gain_kernel,
        grid=(4,),
        in_specs=[
            pl.BlockSpec((2, 2, rows, tokens), lambda m: (0, m, 0, 0)),
            pl.BlockSpec((2, 2, rows + EXTRA, tokens), lambda m: (0, m, 0, 0)),
            pl.BlockSpec((2, 8, EXTRA, tokens), lambda m: (0, 0, rows // EXTRA, 0)),
        ],
        out_specs=[
            pl.BlockSpec((8, 256), lambda m: (0, 0)),
            pl.BlockSpec((2, 8, tokens), lambda m: (0, 0, 0)),
        ],
        out_shape=[
            jax.ShapeDtypeStruct((8, 256), F32),
            jax.ShapeDtypeStruct((2, 8, tokens), F32),
        ],
        compiler_params=WIDE,
    )(parts, x_all, x_all)


def sum_kernel(core_ref, parts_ref, x_ref, gain_ref, stat_ref, d_ref, moments_ref):
    stat = stat_ref[core_ref[0]]
    mean, rstd = stat[0:1], stat[1:2]
    first, second = 0.0, 0.0
    for z in range(4):
        for c in range(2):
            total = parts_ref[c * 8, pl.ds(z * SHARD, SHARD), :].astype(F32)
            for m in range(1, 8):
                total += parts_ref[c * 8 + m, pl.ds(z * SHARD, SHARD), :].astype(F32)
            at = pl.ds((z * 2 + c) * SHARD, SHARD)
            g = total * gain_ref[at, :]
            d_ref[at, :] = g
            xhat = (x_ref[at, :].astype(F32) - mean) * rstd
            first += jnp.sum(g, axis=0, keepdims=True)
            second += jnp.sum(g * xhat, axis=0, keepdims=True)
    rows = [m[:, i * 128 : (i + 1) * 128] for m in (first, second) for i in range(3)]
    moments_ref[...] = jnp.concatenate(rows + [jnp.zeros((2, 128), F32)], axis=0)


def final_kernel(here_ref, d_ref, x_ref, stat_ref, small_ref, out_ref, gain_ref):
    core = here_ref[0]
    mean, rstd = stat_ref[core][0:1], stat_ref[core][1:2]
    total = small_ref[core * 8]
    for m in range(1, 8):
        total += small_ref[core * 8 + m]
    total = total * (1.0 / (8 * SHARE))
    first, second = (jnp.concatenate([total[k + i : k + i + 1] for i in range(3)], axis=1) for k in (0, 3))
    xhat = (x_ref[...].astype(F32) - mean) * rstd
    value = rstd * (d_ref[...] - first - xhat * second)
    out_ref[...] = value.T.astype(BF16)
    rows = []
    for c in range(2):
        both = jnp.zeros((8, 128), F32)
        for m in range(8):
            both += small_ref[c * 8 + m]
        rows.append(jnp.concatenate([both[6:7], both[7:8]], axis=1))
    gain_ref[...] = jnp.concatenate(rows + [jnp.zeros((6, 256), F32)], axis=0)


def on_device(tokens, gain, pre_act, w_in, act_cotangent):
    rows, share = tokens.shape
    here = [lax.axis_index(a).astype(jnp.int32).reshape(1) for a in ("y", "c")]
    place = jnp.concatenate(here)

    def step(array, way):
        moves = [((i + way) % 8, i, 0) for i in range(8)] + [((i - way) % 8, i, 1) for i in range(8)]
        return lax.ppermute(array, ("y", "c"), [(a * 2 + c, b * 2 + c) for a, b, c in moves])

    def tie(first, second, done, *later):
        (first_next, _), (second_next, _) = together((first, done)), together((second, done))
        return first_next, second_next, *together((first, second, done, *later))[2:]

    w0 = lax.all_gather(w_in, "zh", axis=0, tiled=True)
    w0, pre_act, act_cotangent, tokens = together((w0, pre_act, act_cotangent, tokens))
    first1, second1 = step(w0, 1), step(w0, -1)
    _, gelu_back = jax.vjp(gelu_exact, pre_act.astype(F32))
    d_own = gelu_back(act_cotangent.astype(F32))[0].astype(BF16)

    x, x_all = transposed(tokens)

    first, second, (d_own, x_all) = tie(first1, second1, (d_own, x_all))
    first2, second2 = step(first, 1), step(second, -1)
    d_other = partner(d_own, "c", 2, 1)
    x_all = lax.all_to_all(x_all.reshape(16, -1, rows), CHIPS, 0, 0)
    parts = products([(0, w0)], d_own, d_other, place, None, long=True)

    first, second, parts = tie(first2, second2, parts)
    first3, second3 = step(first, 1), step(second, -1)
    groups = [(1, first1), (7, second1), (2, first2), (6, second2)]
    parts = products(groups, d_own, d_other, place, parts)

    first, second, parts = tie(first3, second3, parts)
    first4 = step(first, 1)
    parts = products([(3, first3), (5, second)], d_own, d_other, place, parts)

    first4, parts, x_all = together((first4, parts, x_all))
    parts = products([(4, first4)], d_own, d_other, place, parts)
    received = lax.all_to_all(parts.reshape(16, share // 2, rows), CHIPS, 0, 0)

    shares, stat = gain_share(parts, x_all)
    shares = lax.psum(lax.psum(shares, "y"), "zh")

    vmem, smem = pl.BlockSpec(memory_space=pltpu.VMEM), pl.BlockSpec(memory_space=pltpu.SMEM)
    d_scaled, moments = pl.pallas_call(
        sum_kernel,
        in_specs=[smem] + [vmem] * 4,
        out_shape=[
            jax.ShapeDtypeStruct((share, rows), F32),
            jax.ShapeDtypeStruct((8, 128), F32),
        ],
        compiler_params=PARAMS,
    )(here[1], received, x, gain.astype(F32)[:, None], stat)

    small = jnp.concatenate(
        [jnp.broadcast_to(moments[None, :6], (8, 6, 128)), shares.reshape(8, 2, 128)], axis=1
    )
    small = lax.all_to_all(jnp.concatenate([small, small], axis=0), CHIPS, 0, 0)
    token_gradient, gain_rows = pl.pallas_call(
        final_kernel,
        in_specs=[smem] + [vmem] * 4,
        out_shape=[
            jax.ShapeDtypeStruct((rows, share), BF16),
            jax.ShapeDtypeStruct((8, 256), F32),
        ],
        compiler_params=PARAMS,
    )(here[1], d_scaled, x, stat, small)
    gain_gradient = jnp.swapaxes(gain_rows[:2, : share // 2].reshape(2, 4, SHARD), 0, 1).reshape(share)
    return (token_gradient, gain_gradient)


def solution(mesh):
    fine = Mesh(mesh.devices.reshape(SIZES), NAMES)
    placed = (P(DP, MP), P(MP), P(DP, MP), P(DP, MP), P(DP, MP))
    return jax.shard_map(
        on_device, mesh=fine, in_specs=placed, out_specs=(P(DP, MP), P(MP)), check_vma=False
    )
```

```python
import jax
import jax.numpy as jnp
from jax import lax
from jax.experimental import pallas as pl
from jax.experimental.pallas import tpu as pltpu
from jax.sharding import Mesh, PartitionSpec as P

NAMES = ("y", "zh", "c", "zl", "x")
SIZES = (8, 4, 2, 2, 4)
DP, MP, CHIPS = ("y", "zh", "c"), ("zl", "x"), ("c", "zl", "x")
F32, BF16 = jnp.float32, jnp.bfloat16
SHARD = 48
SHARE = 384
EXTRA = 16
PARAMS = pltpu.CompilerParams(vmem_limit_bytes=20 * 1024 * 1024)
WIDE = pltpu.CompilerParams(vmem_limit_bytes=52 * 1024 * 1024)
together = lax.optimization_barrier


def gelu_exact(value):
    return jax.nn.gelu(value, approximate=False)


def partner(array, axis, n, bit):
    return lax.ppermute(array, axis, [(i, i ^ bit) for i in range(n)])


def products(groups, halves, place, parts, long=False):
    tokens, hidden = halves[0][1].shape
    weights, operands = [w for _, w in groups], [d for _, d in halves]
    rows, n, both = weights[0].shape[0], len(groups), len(halves)

    def kernel(place_ref, *refs):
        w_refs, d_refs = refs[:n], refs[n : n + both]
        out_ref, w_held, d_held, held, w_sem, d_sem, sem = refs[-7:]
        loads = [
            pltpu.make_async_copy(w, w_held.at[pl.ds(g * rows, rows)], w_sem.at[g])
            for g, w in enumerate(w_refs)
        ]
        d_loads = [pltpu.make_async_copy(d, d_held.at[h], d_sem.at[h]) for h, d in enumerate(d_refs)]
        for load in loads + d_loads:
            load.start()
        for load in loads:
            load.wait()
        copies = []
        for h, (k, _) in enumerate(halves):
            d_loads[h].wait()
            half = lax.rem(place_ref[1] + k, 2)
            out = lax.dot_general(
                w_held[...], d_held[h], (((1,), (1,)), ((), ())), preferred_element_type=F32
            ).astype(BF16)
            for g, (offset, _) in enumerate(groups):
                held[h, g] = out[g * rows : (g + 1) * rows]
                block = lax.rem(place_ref[0] + offset + place_ref[1] * ((8 - 2 * offset) % 8), 8)
                to = out_ref.at[half, block]
                copies.append(pltpu.make_async_copy(held.at[h, g], to, sem.at[h, g]))
                copies[-1].start()
        for copy in copies:
            copy.wait()

    anywhere = pl.BlockSpec(memory_space=pl.ANY)
    return pl.pallas_call(
        kernel,
        in_specs=[pl.BlockSpec(memory_space=pltpu.SMEM)] + [anywhere] * (n + both + (parts is not None)),
        out_specs=anywhere,
        out_shape=jax.ShapeDtypeStruct((2, 8, rows, tokens), BF16),
        scratch_shapes=[
            pltpu.VMEM((n * rows, hidden), BF16),
            pltpu.VMEM((both, tokens, hidden), BF16),
            pltpu.VMEM((both, n, rows, tokens), BF16),
            pltpu.SemaphoreType.DMA((n,)),
            pltpu.SemaphoreType.DMA((both,)),
            pltpu.SemaphoreType.DMA((both, n)),
        ],
        input_output_aliases={} if parts is None else {1 + n + both: 0},
        compiler_params=WIDE,
        cost_estimate=pl.CostEstimate(
            flops=1 << 38 if long else rows * hidden * tokens, bytes_accessed=1 << 18, transcendentals=0
        ),
    )(place, *weights, *operands, *([] if parts is None else [parts]))


def tokens_kernel(tokens_ref, x_ref, send_ref, held, sem):
    x = tokens_ref[...].astype(F32).T
    x_ref[...] = x.astype(BF16)
    mean = jnp.sum(x, axis=0, keepdims=True) * (1.0 / SHARE)
    parts = []
    for rest in (mean, jnp.sum((x - mean) ** 2, axis=0, keepdims=True)):
        for _ in range(3):
            parts.append(rest.astype(BF16).astype(F32))
            rest = rest - parts[-1]
    parts = jnp.concatenate(parts + [jnp.zeros((EXTRA - 6, x.shape[1]), F32)], axis=0).astype(BF16)
    copies = []
    for c in range(2):
        for z in range(4):
            held[c, pl.ds(z * SHARD, SHARD)] = x[(z * 2 + c) * SHARD : (z * 2 + c + 1) * SHARD].astype(BF16)
        held[c, pl.ds(4 * SHARD, EXTRA)] = parts
        for m in range(8):
            copies.append(pltpu.make_async_copy(held.at[c], send_ref.at[c, m], sem.at[c, m]))
            copies[-1].start()
    for copy in copies:
        copy.wait()


def transposed(tokens):
    rows, share = tokens.shape
    return pl.pallas_call(
        tokens_kernel,
        out_specs=[pl.BlockSpec(memory_space=pltpu.VMEM), pl.BlockSpec(memory_space=pl.ANY)],
        out_shape=[
            jax.ShapeDtypeStruct((share, rows), BF16),
            jax.ShapeDtypeStruct((2, 8, share // 2 + EXTRA, rows), BF16),
        ],
        scratch_shapes=[
            pltpu.VMEM((2, share // 2 + EXTRA, rows), BF16),
            pltpu.SemaphoreType.DMA((2, 8)),
        ],
        compiler_params=WIDE,
    )(tokens)


def gain_kernel(parts_ref, x_ref, extra_ref, out_ref, stat_ref):
    @pl.when(pl.program_id(0) == 0)
    def _():
        for t in range(2):
            means, squares = [], []
            for m in range(8):
                rows = extra_ref[t, m].astype(F32)
                means.append(rows[0:1] + rows[1:2] + rows[2:3])
                squares.append(rows[3:4] + rows[4:5] + rows[5:6])
            mean = sum(means) * 0.125
            between = sum((m - mean) ** 2 for m in means)
            variance = (sum(squares) + SHARE * between) * (1.0 / (8 * SHARE))
            rstd = 1.0 / jnp.sqrt(variance + 1e-06)
            stat_ref[t] = jnp.concatenate([mean, rstd] * 4, axis=0)

    per_step, features = x_ref.shape[1], parts_ref.shape[2]
    for k in range(per_step):
        total = jnp.zeros((features, 128), F32)
        for t in range(2):
            xhat = (x_ref[t, k, :features].astype(F32) - stat_ref[t, 0:1]) * stat_ref[t, 1:2]
            value = parts_ref[t, k].astype(F32) * xhat
            total += value[:, :128] + value[:, 128:256] + value[:, 256:]
        total = jnp.concatenate([total, jnp.zeros((256 - features, 128), F32)], axis=0)
        row = jnp.sum(total.T, axis=0, keepdims=True)
        out_ref[pl.ds(pl.program_id(0) * per_step + k, 1), :] = row


def gain_share(parts, x_all):
    _, _, rows, tokens = parts.shape
    x_all = x_all.reshape(2, 8, rows + EXTRA, tokens)
    return pl.pallas_call(
        gain_kernel,
        grid=(4,),
        in_specs=[
            pl.BlockSpec((2, 2, rows, tokens), lambda m: (0, m, 0, 0)),
            pl.BlockSpec((2, 2, rows + EXTRA, tokens), lambda m: (0, m, 0, 0)),
            pl.BlockSpec((2, 8, EXTRA, tokens), lambda m: (0, 0, rows // EXTRA, 0)),
        ],
        out_specs=[
            pl.BlockSpec((8, 256), lambda m: (0, 0)),
            pl.BlockSpec((2, 8, tokens), lambda m: (0, 0, 0)),
        ],
        out_shape=[
            jax.ShapeDtypeStruct((8, 256), F32),
            jax.ShapeDtypeStruct((2, 8, tokens), F32),
        ],
        compiler_params=WIDE,
    )(parts, x_all, x_all)


def sum_kernel(core_ref, parts_ref, x_ref, gain_ref, stat_ref, d_ref, moments_ref):
    stat = stat_ref[core_ref[0]]
    mean, rstd = stat[0:1], stat[1:2]
    first, second = 0.0, 0.0
    for z in range(4):
        for c in range(2):
            total = parts_ref[c * 8, pl.ds(z * SHARD, SHARD), :].astype(F32)
            for m in range(1, 8):
                total += parts_ref[c * 8 + m, pl.ds(z * SHARD, SHARD), :].astype(F32)
            at = pl.ds((z * 2 + c) * SHARD, SHARD)
            g = total * gain_ref[at, :]
            d_ref[at, :] = g
            xhat = (x_ref[at, :].astype(F32) - mean) * rstd
            first += jnp.sum(g, axis=0, keepdims=True)
            second += jnp.sum(g * xhat, axis=0, keepdims=True)
    rows = [m[:, i * 128 : (i + 1) * 128] for m in (first, second) for i in range(3)]
    moments_ref[...] = jnp.concatenate(rows + [jnp.zeros((2, 128), F32)], axis=0)


def final_kernel(here_ref, d_ref, x_ref, stat_ref, small_ref, out_ref, gain_ref):
    core = here_ref[0]
    mean, rstd = stat_ref[core][0:1], stat_ref[core][1:2]
    total = small_ref[core * 8]
    for m in range(1, 8):
        total += small_ref[core * 8 + m]
    total = total * (1.0 / (8 * SHARE))
    first, second = (jnp.concatenate([total[k + i : k + i + 1] for i in range(3)], axis=1) for k in (0, 3))
    xhat = (x_ref[...].astype(F32) - mean) * rstd
    value = rstd * (d_ref[...] - first - xhat * second)
    out_ref[...] = value.T.astype(BF16)
    rows = []
    for c in range(2):
        both = jnp.zeros((8, 128), F32)
        for m in range(8):
            both += small_ref[c * 8 + m]
        rows.append(jnp.concatenate([both[6:7], both[7:8]], axis=1))
    gain_ref[...] = jnp.concatenate(rows + [jnp.zeros((6, 256), F32)], axis=0)


def on_device(tokens, gain, pre_act, w_in, act_cotangent):
    rows, share = tokens.shape
    here = [lax.axis_index(a).astype(jnp.int32).reshape(1) for a in ("y", "c")]
    place = jnp.concatenate(here)

    def step(array, way):
        moves = [((i + way) % 8, i, 0) for i in range(8)] + [((i - way) % 8, i, 1) for i in range(8)]
        return lax.ppermute(array, ("y", "c"), [(a * 2 + c, b * 2 + c) for a, b, c in moves])

    def tie(first, second, done, *later):
        (first_next, _), (second_next, _) = together((first, done)), together((second, done))
        return first_next, second_next, *together((first, second, done, *later))[2:]

    w0 = lax.all_gather(w_in, "zh", axis=0, tiled=True)
    w0, pre_act, act_cotangent, tokens = together((w0, pre_act, act_cotangent, tokens))
    first1, second1 = step(w0, 1), step(w0, -1)
    _, gelu_back = jax.vjp(gelu_exact, pre_act.astype(F32))
    d_own = gelu_back(act_cotangent.astype(F32))[0].astype(BF16)

    x, x_all = transposed(tokens)

    first, second, (d_own, x_all) = tie(first1, second1, (d_own, x_all))
    first2, second2 = step(first, 1), step(second, -1)
    d_other = partner(d_own, "c", 2, 1)
    x_all = lax.all_to_all(x_all.reshape(16, -1, rows), CHIPS, 0, 0)
    parts = products([(0, w0)], [(0, d_own)], place, None, long=True)

    first, second, parts = tie(first2, second2, parts)
    first3, second3 = step(first, 1), step(second, -1)
    groups = [(1, first1), (7, second1), (2, first2), (6, second2)]
    halves = [(0, d_own), (1, d_other)]
    parts = products([(0, w0)], [(1, d_other)], place, parts)
    parts = products(groups, halves, place, parts)

    first, second, parts = tie(first3, second3, parts)
    first4 = step(first, 1)
    parts = products([(3, first3), (5, second)], halves, place, parts)

    first4, parts, x_all = together((first4, parts, x_all))
    parts = products([(4, first4)], halves, place, parts)
    received = lax.all_to_all(parts.reshape(16, share // 2, rows), CHIPS, 0, 0)

    shares, stat = gain_share(parts, x_all)
    shares = lax.psum(lax.psum(shares, "y"), "zh")

    vmem, smem = pl.BlockSpec(memory_space=pltpu.VMEM), pl.BlockSpec(memory_space=pltpu.SMEM)
    d_scaled, moments = pl.pallas_call(
        sum_kernel,
        in_specs=[smem] + [vmem] * 4,
        out_shape=[
            jax.ShapeDtypeStruct((share, rows), F32),
            jax.ShapeDtypeStruct((8, 128), F32),
        ],
        compiler_params=PARAMS,
    )(here[1], received, x, gain.astype(F32)[:, None], stat)

    small = jnp.concatenate(
        [jnp.broadcast_to(moments[None, :6], (8, 6, 128)), shares.reshape(8, 2, 128)], axis=1
    )
    small = lax.all_to_all(jnp.concatenate([small, small], axis=0), CHIPS, 0, 0)
    token_gradient, gain_rows = pl.pallas_call(
        final_kernel,
        in_specs=[smem] + [vmem] * 4,
        out_shape=[
            jax.ShapeDtypeStruct((rows, share), BF16),
            jax.ShapeDtypeStruct((8, 256), F32),
        ],
        compiler_params=PARAMS,
    )(here[1], d_scaled, x, stat, small)
    gain_gradient = jnp.swapaxes(gain_rows[:2, : share // 2].reshape(2, 4, SHARD), 0, 1).reshape(share)
    return (token_gradient, gain_gradient)


def solution(mesh):
    fine = Mesh(mesh.devices.reshape(SIZES), NAMES)
    placed = (P(DP, MP), P(MP), P(DP, MP), P(DP, MP), P(DP, MP))
    return jax.shard_map(
        on_device, mesh=fine, in_specs=placed, out_specs=(P(DP, MP), P(MP)), check_vma=False
    )
```

```python
import jax
import jax.numpy as jnp
from jax import lax
from jax.experimental import pallas as pl
from jax.experimental.pallas import tpu as pltpu
from jax.sharding import Mesh, PartitionSpec as P

NAMES = ("y", "zh", "c", "zl", "x")
SIZES = (8, 4, 2, 2, 4)
DP, MP, CHIPS = ("y", "zh", "c"), ("zl", "x"), ("c", "zl", "x")
F32, BF16 = jnp.float32, jnp.bfloat16
SHARD = 48
SHARE = 384
EXTRA = 16
PARAMS = pltpu.CompilerParams(vmem_limit_bytes=20 * 1024 * 1024)
WIDE = pltpu.CompilerParams(vmem_limit_bytes=52 * 1024 * 1024)
together = lax.optimization_barrier


def gelu_exact(value):
    return jax.nn.gelu(value, approximate=False)


def partner(array, axis, n, bit):
    return lax.ppermute(array, axis, [(i, i ^ bit) for i in range(n)])


def products(groups, halves, place, parts, long=False):
    tokens, hidden = halves[0][1].shape
    weights, operands = [w for _, w in groups], [d for _, d, _ in halves]
    rows, n, both = weights[0].shape[0], len(groups), len(halves)

    def kernel(place_ref, *refs):
        w_refs, d_refs = refs[:n], refs[n : n + both]
        out_ref, held, sem = refs[-3:]
        copies = []
        w = jnp.concatenate([r[...] for r in w_refs], axis=0)
        for h, (k, _, count) in enumerate(halves):
            half = lax.rem(place_ref[1] + k, 2)
            out = lax.dot_general(
                w[: count * rows], d_refs[h][...], (((1,), (1,)), ((), ())), preferred_element_type=F32
            ).astype(BF16)
            for g, (offset, _) in enumerate(groups[:count]):
                held[h, g] = out[g * rows : (g + 1) * rows]
                block = lax.rem(place_ref[0] + offset + place_ref[1] * ((8 - 2 * offset) % 8), 8)
                to = out_ref.at[half, block]
                copies.append(pltpu.make_async_copy(held.at[h, g], to, sem.at[h, g]))
                copies[-1].start()
        for copy in copies:
            copy.wait()

    anywhere, whole = pl.BlockSpec(memory_space=pl.ANY), pl.BlockSpec(memory_space=pltpu.VMEM)
    return pl.pallas_call(
        kernel,
        in_specs=[pl.BlockSpec(memory_space=pltpu.SMEM)] + [whole] * (n + both) + [anywhere] * (parts is not None),
        out_specs=anywhere,
        out_shape=jax.ShapeDtypeStruct((2, 8, rows, tokens), BF16),
        scratch_shapes=[
            pltpu.VMEM((both, n, rows, tokens), BF16),
            pltpu.SemaphoreType.DMA((both, n)),
        ],
        input_output_aliases={} if parts is None else {1 + n + both: 0},
        compiler_params=WIDE,
        cost_estimate=pl.CostEstimate(
            flops=1 << 38 if long else rows * hidden * tokens, bytes_accessed=1 << 18, transcendentals=0
        ),
    )(place, *weights, *operands, *([] if parts is None else [parts]))


def tokens_kernel(tokens_ref, x_ref, send_ref, held, sem):
    x = tokens_ref[...].astype(F32).T
    x_ref[...] = x.astype(BF16)
    mean = jnp.sum(x, axis=0, keepdims=True) * (1.0 / SHARE)
    parts = []
    for rest in (mean, jnp.sum((x - mean) ** 2, axis=0, keepdims=True)):
        for _ in range(3):
            parts.append(rest.astype(BF16).astype(F32))
            rest = rest - parts[-1]
    parts = jnp.concatenate(parts + [jnp.zeros((EXTRA - 6, x.shape[1]), F32)], axis=0).astype(BF16)
    copies = []
    for c in range(2):
        for z in range(4):
            held[c, pl.ds(z * SHARD, SHARD)] = x[(z * 2 + c) * SHARD : (z * 2 + c + 1) * SHARD].astype(BF16)
        held[c, pl.ds(4 * SHARD, EXTRA)] = parts
        for m in range(8):
            copies.append(pltpu.make_async_copy(held.at[c], send_ref.at[c, m], sem.at[c, m]))
            copies[-1].start()
    for copy in copies:
        copy.wait()


def transposed(tokens):
    rows, share = tokens.shape
    return pl.pallas_call(
        tokens_kernel,
        out_specs=[pl.BlockSpec(memory_space=pltpu.VMEM), pl.BlockSpec(memory_space=pl.ANY)],
        out_shape=[
            jax.ShapeDtypeStruct((share, rows), BF16),
            jax.ShapeDtypeStruct((2, 8, share // 2 + EXTRA, rows), BF16),
        ],
        scratch_shapes=[
            pltpu.VMEM((2, share // 2 + EXTRA, rows), BF16),
            pltpu.SemaphoreType.DMA((2, 8)),
        ],
        compiler_params=WIDE,
    )(tokens)


def gain_kernel(parts_ref, x_ref, extra_ref, out_ref, stat_ref):
    @pl.when(pl.program_id(0) == 0)
    def _():
        for t in range(2):
            means, squares = [], []
            for m in range(8):
                rows = extra_ref[t, m].astype(F32)
                means.append(rows[0:1] + rows[1:2] + rows[2:3])
                squares.append(rows[3:4] + rows[4:5] + rows[5:6])
            mean = sum(means) * 0.125
            between = sum((m - mean) ** 2 for m in means)
            variance = (sum(squares) + SHARE * between) * (1.0 / (8 * SHARE))
            rstd = 1.0 / jnp.sqrt(variance + 1e-06)
            stat_ref[t] = jnp.concatenate([mean, rstd] * 4, axis=0)

    per_step, features = x_ref.shape[1], parts_ref.shape[2]
    for k in range(per_step):
        total = jnp.zeros((features, 128), F32)
        for t in range(2):
            xhat = (x_ref[t, k, :features].astype(F32) - stat_ref[t, 0:1]) * stat_ref[t, 1:2]
            value = parts_ref[t, k].astype(F32) * xhat
            total += value[:, :128] + value[:, 128:256] + value[:, 256:]
        total = jnp.concatenate([total, jnp.zeros((256 - features, 128), F32)], axis=0)
        row = jnp.sum(total.T, axis=0, keepdims=True)
        out_ref[pl.ds(pl.program_id(0) * per_step + k, 1), :] = row


def gain_share(parts, x_all):
    _, _, rows, tokens = parts.shape
    x_all = x_all.reshape(2, 8, rows + EXTRA, tokens)
    return pl.pallas_call(
        gain_kernel,
        grid=(4,),
        in_specs=[
            pl.BlockSpec((2, 2, rows, tokens), lambda m: (0, m, 0, 0)),
            pl.BlockSpec((2, 2, rows + EXTRA, tokens), lambda m: (0, m, 0, 0)),
            pl.BlockSpec((2, 8, EXTRA, tokens), lambda m: (0, 0, rows // EXTRA, 0)),
        ],
        out_specs=[
            pl.BlockSpec((8, 256), lambda m: (0, 0)),
            pl.BlockSpec((2, 8, tokens), lambda m: (0, 0, 0)),
        ],
        out_shape=[
            jax.ShapeDtypeStruct((8, 256), F32),
            jax.ShapeDtypeStruct((2, 8, tokens), F32),
        ],
        compiler_params=WIDE,
    )(parts, x_all, x_all)


def sum_kernel(core_ref, parts_ref, x_ref, gain_ref, stat_ref, d_ref, moments_ref):
    stat = stat_ref[core_ref[0]]
    mean, rstd = stat[0:1], stat[1:2]
    first, second = 0.0, 0.0
    for z in range(4):
        for c in range(2):
            total = parts_ref[c * 8, pl.ds(z * SHARD, SHARD), :].astype(F32)
            for m in range(1, 8):
                total += parts_ref[c * 8 + m, pl.ds(z * SHARD, SHARD), :].astype(F32)
            at = pl.ds((z * 2 + c) * SHARD, SHARD)
            g = total * gain_ref[at, :]
            d_ref[at, :] = g
            xhat = (x_ref[at, :].astype(F32) - mean) * rstd
            first += jnp.sum(g, axis=0, keepdims=True)
            second += jnp.sum(g * xhat, axis=0, keepdims=True)
    rows = [m[:, i * 128 : (i + 1) * 128] for m in (first, second) for i in range(3)]
    moments_ref[...] = jnp.concatenate(rows + [jnp.zeros((2, 128), F32)], axis=0)


def final_kernel(here_ref, d_ref, x_ref, stat_ref, small_ref, out_ref, gain_ref):
    core = here_ref[0]
    mean, rstd = stat_ref[core][0:1], stat_ref[core][1:2]
    total = small_ref[core * 8]
    for m in range(1, 8):
        total += small_ref[core * 8 + m]
    total = total * (1.0 / (8 * SHARE))
    first, second = (jnp.concatenate([total[k + i : k + i + 1] for i in range(3)], axis=1) for k in (0, 3))
    xhat = (x_ref[...].astype(F32) - mean) * rstd
    value = rstd * (d_ref[...] - first - xhat * second)
    out_ref[...] = value.T.astype(BF16)
    rows = []
    for c in range(2):
        both = jnp.zeros((8, 128), F32)
        for m in range(8):
            both += small_ref[c * 8 + m]
        rows.append(jnp.concatenate([both[6:7], both[7:8]], axis=1))
    gain_ref[...] = jnp.concatenate(rows + [jnp.zeros((6, 256), F32)], axis=0)


def on_device(tokens, gain, pre_act, w_in, act_cotangent):
    rows, share = tokens.shape
    here = [lax.axis_index(a).astype(jnp.int32).reshape(1) for a in ("y", "c")]
    place = jnp.concatenate(here)

    def step(array, way):
        moves = [((i + way) % 8, i, 0) for i in range(8)] + [((i - way) % 8, i, 1) for i in range(8)]
        return lax.ppermute(array, ("y", "c"), [(a * 2 + c, b * 2 + c) for a, b, c in moves])

    def tie(first, second, done, *later):
        (first_next, _), (second_next, _) = together((first, done)), together((second, done))
        return first_next, second_next, *together((first, second, done, *later))[2:]

    w0 = lax.all_gather(w_in, "zh", axis=0, tiled=True)
    w0, pre_act, act_cotangent, tokens = together((w0, pre_act, act_cotangent, tokens))
    first1, second1 = step(w0, 1), step(w0, -1)
    _, gelu_back = jax.vjp(gelu_exact, pre_act.astype(F32))
    d_own = gelu_back(act_cotangent.astype(F32))[0].astype(BF16)

    x, x_all = transposed(tokens)

    first, second, (d_own, x_all) = tie(first1, second1, (d_own, x_all))
    first2, second2 = step(first, 1), step(second, -1)
    d_other = partner(d_own, "c", 2, 1)
    x_all = lax.all_to_all(x_all.reshape(16, -1, rows), CHIPS, 0, 0)
    parts = products([(0, w0)], [(0, d_own, 1)], place, None, long=True)

    first, second, parts = tie(first2, second2, parts)
    first3, second3 = step(first, 1), step(second, -1)
    groups = [(1, first1), (7, second1), (2, first2), (6, second2), (0, w0)]
    parts = products(groups, [(0, d_own, 4), (1, d_other, 5)], place, parts)

    first, second, parts = tie(first3, second3, parts)
    first4 = step(first, 1)
    parts = products([(3, first3), (5, second)], [(0, d_own, 2), (1, d_other, 2)], place, parts)

    first4, parts, x_all = together((first4, parts, x_all))
    parts = products([(4, first4)], [(0, d_own, 1), (1, d_other, 1)], place, parts)
    received = lax.all_to_all(parts.reshape(16, share // 2, rows), CHIPS, 0, 0)

    shares, stat = gain_share(parts, x_all)
    shares = lax.psum(lax.psum(shares, "y"), "zh")

    vmem, smem = pl.BlockSpec(memory_space=pltpu.VMEM), pl.BlockSpec(memory_space=pltpu.SMEM)
    d_scaled, moments = pl.pallas_call(
        sum_kernel,
        in_specs=[smem] + [vmem] * 4,
        out_shape=[
            jax.ShapeDtypeStruct((share, rows), F32),
            jax.ShapeDtypeStruct((8, 128), F32),
        ],
        compiler_params=PARAMS,
    )(here[1], received, x, gain.astype(F32)[:, None], stat)

    small = jnp.concatenate(
        [jnp.broadcast_to(moments[None, :6], (8, 6, 128)), shares.reshape(8, 2, 128)], axis=1
    )
    small = lax.all_to_all(jnp.concatenate([small, small], axis=0), CHIPS, 0, 0)
    token_gradient, gain_rows = pl.pallas_call(
        final_kernel,
        in_specs=[smem] + [vmem] * 4,
        out_shape=[
            jax.ShapeDtypeStruct((rows, share), BF16),
            jax.ShapeDtypeStruct((8, 256), F32),
        ],
        compiler_params=PARAMS,
    )(here[1], d_scaled, x, stat, small)
    gain_gradient = jnp.swapaxes(gain_rows[:2, : share // 2].reshape(2, 4, SHARD), 0, 1).reshape(share)
    return (token_gradient, gain_gradient)


def solution(mesh):
    fine = Mesh(mesh.devices.reshape(SIZES), NAMES)
    placed = (P(DP, MP), P(MP), P(DP, MP), P(DP, MP), P(DP, MP))
    return jax.shard_map(
        on_device, mesh=fine, in_specs=placed, out_specs=(P(DP, MP), P(MP)), check_vma=False
    )
```

```python
import jax
import jax.numpy as jnp
from jax import lax
from jax.experimental import pallas as pl
from jax.experimental.pallas import tpu as pltpu
from jax.sharding import Mesh, PartitionSpec as P

NAMES = ("y", "zh", "c", "zl", "x")
SIZES = (8, 4, 2, 2, 4)
DP, MP, CHIPS = ("y", "zh", "c"), ("zl", "x"), ("c", "zl", "x")
F32, BF16 = jnp.float32, jnp.bfloat16
SHARD = 48
SHARE = 384
EXTRA = 16
PARAMS = pltpu.CompilerParams(vmem_limit_bytes=20 * 1024 * 1024)
WIDE = pltpu.CompilerParams(vmem_limit_bytes=52 * 1024 * 1024)
together = lax.optimization_barrier


def gelu_exact(value):
    return jax.nn.gelu(value, approximate=False)


def partner(array, axis, n, bit):
    return lax.ppermute(array, axis, [(i, i ^ bit) for i in range(n)])


def products(groups, halves, place, parts, long=False):
    tokens, hidden = halves[0][1].shape
    weights, operands = [w for _, w in groups], [d for _, d, _ in halves]
    rows, n, both = weights[0].shape[0], len(groups), len(halves)

    def kernel(place_ref, *refs):
        w_refs, d_refs = refs[:n], refs[n : n + both]
        out_ref, held, sem = refs[-3:]
        copies = []
        w = jnp.concatenate([r[...] for r in w_refs], axis=0)
        for h, (k, _, count) in enumerate(halves):
            half = lax.rem(place_ref[1] + k, 2)
            out = lax.dot_general(
                w[: count * rows], d_refs[h][...], (((1,), (1,)), ((), ())), preferred_element_type=F32
            ).astype(BF16)
            for g, (offset, _) in enumerate(groups[:count]):
                held[h, g] = out[g * rows : (g + 1) * rows]
                block = lax.rem(place_ref[0] + offset + place_ref[1] * ((8 - 2 * offset) % 8), 8)
                to = out_ref.at[half, block]
                copies.append(pltpu.make_async_copy(held.at[h, g], to, sem.at[h, g]))
                copies[-1].start()
        for copy in copies:
            copy.wait()

    anywhere, whole = pl.BlockSpec(memory_space=pl.ANY), pl.BlockSpec(memory_space=pltpu.VMEM)
    return pl.pallas_call(
        kernel,
        in_specs=[pl.BlockSpec(memory_space=pltpu.SMEM)] + [whole] * (n + both) + [anywhere] * (parts is not None),
        out_specs=anywhere,
        out_shape=jax.ShapeDtypeStruct((2, 8, rows, tokens), BF16),
        scratch_shapes=[
            pltpu.VMEM((both, n, rows, tokens), BF16),
            pltpu.SemaphoreType.DMA((both, n)),
        ],
        input_output_aliases={} if parts is None else {1 + n + both: 0},
        compiler_params=WIDE,
        cost_estimate=pl.CostEstimate(
            flops=1 << 38 if long else rows * hidden * tokens, bytes_accessed=1 << 18, transcendentals=0
        ),
    )(place, *weights, *operands, *([] if parts is None else [parts]))


def tokens_kernel(tokens_ref, x_ref, send_ref, held, sem):
    x = tokens_ref[...].astype(F32).T
    x_ref[...] = x.astype(BF16)
    mean = jnp.sum(x, axis=0, keepdims=True) * (1.0 / SHARE)
    parts = []
    for rest in (mean, jnp.sum((x - mean) ** 2, axis=0, keepdims=True)):
        for _ in range(3):
            parts.append(rest.astype(BF16).astype(F32))
            rest = rest - parts[-1]
    parts = jnp.concatenate(parts + [jnp.zeros((EXTRA - 6, x.shape[1]), F32)], axis=0).astype(BF16)
    copies = []
    for c in range(2):
        for z in range(4):
            held[c, pl.ds(z * SHARD, SHARD)] = x[(z * 2 + c) * SHARD : (z * 2 + c + 1) * SHARD].astype(BF16)
        held[c, pl.ds(4 * SHARD, EXTRA)] = parts
        for m in range(8):
            copies.append(pltpu.make_async_copy(held.at[c], send_ref.at[c, m], sem.at[c, m]))
            copies[-1].start()
    for copy in copies:
        copy.wait()


def transposed(tokens):
    rows, share = tokens.shape
    return pl.pallas_call(
        tokens_kernel,
        out_specs=[pl.BlockSpec(memory_space=pltpu.VMEM), pl.BlockSpec(memory_space=pl.ANY)],
        out_shape=[
            jax.ShapeDtypeStruct((share, rows), BF16),
            jax.ShapeDtypeStruct((2, 8, share // 2 + EXTRA, rows), BF16),
        ],
        scratch_shapes=[
            pltpu.VMEM((2, share // 2 + EXTRA, rows), BF16),
            pltpu.SemaphoreType.DMA((2, 8)),
        ],
        compiler_params=WIDE,
    )(tokens)


def gain_kernel(parts_ref, x_ref, extra_ref, out_ref, stat_ref):
    @pl.when(pl.program_id(0) == 0)
    def _():
        for t in range(2):
            means, squares = [], []
            for m in range(8):
                rows = extra_ref[t, m].astype(F32)
                means.append(rows[0:1] + rows[1:2] + rows[2:3])
                squares.append(rows[3:4] + rows[4:5] + rows[5:6])
            mean = sum(means) * 0.125
            between = sum((m - mean) ** 2 for m in means)
            variance = (sum(squares) + SHARE * between) * (1.0 / (8 * SHARE))
            rstd = 1.0 / jnp.sqrt(variance + 1e-06)
            stat_ref[t] = jnp.concatenate([mean, rstd] * 4, axis=0)

    per_step, features = x_ref.shape[1], parts_ref.shape[2]
    for k in range(per_step):
        total = jnp.zeros((features, 128), F32)
        for t in range(2):
            xhat = (x_ref[t, k, :features].astype(F32) - stat_ref[t, 0:1]) * stat_ref[t, 1:2]
            value = parts_ref[t, k].astype(F32) * xhat
            total += value[:, :128] + value[:, 128:256] + value[:, 256:]
        total = jnp.concatenate([total, jnp.zeros((256 - features, 128), F32)], axis=0)
        row = jnp.sum(total.T, axis=0, keepdims=True)
        out_ref[pl.ds(pl.program_id(0) * per_step + k, 1), :] = row


def gain_share(parts, x_all):
    _, _, rows, tokens = parts.shape
    x_all = x_all.reshape(2, 8, rows + EXTRA, tokens)
    return pl.pallas_call(
        gain_kernel,
        grid=(4,),
        in_specs=[
            pl.BlockSpec((2, 2, rows, tokens), lambda m: (0, m, 0, 0)),
            pl.BlockSpec((2, 2, rows + EXTRA, tokens), lambda m: (0, m, 0, 0)),
            pl.BlockSpec((2, 8, EXTRA, tokens), lambda m: (0, 0, rows // EXTRA, 0)),
        ],
        out_specs=[
            pl.BlockSpec((8, 256), lambda m: (0, 0)),
            pl.BlockSpec((2, 8, tokens), lambda m: (0, 0, 0)),
        ],
        out_shape=[
            jax.ShapeDtypeStruct((8, 256), F32),
            jax.ShapeDtypeStruct((2, 8, tokens), F32),
        ],
        compiler_params=WIDE,
    )(parts, x_all, x_all)


def sum_kernel(core_ref, parts_ref, x_ref, gain_ref, stat_ref, d_ref, moments_ref):
    stat = stat_ref[core_ref[0]]
    mean, rstd = stat[0:1], stat[1:2]
    first, second = 0.0, 0.0
    for z in range(4):
        for c in range(2):
            total = parts_ref[c * 8, pl.ds(z * SHARD, SHARD), :].astype(F32)
            for m in range(1, 8):
                total += parts_ref[c * 8 + m, pl.ds(z * SHARD, SHARD), :].astype(F32)
            at = pl.ds((z * 2 + c) * SHARD, SHARD)
            g = total * gain_ref[at, :]
            d_ref[at, :] = g
            xhat = (x_ref[at, :].astype(F32) - mean) * rstd
            first += jnp.sum(g, axis=0, keepdims=True)
            second += jnp.sum(g * xhat, axis=0, keepdims=True)
    rows = [m[:, i * 128 : (i + 1) * 128] for m in (first, second) for i in range(3)]
    moments_ref[...] = jnp.concatenate(rows + [jnp.zeros((2, 128), F32)], axis=0)


def final_kernel(here_ref, d_ref, x_ref, stat_ref, small_ref, out_ref, gain_ref):
    core = here_ref[0]
    mean, rstd = stat_ref[core][0:1], stat_ref[core][1:2]
    total = small_ref[core * 8]
    for m in range(1, 8):
        total += small_ref[core * 8 + m]
    total = total * (1.0 / (8 * SHARE))
    first, second = (jnp.concatenate([total[k + i : k + i + 1] for i in range(3)], axis=1) for k in (0, 3))
    xhat = (x_ref[...].astype(F32) - mean) * rstd
    value = rstd * (d_ref[...] - first - xhat * second)
    out_ref[...] = value.T.astype(BF16)
    rows = []
    for c in range(2):
        both = jnp.zeros((8, 128), F32)
        for m in range(8):
            both += small_ref[c * 8 + m]
        rows.append(jnp.concatenate([both[6:7], both[7:8]], axis=1))
    gain_ref[...] = jnp.concatenate(rows + [jnp.zeros((6, 256), F32)], axis=0)


def on_device(tokens, gain, pre_act, w_in, act_cotangent):
    rows, share = tokens.shape
    here = [lax.axis_index(a).astype(jnp.int32).reshape(1) for a in ("y", "c")]
    place = jnp.concatenate(here)

    def step(array, way):
        moves = [((i + way) % 8, i, 0) for i in range(8)] + [((i - way) % 8, i, 1) for i in range(8)]
        return lax.ppermute(array, ("y", "c"), [(a * 2 + c, b * 2 + c) for a, b, c in moves])

    def tie(first, second, done, *later):
        (first_next, _), (second_next, _) = together((first, done)), together((second, done))
        return first_next, second_next, *together((first, second, done, *later))[2:]

    w0 = lax.all_gather(w_in, "zh", axis=0, tiled=True)
    w0, pre_act, act_cotangent, tokens = together((w0, pre_act, act_cotangent, tokens))
    first1, second1 = step(w0, 1), step(w0, -1)
    _, gelu_back = jax.vjp(gelu_exact, pre_act.astype(F32))
    d_own = gelu_back(act_cotangent.astype(F32))[0].astype(BF16)

    x, x_all = transposed(tokens)

    first, second, (d_own, x_all) = tie(first1, second1, (d_own, x_all))
    first2, second2 = step(first, 1), step(second, -1)
    d_other = partner(d_own, "c", 2, 1)
    x_all = lax.all_to_all(x_all.reshape(16, -1, rows), CHIPS, 0, 0)
    parts = products([(0, w0)], [(0, d_own, 1)], place, None, long=True)

    first, second, parts = tie(first2, second2, parts)
    first3, second3 = step(first, 1), step(second, -1)
    groups = [(1, first1), (7, second1), (2, first2), (6, second2)]
    parts = products([(0, w0)], [(1, d_other, 1)], place, parts)
    parts = products(groups, [(0, d_own, 4), (1, d_other, 4)], place, parts)

    first, second, parts = tie(first3, second3, parts)
    first4 = step(first, 1)
    parts = products([(3, first3), (5, second)], [(0, d_own, 2), (1, d_other, 2)], place, parts)

    first4, parts, x_all = together((first4, parts, x_all))
    parts = products([(4, first4)], [(0, d_own, 1), (1, d_other, 1)], place, parts)
    received = lax.all_to_all(parts.reshape(16, share // 2, rows), CHIPS, 0, 0)

    shares, stat = gain_share(parts, x_all)
    shares = lax.psum(lax.psum(shares, "y"), "zh")

    vmem, smem = pl.BlockSpec(memory_space=pltpu.VMEM), pl.BlockSpec(memory_space=pltpu.SMEM)
    d_scaled, moments = pl.pallas_call(
        sum_kernel,
        in_specs=[smem] + [vmem] * 4,
        out_shape=[
            jax.ShapeDtypeStruct((share, rows), F32),
            jax.ShapeDtypeStruct((8, 128), F32),
        ],
        compiler_params=PARAMS,
    )(here[1], received, x, gain.astype(F32)[:, None], stat)

    small = jnp.concatenate(
        [jnp.broadcast_to(moments[None, :6], (8, 6, 128)), shares.reshape(8, 2, 128)], axis=1
    )
    small = lax.all_to_all(jnp.concatenate([small, small], axis=0), CHIPS, 0, 0)
    token_gradient, gain_rows = pl.pallas_call(
        final_kernel,
        in_specs=[smem] + [vmem] * 4,
        out_shape=[
            jax.ShapeDtypeStruct((rows, share), BF16),
            jax.ShapeDtypeStruct((8, 256), F32),
        ],
        compiler_params=PARAMS,
    )(here[1], d_scaled, x, stat, small)
    gain_gradient = jnp.swapaxes(gain_rows[:2, : share // 2].reshape(2, 4, SHARD), 0, 1).reshape(share)
    return (token_gradient, gain_gradient)


def solution(mesh):
    fine = Mesh(mesh.devices.reshape(SIZES), NAMES)
    placed = (P(DP, MP), P(MP), P(DP, MP), P(DP, MP), P(DP, MP))
    return jax.shard_map(
        on_device, mesh=fine, in_specs=placed, out_specs=(P(DP, MP), P(MP)), check_vma=False
    )
```

```python
import jax
import jax.numpy as jnp
from jax import lax
from jax.experimental import pallas as pl
from jax.experimental.pallas import tpu as pltpu
from jax.sharding import Mesh, PartitionSpec as P

NAMES = ("y", "zh", "c", "zl", "x")
SIZES = (8, 4, 2, 2, 4)
DP, MP, CHIPS = ("y", "zh", "c"), ("zl", "x"), ("c", "zl", "x")
F32, BF16 = jnp.float32, jnp.bfloat16
SHARD = 48
SHARE = 384
EXTRA = 16
PARAMS = pltpu.CompilerParams(vmem_limit_bytes=20 * 1024 * 1024)
WIDE = pltpu.CompilerParams(vmem_limit_bytes=52 * 1024 * 1024)
together = lax.optimization_barrier


def gelu_exact(value):
    return jax.nn.gelu(value, approximate=False)


def partner(array, axis, n, bit):
    return lax.ppermute(array, axis, [(i, i ^ bit) for i in range(n)])


def products(groups, halves, place, parts, long=False):
    tokens, hidden = halves[0][1].shape
    weights, operands = [w for _, w in groups], [d for _, d, _ in halves]
    rows, n, both = weights[0].shape[0], len(groups), len(halves)

    def kernel(place_ref, *refs):
        w_refs, d_refs = refs[:n], refs[n : n + both]
        out_ref, held, sem = refs[-3:]
        copies = []
        w = jnp.concatenate([r[...] for r in w_refs], axis=0)
        for h, (k, _, count) in enumerate(halves):
            half = lax.rem(place_ref[1] + k, 2)
            out = lax.dot_general(
                w[: count * rows], d_refs[h][...], (((1,), (1,)), ((), ())), preferred_element_type=F32
            ).astype(BF16)
            for g, (offset, _) in enumerate(groups[:count]):
                held[h, g] = out[g * rows : (g + 1) * rows]
                block = lax.rem(place_ref[0] + offset + place_ref[1] * ((8 - 2 * offset) % 8), 8)
                to = out_ref.at[half, block]
                copies.append(pltpu.make_async_copy(held.at[h, g], to, sem.at[h, g]))
                copies[-1].start()
        for copy in copies:
            copy.wait()

    anywhere, whole = pl.BlockSpec(memory_space=pl.ANY), pl.BlockSpec(memory_space=pltpu.VMEM)
    return pl.pallas_call(
        kernel,
        in_specs=[pl.BlockSpec(memory_space=pltpu.SMEM)] + [whole] * (n + both) + [anywhere] * (parts is not None),
        out_specs=anywhere,
        out_shape=jax.ShapeDtypeStruct((2, 8, rows, tokens), BF16),
        scratch_shapes=[
            pltpu.VMEM((both, n, rows, tokens), BF16),
            pltpu.SemaphoreType.DMA((both, n)),
        ],
        input_output_aliases={} if parts is None else {1 + n + both: 0},
        compiler_params=WIDE,
        cost_estimate=pl.CostEstimate(
            flops=1 << 38 if long else rows * hidden * tokens, bytes_accessed=1 << 18, transcendentals=0
        ),
    )(place, *weights, *operands, *([] if parts is None else [parts]))


def tokens_kernel(tokens_ref, x_ref, send_ref, held, sem):
    x = tokens_ref[...].astype(F32).T
    x_ref[...] = x.astype(BF16)
    mean = jnp.sum(x, axis=0, keepdims=True) * (1.0 / SHARE)
    parts = []
    for rest in (mean, jnp.sum((x - mean) ** 2, axis=0, keepdims=True)):
        for _ in range(3):
            parts.append(rest.astype(BF16).astype(F32))
            rest = rest - parts[-1]
    parts = jnp.concatenate(parts + [jnp.zeros((EXTRA - 6, x.shape[1]), F32)], axis=0).astype(BF16)
    copies = []
    for c in range(2):
        for z in range(4):
            held[c, pl.ds(z * SHARD, SHARD)] = x[(z * 2 + c) * SHARD : (z * 2 + c + 1) * SHARD].astype(BF16)
        held[c, pl.ds(4 * SHARD, EXTRA)] = parts
        for m in range(8):
            copies.append(pltpu.make_async_copy(held.at[c], send_ref.at[c, m], sem.at[c, m]))
            copies[-1].start()
    for copy in copies:
        copy.wait()


def transposed(tokens):
    rows, share = tokens.shape
    return pl.pallas_call(
        tokens_kernel,
        out_specs=[pl.BlockSpec(memory_space=pltpu.VMEM), pl.BlockSpec(memory_space=pl.ANY)],
        out_shape=[
            jax.ShapeDtypeStruct((share, rows), BF16),
            jax.ShapeDtypeStruct((2, 8, share // 2 + EXTRA, rows), BF16),
        ],
        scratch_shapes=[
            pltpu.VMEM((2, share // 2 + EXTRA, rows), BF16),
            pltpu.SemaphoreType.DMA((2, 8)),
        ],
        compiler_params=WIDE,
    )(tokens)


def gain_kernel(y_ref, parts_ref, x_ref, extra_ref, out_ref, stat_ref):
    @pl.when(pl.program_id(0) == 0)
    def _():
        out_ref[...] = jnp.zeros_like(out_ref)
        for t in range(2):
            means, squares = [], []
            for m in range(8):
                rows = extra_ref[t, m].astype(F32)
                means.append(rows[0:1] + rows[1:2] + rows[2:3])
                squares.append(rows[3:4] + rows[4:5] + rows[5:6])
            mean = sum(means) * 0.125
            between = sum((m - mean) ** 2 for m in means)
            variance = (sum(squares) + SHARE * between) * (1.0 / (8 * SHARE))
            rstd = 1.0 / jnp.sqrt(variance + 1e-06)
            stat_ref[t] = jnp.concatenate([mean, rstd] * 4, axis=0)

    out_ref[pl.ds(lax.rem(y_ref[0] + 5 + pl.program_id(0), 8), 1), :] = share_row(parts_ref, x_ref, stat_ref)


def share_row(parts_ref, x_ref, stat_ref):
    features = parts_ref.shape[2]
    total = jnp.zeros((features, 128), F32)
    for t in range(2):
        xhat = (x_ref[t, 0, :features].astype(F32) - stat_ref[t, 0:1]) * stat_ref[t, 1:2]
        value = parts_ref[t, 0].astype(F32) * xhat
        total += value[:, :128] + value[:, 128:256] + value[:, 256:]
    total = jnp.concatenate([total, jnp.zeros((256 - features, 128), F32)], axis=0)
    return jnp.sum(total.T, axis=0, keepdims=True)


def last_kernel(y_ref, parts_ref, x_ref, stat_ref, shares_ref, out_ref):
    out_ref[...] = shares_ref[...]
    out_ref[pl.ds(lax.rem(y_ref[0] + 4, 8), 1), :] = share_row(parts_ref, x_ref, stat_ref)


def gain_shares(parts, x_all, y, early=None):
    _, _, rows, tokens = parts.shape
    x_all = x_all.reshape(2, 8, rows + EXTRA, tokens)
    first = 5 if early is None else 4
    blocks = [
        pl.BlockSpec((2, 1, r, tokens), lambda m, y: (0, lax.rem(y[0] + first + m, 8), 0, 0))
        for r in (rows, rows + EXTRA)
    ]
    shares = pl.BlockSpec((8, 256), lambda m, _: (0, 0))
    stat = pl.BlockSpec((2, 8, tokens), lambda m, _: (0, 0, 0))
    shares_shape = jax.ShapeDtypeStruct((8, 256), F32)
    if early is not None:
        return pl.pallas_call(
            last_kernel,
            grid_spec=pltpu.PrefetchScalarGridSpec(
                num_scalar_prefetch=1, grid=(1,), in_specs=blocks + [stat, shares], out_specs=shares
            ),
            out_shape=shares_shape,
            compiler_params=WIDE,
        )(y, parts, x_all, early[1], early[0])
    extra = pl.BlockSpec((2, 8, EXTRA, tokens), lambda m, _: (0, 0, rows // EXTRA, 0))
    return pl.pallas_call(
        gain_kernel,
        grid_spec=pltpu.PrefetchScalarGridSpec(
            num_scalar_prefetch=1, grid=(7,), in_specs=blocks + [extra], out_specs=[shares, stat]
        ),
        out_shape=[shares_shape, jax.ShapeDtypeStruct((2, 8, tokens), F32)],
        compiler_params=WIDE,
    )(y, parts, x_all, x_all)


def sum_kernel(core_ref, parts_ref, x_ref, gain_ref, stat_ref, d_ref, moments_ref):
    stat = stat_ref[core_ref[0]]
    mean, rstd = stat[0:1], stat[1:2]
    first, second = 0.0, 0.0
    for z in range(4):
        for c in range(2):
            total = parts_ref[c * 8, pl.ds(z * SHARD, SHARD), :].astype(F32)
            for m in range(1, 8):
                total += parts_ref[c * 8 + m, pl.ds(z * SHARD, SHARD), :].astype(F32)
            at = pl.ds((z * 2 + c) * SHARD, SHARD)
            g = total * gain_ref[at, :]
            d_ref[at, :] = g
            xhat = (x_ref[at, :].astype(F32) - mean) * rstd
            first += jnp.sum(g, axis=0, keepdims=True)
            second += jnp.sum(g * xhat, axis=0, keepdims=True)
    rows = [m[:, i * 128 : (i + 1) * 128] for m in (first, second) for i in range(3)]
    moments_ref[...] = jnp.concatenate(rows + [jnp.zeros((2, 128), F32)], axis=0)


def final_kernel(here_ref, d_ref, x_ref, stat_ref, small_ref, out_ref, gain_ref):
    core = here_ref[0]
    mean, rstd = stat_ref[core][0:1], stat_ref[core][1:2]
    total = small_ref[core * 8]
    for m in range(1, 8):
        total += small_ref[core * 8 + m]
    total = total * (1.0 / (8 * SHARE))
    first, second = (jnp.concatenate([total[k + i : k + i + 1] for i in range(3)], axis=1) for k in (0, 3))
    xhat = (x_ref[...].astype(F32) - mean) * rstd
    value = rstd * (d_ref[...] - first - xhat * second)
    out_ref[...] = value.T.astype(BF16)
    rows = []
    for c in range(2):
        both = jnp.zeros((8, 128), F32)
        for m in range(8):
            both += small_ref[c * 8 + m]
        rows.append(jnp.concatenate([both[6:7], both[7:8]], axis=1))
    gain_ref[...] = jnp.concatenate(rows + [jnp.zeros((6, 256), F32)], axis=0)


def on_device(tokens, gain, pre_act, w_in, act_cotangent):
    rows, share = tokens.shape
    here = [lax.axis_index(a).astype(jnp.int32).reshape(1) for a in ("y", "c")]
    place = jnp.concatenate(here)

    def step(array, way):
        moves = [((i + way) % 8, i, 0) for i in range(8)] + [((i - way) % 8, i, 1) for i in range(8)]
        return lax.ppermute(array, ("y", "c"), [(a * 2 + c, b * 2 + c) for a, b, c in moves])

    def tie(first, second, done, *later):
        (first_next, _), (second_next, _) = together((first, done)), together((second, done))
        return first_next, second_next, *together((first, second, done, *later))[2:]

    w0 = lax.all_gather(w_in, "zh", axis=0, tiled=True)
    w0, pre_act, act_cotangent, tokens = together((w0, pre_act, act_cotangent, tokens))
    first1, second1 = step(w0, 1), step(w0, -1)
    _, gelu_back = jax.vjp(gelu_exact, pre_act.astype(F32))
    d_own = gelu_back(act_cotangent.astype(F32))[0].astype(BF16)

    x, x_all = transposed(tokens)

    first, second, (d_own, x_all) = tie(first1, second1, (d_own, x_all))
    first2, second2 = step(first, 1), step(second, -1)
    d_other = partner(d_own, "c", 2, 1)
    x_all = lax.all_to_all(x_all.reshape(16, -1, rows), CHIPS, 0, 0)
    parts = products([(0, w0)], [(0, d_own, 1)], place, None, long=True)

    first, second, parts = tie(first2, second2, parts)
    first3, second3 = step(first, 1), step(second, -1)
    groups = [(1, first1), (7, second1), (2, first2), (6, second2)]
    parts = products([(0, w0)], [(1, d_other, 1)], place, parts)
    parts = products(groups, [(0, d_own, 4), (1, d_other, 4)], place, parts)

    first, second, parts = tie(first3, second3, parts)
    first4 = step(first, 1)
    parts = products([(3, first3), (5, second)], [(0, d_own, 2), (1, d_other, 2)], place, parts)

    parts, x_all = together((parts, x_all))
    shares, stat = gain_shares(parts, x_all, here[0])

    first4, parts, x_all, shares, stat = together((first4, parts, x_all, shares, stat))
    parts = products([(4, first4)], [(0, d_own, 1), (1, d_other, 1)], place, parts)
    received = lax.all_to_all(parts.reshape(16, share // 2, rows), CHIPS, 0, 0)

    shares = gain_shares(parts, x_all, here[0], (shares, stat))
    shares = lax.psum(lax.psum(shares, "y"), "zh")

    vmem, smem = pl.BlockSpec(memory_space=pltpu.VMEM), pl.BlockSpec(memory_space=pltpu.SMEM)
    d_scaled, moments = pl.pallas_call(
        sum_kernel,
        in_specs=[smem] + [vmem] * 4,
        out_shape=[
            jax.ShapeDtypeStruct((share, rows), F32),
            jax.ShapeDtypeStruct((8, 128), F32),
        ],
        compiler_params=PARAMS,
    )(here[1], received, x, gain.astype(F32)[:, None], stat)

    small = jnp.concatenate(
        [jnp.broadcast_to(moments[None, :6], (8, 6, 128)), shares.reshape(8, 2, 128)], axis=1
    )
    small = lax.all_to_all(jnp.concatenate([small, small], axis=0), CHIPS, 0, 0)
    token_gradient, gain_rows = pl.pallas_call(
        final_kernel,
        in_specs=[smem] + [vmem] * 4,
        out_shape=[
            jax.ShapeDtypeStruct((rows, share), BF16),
            jax.ShapeDtypeStruct((8, 256), F32),
        ],
        compiler_params=PARAMS,
    )(here[1], d_scaled, x, stat, small)
    gain_gradient = jnp.swapaxes(gain_rows[:2, : share // 2].reshape(2, 4, SHARD), 0, 1).reshape(share)
    return (token_gradient, gain_gradient)


def solution(mesh):
    fine = Mesh(mesh.devices.reshape(SIZES), NAMES)
    placed = (P(DP, MP), P(MP), P(DP, MP), P(DP, MP), P(DP, MP))
    return jax.shard_map(
        on_device, mesh=fine, in_specs=placed, out_specs=(P(DP, MP), P(MP)), check_vma=False
    )
```

```python
import jax
import jax.numpy as jnp
from jax import lax
from jax.experimental import pallas as pl
from jax.experimental.pallas import tpu as pltpu
from jax.sharding import Mesh, PartitionSpec as P

NAMES = ("y", "zh", "c", "zl", "x")
SIZES = (8, 4, 2, 2, 4)
DP, MP, CHIPS = ("y", "zh", "c"), ("zl", "x"), ("c", "zl", "x")
F32, BF16 = jnp.float32, jnp.bfloat16
SHARD = 48
SHARE = 384
EXTRA = 16
PARAMS = pltpu.CompilerParams(vmem_limit_bytes=20 * 1024 * 1024)
WIDE = pltpu.CompilerParams(vmem_limit_bytes=52 * 1024 * 1024)
together = lax.optimization_barrier


def gelu_exact(value):
    return jax.nn.gelu(value, approximate=False)


def partner(array, axis, n, bit):
    return lax.ppermute(array, axis, [(i, i ^ bit) for i in range(n)])


def products(groups, halves, place, parts, long=False):
    tokens, hidden = halves[0][1].shape
    weights, operands = [w for _, w in groups], [d for _, d, _ in halves]
    rows, n, both = weights[0].shape[0], len(groups), len(halves)

    def kernel(place_ref, *refs):
        w_refs, d_refs = refs[:n], refs[n : n + both]
        out_ref, held, sem = refs[-3:]
        copies = []
        w = jnp.concatenate([r[...] for r in w_refs], axis=0)
        for h, (k, _, count) in enumerate(halves):
            half = lax.rem(place_ref[1] + k, 2)
            out = lax.dot_general(
                d_refs[h][...], w[: count * rows], (((1,), (1,)), ((), ())), preferred_element_type=F32
            ).T.astype(BF16)
            for g, (offset, _) in enumerate(groups[:count]):
                held[h, g] = out[g * rows : (g + 1) * rows]
                block = lax.rem(place_ref[0] + offset + place_ref[1] * ((8 - 2 * offset) % 8), 8)
                to = out_ref.at[half, block]
                copies.append(pltpu.make_async_copy(held.at[h, g], to, sem.at[h, g]))
                copies[-1].start()
        for copy in copies:
            copy.wait()

    anywhere, whole = pl.BlockSpec(memory_space=pl.ANY), pl.BlockSpec(memory_space=pltpu.VMEM)
    return pl.pallas_call(
        kernel,
        in_specs=[pl.BlockSpec(memory_space=pltpu.SMEM)] + [whole] * (n + both) + [anywhere] * (parts is not None),
        out_specs=anywhere,
        out_shape=jax.ShapeDtypeStruct((2, 8, rows, tokens), BF16),
        scratch_shapes=[
            pltpu.VMEM((both, n, rows, tokens), BF16),
            pltpu.SemaphoreType.DMA((both, n)),
        ],
        input_output_aliases={} if parts is None else {1 + n + both: 0},
        compiler_params=WIDE,
        cost_estimate=pl.CostEstimate(
            flops=1 << 38 if long else rows * hidden * tokens, bytes_accessed=1 << 18, transcendentals=0
        ),
    )(place, *weights, *operands, *([] if parts is None else [parts]))


def tokens_kernel(tokens_ref, x_ref, send_ref, held, sem):
    x = tokens_ref[...].astype(F32).T
    x_ref[...] = x.astype(BF16)
    mean = jnp.sum(x, axis=0, keepdims=True) * (1.0 / SHARE)
    parts = []
    for rest in (mean, jnp.sum((x - mean) ** 2, axis=0, keepdims=True)):
        for _ in range(3):
            parts.append(rest.astype(BF16).astype(F32))
            rest = rest - parts[-1]
    parts = jnp.concatenate(parts + [jnp.zeros((EXTRA - 6, x.shape[1]), F32)], axis=0).astype(BF16)
    copies = []
    for c in range(2):
        for z in range(4):
            held[c, pl.ds(z * SHARD, SHARD)] = x[(z * 2 + c) * SHARD : (z * 2 + c + 1) * SHARD].astype(BF16)
        held[c, pl.ds(4 * SHARD, EXTRA)] = parts
        for m in range(8):
            copies.append(pltpu.make_async_copy(held.at[c], send_ref.at[c, m], sem.at[c, m]))
            copies[-1].start()
    for copy in copies:
        copy.wait()


def transposed(tokens):
    rows, share = tokens.shape
    return pl.pallas_call(
        tokens_kernel,
        out_specs=[pl.BlockSpec(memory_space=pltpu.VMEM), pl.BlockSpec(memory_space=pl.ANY)],
        out_shape=[
            jax.ShapeDtypeStruct((share, rows), BF16),
            jax.ShapeDtypeStruct((2, 8, share // 2 + EXTRA, rows), BF16),
        ],
        scratch_shapes=[
            pltpu.VMEM((2, share // 2 + EXTRA, rows), BF16),
            pltpu.SemaphoreType.DMA((2, 8)),
        ],
        compiler_params=WIDE,
    )(tokens)


def gain_kernel(parts_ref, x_ref, extra_ref, out_ref, stat_ref):
    @pl.when(pl.program_id(0) == 0)
    def _():
        for t in range(2):
            means, squares = [], []
            for m in range(8):
                rows = extra_ref[t, m].astype(F32)
                means.append(rows[0:1] + rows[1:2] + rows[2:3])
                squares.append(rows[3:4] + rows[4:5] + rows[5:6])
            mean = sum(means) * 0.125
            between = sum((m - mean) ** 2 for m in means)
            variance = (sum(squares) + SHARE * between) * (1.0 / (8 * SHARE))
            rstd = 1.0 / jnp.sqrt(variance + 1e-06)
            stat_ref[t] = jnp.concatenate([mean, rstd] * 4, axis=0)

    per_step, features = x_ref.shape[1], parts_ref.shape[2]
    for k in range(per_step):
        total = jnp.zeros((features, 128), F32)
        for t in range(2):
            xhat = (x_ref[t, k, :features].astype(F32) - stat_ref[t, 0:1]) * stat_ref[t, 1:2]
            value = parts_ref[t, k].astype(F32) * xhat
            total += value[:, :128] + value[:, 128:256] + value[:, 256:]
        total = jnp.concatenate([total, jnp.zeros((256 - features, 128), F32)], axis=0)
        row = jnp.sum(total.T, axis=0, keepdims=True)
        out_ref[pl.ds(pl.program_id(0) * per_step + k, 1), :] = row


def gain_share(parts, x_all):
    _, _, rows, tokens = parts.shape
    x_all = x_all.reshape(2, 8, rows + EXTRA, tokens)
    return pl.pallas_call(
        gain_kernel,
        grid=(4,),
        in_specs=[
            pl.BlockSpec((2, 2, rows, tokens), lambda m: (0, m, 0, 0)),
            pl.BlockSpec((2, 2, rows + EXTRA, tokens), lambda m: (0, m, 0, 0)),
            pl.BlockSpec((2, 8, EXTRA, tokens), lambda m: (0, 0, rows // EXTRA, 0)),
        ],
        out_specs=[
            pl.BlockSpec((8, 256), lambda m: (0, 0)),
            pl.BlockSpec((2, 8, tokens), lambda m: (0, 0, 0)),
        ],
        out_shape=[
            jax.ShapeDtypeStruct((8, 256), F32),
            jax.ShapeDtypeStruct((2, 8, tokens), F32),
        ],
        compiler_params=WIDE,
    )(parts, x_all, x_all)


def sum_kernel(core_ref, parts_ref, x_ref, gain_ref, stat_ref, d_ref, moments_ref):
    stat = stat_ref[core_ref[0]]
    mean, rstd = stat[0:1], stat[1:2]
    first, second = 0.0, 0.0
    for z in range(4):
        for c in range(2):
            total = parts_ref[c * 8, pl.ds(z * SHARD, SHARD), :].astype(F32)
            for m in range(1, 8):
                total += parts_ref[c * 8 + m, pl.ds(z * SHARD, SHARD), :].astype(F32)
            at = pl.ds((z * 2 + c) * SHARD, SHARD)
            g = total * gain_ref[at, :]
            d_ref[at, :] = g
            xhat = (x_ref[at, :].astype(F32) - mean) * rstd
            first += jnp.sum(g, axis=0, keepdims=True)
            second += jnp.sum(g * xhat, axis=0, keepdims=True)
    rows = [m[:, i * 128 : (i + 1) * 128] for m in (first, second) for i in range(3)]
    moments_ref[...] = jnp.concatenate(rows + [jnp.zeros((2, 128), F32)], axis=0)


def final_kernel(here_ref, d_ref, x_ref, stat_ref, small_ref, out_ref, gain_ref):
    core = here_ref[0]
    mean, rstd = stat_ref[core][0:1], stat_ref[core][1:2]
    total = small_ref[core * 8]
    for m in range(1, 8):
        total += small_ref[core * 8 + m]
    total = total * (1.0 / (8 * SHARE))
    first, second = (jnp.concatenate([total[k + i : k + i + 1] for i in range(3)], axis=1) for k in (0, 3))
    xhat = (x_ref[...].astype(F32) - mean) * rstd
    value = rstd * (d_ref[...] - first - xhat * second)
    out_ref[...] = value.T.astype(BF16)
    rows = []
    for c in range(2):
        both = jnp.zeros((8, 128), F32)
        for m in range(8):
            both += small_ref[c * 8 + m]
        rows.append(jnp.concatenate([both[6:7], both[7:8]], axis=1))
    gain_ref[...] = jnp.concatenate(rows + [jnp.zeros((6, 256), F32)], axis=0)


def on_device(tokens, gain, pre_act, w_in, act_cotangent):
    rows, share = tokens.shape
    here = [lax.axis_index(a).astype(jnp.int32).reshape(1) for a in ("y", "c")]
    place = jnp.concatenate(here)

    def step(array, way):
        moves = [((i + way) % 8, i, 0) for i in range(8)] + [((i - way) % 8, i, 1) for i in range(8)]
        return lax.ppermute(array, ("y", "c"), [(a * 2 + c, b * 2 + c) for a, b, c in moves])

    def tie(first, second, done, *later):
        (first_next, _), (second_next, _) = together((first, done)), together((second, done))
        return first_next, second_next, *together((first, second, done, *later))[2:]

    w0 = lax.all_gather(w_in, "zh", axis=0, tiled=True)
    w0, pre_act, act_cotangent, tokens = together((w0, pre_act, act_cotangent, tokens))
    first1, second1 = step(w0, 1), step(w0, -1)
    _, gelu_back = jax.vjp(gelu_exact, pre_act.astype(F32))
    d_own = gelu_back(act_cotangent.astype(F32))[0].astype(BF16)

    x, x_all = transposed(tokens)

    first, second, (d_own, x_all) = tie(first1, second1, (d_own, x_all))
    first2, second2 = step(first, 1), step(second, -1)
    d_other = partner(d_own, "c", 2, 1)
    x_all = lax.all_to_all(x_all.reshape(16, -1, rows), CHIPS, 0, 0)
    parts = products([(0, w0)], [(0, d_own, 1)], place, None, long=True)

    first, second, parts = tie(first2, second2, parts)
    first3, second3 = step(first, 1), step(second, -1)
    groups = [(1, first1), (7, second1), (2, first2), (6, second2)]
    parts = products([(0, w0)], [(1, d_other, 1)], place, parts)
    parts = products(groups, [(0, d_own, 4), (1, d_other, 4)], place, parts)

    first, second, parts = tie(first3, second3, parts)
    first4 = step(first, 1)
    parts = products([(3, first3), (5, second)], [(0, d_own, 2), (1, d_other, 2)], place, parts)

    first4, parts, x_all = together((first4, parts, x_all))
    parts = products([(4, first4)], [(0, d_own, 1), (1, d_other, 1)], place, parts)
    received = lax.all_to_all(parts.reshape(16, share // 2, rows), CHIPS, 0, 0)

    shares, stat = gain_share(parts, x_all)
    shares = lax.psum(lax.psum(shares, "y"), "zh")

    vmem, smem = pl.BlockSpec(memory_space=pltpu.VMEM), pl.BlockSpec(memory_space=pltpu.SMEM)
    d_scaled, moments = pl.pallas_call(
        sum_kernel,
        in_specs=[smem] + [vmem] * 4,
        out_shape=[
            jax.ShapeDtypeStruct((share, rows), F32),
            jax.ShapeDtypeStruct((8, 128), F32),
        ],
        compiler_params=PARAMS,
    )(here[1], received, x, gain.astype(F32)[:, None], stat)

    small = jnp.concatenate(
        [jnp.broadcast_to(moments[None, :6], (8, 6, 128)), shares.reshape(8, 2, 128)], axis=1
    )
    small = lax.all_to_all(jnp.concatenate([small, small], axis=0), CHIPS, 0, 0)
    token_gradient, gain_rows = pl.pallas_call(
        final_kernel,
        in_specs=[smem] + [vmem] * 4,
        out_shape=[
            jax.ShapeDtypeStruct((rows, share), BF16),
            jax.ShapeDtypeStruct((8, 256), F32),
        ],
        compiler_params=PARAMS,
    )(here[1], d_scaled, x, stat, small)
    gain_gradient = jnp.swapaxes(gain_rows[:2, : share // 2].reshape(2, 4, SHARD), 0, 1).reshape(share)
    return (token_gradient, gain_gradient)


def solution(mesh):
    fine = Mesh(mesh.devices.reshape(SIZES), NAMES)
    placed = (P(DP, MP), P(MP), P(DP, MP), P(DP, MP), P(DP, MP))
    return jax.shard_map(
        on_device, mesh=fine, in_specs=placed, out_specs=(P(DP, MP), P(MP)), check_vma=False
    )
```
